32 devices in a mesh: dp: 16 (over z, x, core), tensor: 2 (over y).
Axes of the slice: x: 2, y: 2, z: 4, core: 2. Of those that a mesh axis runs over, the one named last changes fastest.
Arguments:
- hidden: float32 [2, 4096, 2048], P(None, ('dp', 'tensor')), may hold values from -6 to 6
- cotangent: bfloat16 [2, 4096, 2048], P(None, ('dp', 'tensor')), may hold values from -6 to 6
- lengths: int32 [2, 16, 4], P(None, 'dp'), may hold values from 1 to 253, as said below
- order: int32 [2, 16, 4], P(None, 'dp'), may hold values from 0 to 3, each once within a row
- norm_gain: float32 [2048], P('dp'), may hold values from 0.5 to 1.5
- input_weight: bfloat16 [2048, 2, 4096], P('dp', None, 'tensor'), may hold values from -0.125 to 0.125
- conv_weight: float32 [4, 4096], P(None, ('tensor', 'dp')), may hold values from -3 to 3
- conv_bias: float32 [4096], P(('tensor', 'dp')), may hold values from -3 to 3
- select_weight: bfloat16 [4096, 160], P(('tensor', 'dp')), may hold values from -0.09375 to 0.09375
- step_weight: bfloat16 [128, 4096], P('dp', 'tensor'), may hold values from -0.5 to 0.5
- step_bias: float32 [4096], P(('tensor', 'dp')), may hold values from -7 to -2
- decay_log: float32 [16, 4096], P(None, ('tensor', 'dp')), may hold values from -1 to 2.8
- skip_gain: float32 [4096], P(('tensor', 'dp')), may hold values from 0.5 to 1.5
- output_weight: bfloat16 [4096, 2048], P('tensor', 'dp'), may hold values from -0.1875 to 0.1875
Outputs:
- layer_out: float32 [2, 4096, 2048], P(None, ('dp', 'tensor'))
- hidden_grad: float32 [2, 4096, 2048], P(None, ('dp', 'tensor'))
- norm_gain_grad: float32 [2048], P('dp')
- input_weight_grad: float32 [2048, 2, 4096], P('dp', None, 'tensor')
- conv_weight_grad: float32 [4, 4096], P(None, ('tensor', 'dp'))
- conv_bias_grad: float32 [4096], P(('tensor', 'dp'))
- select_weight_grad: float32 [4096, 160], P(('tensor', 'dp'))
- step_weight_grad: float32 [128, 4096], P('dp', 'tensor')
- step_bias_grad: float32 [4096], P(('tensor', 'dp'))
- decay_log_grad: float32 [16, 4096], P(None, ('tensor', 'dp'))
- skip_gain_grad: float32 [4096], P(('tensor', 'dp'))
- output_weight_grad: float32 [4096, 2048], P('tensor', 'dp')
The draws below stay inside these ranges and needn't reach their ends.
Inputs may be any that keep to these rules, and one draw needn't show every extreme that they name: In each micro-batch and data index the 4 lengths sum to at most 256; the slots after their sum are padding.
All inputs are finite; a program needn't handle non-finite values.
Results may differ from the reference program's by a relative error of at most 0.0097.
Values may be sent and summed in bfloat16 or wider, within the bound.
No kernel may reach another device: no remote copies, remote signals or barrier semaphores. Data moves between devices by JAX's collectives and lax.ppermute only.
A program may use at most 384 MiB of HBM per device.

```python
import jax
import jax.numpy as jnp
from jax import lax

D = 2048
INNER = 4096
STATE = 16
RANK = 128
KERNEL = 4
GROUP_TOK = 256
MICRO = 2
SEQS = 4
TOKENS = 4096
N_DP = 16


def draw_lengths(key, part):
    key = jax.random.fold_in(key, 7)
    row_count = MICRO * (TOKENS // GROUP_TOK)
    short_top = max(GROUP_TOK // 32, 1)
    key_list = jax.random.split(key, 4)
    shorts = jax.random.randint(key_list[0], (row_count, SEQS - 1), 1, short_top + 1)
    padding = jax.random.randint(key_list[1], (row_count,), 0, short_top)
    chosen = jax.random.randint(key_list[2], (), 0, row_count)
    marked = jnp.arange(row_count) == chosen
    shorts = jnp.where(marked[:, None], 1, shorts)
    padding = jnp.where(marked, 0, padding)
    longest = GROUP_TOK - padding - jnp.sum(shorts, axis=1)
    listed = jnp.concatenate([longest[:, None], shorts], axis=1)
    rotation = jax.random.randint(key_list[3], (row_count, 1), 0, SEQS)
    columns = (jnp.arange(SEQS)[None, :] + rotation) % SEQS
    placed = jnp.take_along_axis(listed, columns, axis=1)
    return placed.reshape(MICRO, row_count // MICRO, SEQS).astype(jnp.int32)


def level_of(stream_key, dims, pieces, smallest, high):
    level = 1.0
    for axis_at, blocks in pieces:
        steps = jax.random.uniform(jax.random.fold_in(jax.random.fold_in(stream_key, 6), axis_at), (blocks,), jnp.float32, smallest / len(pieces), high / len(pieces))
        level = level * jnp.repeat(jnp.exp(steps), dims[axis_at] // blocks).reshape((-1,) + (1,) * (len(dims) - 1 - axis_at))
    return level


def bell_draw(stream_key, dims, spread, most, cuts=(), kind=jnp.bfloat16):
    values = jax.random.normal(stream_key, dims, jnp.float32) * spread
    if len(cuts) > 0:
        values = level_of(stream_key, dims, cuts, -0.22, 0.18) * values
    return jnp.clip(values, min=-most, max=most).astype(kind)


def setup_inputs(seed: int = 0) -> dict:
    splits = jax.random.split(jax.random.key(seed), 15)
    hidden = bell_draw(splits[0], (MICRO, TOKENS, D), 1.0, 6.0, ((1, 32),), jnp.float32)
    cotangent = bell_draw(splits[1], (MICRO, TOKENS, D), 1.0, 6.0, ((1, 32),))
    lengths = draw_lengths(jax.random.fold_in(splits[14], 71), 0)
    order = jax.vmap(lambda own: jax.random.permutation(own, SEQS))(jax.random.split(splits[3], MICRO * N_DP)).reshape((MICRO, N_DP, SEQS)).astype(jnp.int32)
    norm_gain = jnp.clip(1.0 + 0.1 * jax.random.normal(splits[4], (D,), jnp.float32), 0.5, 1.5)
    input_weight = bell_draw(splits[5], (D, 2, INNER), D ** -0.5, 0.125, ((0, 16), (2, 2)))
    conv_weight = bell_draw(splits[6], (KERNEL, INNER), KERNEL ** -0.5, 3.0, ((1, 32),), jnp.float32)
    conv_bias = bell_draw(splits[7], (INNER,), 0.5, 3.0, ((0, 32),), jnp.float32)
    select_weight = bell_draw(splits[8], (INNER, RANK + 2 * STATE), INNER ** -0.5, 0.09375, ((0, 32),))
    step_weight = bell_draw(splits[9], (RANK, INNER), RANK ** -0.5, 0.5, ((0, 16), (1, 2)))
    step_bias = jnp.clip(-7.0 + 5.0 * jax.random.uniform(splits[10], (INNER,), jnp.float32) ** level_of(splits[10], (INNER,), ((0, 32),), -0.2, 0.2), -7.0, -2.0)
    decay_log = jnp.clip(-1.0 + 3.8 * jax.random.uniform(splits[11], (STATE, INNER), jnp.float32) ** level_of(splits[11], (STATE, INNER), ((1, 32),), -0.2, 0.2), -1.0, 2.8)
    skip_gain = jnp.clip(0.5 + 1.0 * jax.random.uniform(splits[12], (INNER,), jnp.float32) ** level_of(splits[12], (INNER,), ((0, 32),), -0.2, 0.2), 0.5, 1.5)
    output_weight = bell_draw(splits[13], (INNER, D), (INNER // 4) ** -0.5, 0.1875, ((0, 2), (1, 16)))
    return dict(hidden=hidden, cotangent=cotangent, lengths=lengths, order=order, norm_gain=norm_gain, input_weight=input_weight, conv_weight=conv_weight, conv_bias=conv_bias, select_weight=select_weight, step_weight=step_weight, step_bias=step_bias, decay_log=decay_log, skip_gain=skip_gain, output_weight=output_weight)


@jax.custom_vjp
def low(v):
    return lax.optimization_barrier(v.astype(jnp.bfloat16)).astype(jnp.float32)

@jax.custom_vjp
def low_back(v):
    return v

def low_keep(v):
    return (low(v), None)

def low_pass(kept, grad):
    return (grad,)

def back_keep(v):
    return (v, None)

def back_low(kept, grad):
    return (low(grad),)
low.defvjp(low_keep, low_pass)
low_back.defvjp(back_keep, back_low)
epsilon = 1e-05

def positions(length_row, order_row):
    ordered = jnp.take(length_row, order_row).astype(jnp.int32)
    seq_ends = jnp.cumsum(ordered).astype(jnp.int32)
    starts = jnp.concatenate([jnp.zeros((1,), jnp.int32), seq_ends]).astype(jnp.int32)
    slot_ids = jnp.arange(GROUP_TOK, dtype=jnp.int32)
    seq_begin = lax.optimization_barrier(jnp.max(jnp.where(starts[None, :] <= slot_ids[:, None], starts[None, :], 0), axis=1)).astype(jnp.int32)
    return ((slot_ids - seq_begin).astype(jnp.int32), (slot_ids < seq_ends[-1]).astype(jnp.float32))

def delayed(values, steps_back):
    if steps_back == 0:
        return values
    return jnp.concatenate([jnp.zeros((steps_back,) + values.shape[1:], values.dtype), values[:-steps_back]], axis=0)

def mixer(token_rows, position, live_mask, norm_gain, input_weight, conv_weight, conv_bias, select_weight, step_weight, step_bias, decay_log, skip_gain, output_weight):
    highest = lax.Precision.HIGHEST
    inverse_rms = lax.rsqrt(lax.optimization_barrier(jnp.mean(token_rows * token_rows, axis=-1, keepdims=True)) + epsilon)
    normed = low(token_rows * inverse_rms * norm_gain)
    projected = low_back(jnp.einsum('gd,dkc->gkc', normed, input_weight, precision=highest))
    inner_part = projected[:, 0]
    gate_part = projected[:, 1]
    convolved = jnp.zeros_like(inner_part) + conv_bias
    for tap_index in range(KERNEL):
        delay_by = KERNEL - 1 - tap_index
        tap_mask = (position >= delay_by).astype(jnp.float32)[:, None]
        convolved = convolved + conv_weight[tap_index] * delayed(inner_part, delay_by) * tap_mask
    activated = low(jax.nn.silu(convolved))
    selected = low_back(jnp.dot(activated, select_weight, precision=highest))
    rank_part = low(selected[:, :RANK])
    in_cols = selected[:, RANK:RANK + STATE]
    out_cols = selected[:, RANK + STATE:]
    step_size = jax.nn.softplus(low_back(jnp.dot(rank_part, step_weight, precision=highest) + step_bias))
    decay_rate = -jnp.exp(decay_log)
    keep_mask = (position > 0).astype(jnp.float32)

    def recur(state, sliced):
        step_row, in_row, out_row, act_row, keep_row = sliced
        state = jnp.exp(step_row[None, :] * decay_rate) * keep_row * state + (step_row * act_row)[None, :] * in_row[:, None]
        return (state, jnp.dot(out_row, state, precision=highest))
    _, scanned = lax.scan(recur, jnp.zeros((STATE, INNER), jnp.float32), (step_size, in_cols, out_cols, activated, keep_mask))
    gated = low((scanned + skip_gain * activated) * jax.nn.silu(gate_part) * live_mask[:, None])
    return token_rows + jnp.dot(gated, output_weight, precision=highest)

def reference(hidden, cotangent, lengths, order, norm_gain, input_weight, conv_weight, conv_bias, select_weight, step_weight, step_bias, decay_log, skip_gain, output_weight):
    group_count = MICRO * N_DP
    tokens_all = hidden.astype(jnp.float32).reshape(group_count, GROUP_TOK, D)
    cot_all = cotangent.astype(jnp.float32).reshape(group_count, GROUP_TOK, D)
    position, live_mask = jax.vmap(positions)(lengths.reshape(group_count, SEQS), order.reshape(group_count, SEQS))

    def forward(tokens_in, gain_in, in_weight, conv_w, conv_b, sel_weight, stp_weight, stp_bias, dec_log, skp_gain, out_weight):

        def one_group(carried, sliced):
            group_rows, pos_row, live_row = sliced
            result = jax.checkpoint(mixer)(group_rows, pos_row, live_row, gain_in, in_weight, conv_w, conv_b, sel_weight, stp_weight, stp_bias, dec_log, skp_gain, out_weight)
            return (carried, result)
        _, results = lax.scan(one_group, jnp.zeros((), jnp.float32), (tokens_in, position, live_mask))
        return results
    outputs, pull_back = jax.vjp(forward, tokens_all, norm_gain.astype(jnp.float32), input_weight.astype(jnp.float32), conv_weight.astype(jnp.float32), conv_bias.astype(jnp.float32), select_weight.astype(jnp.float32), step_weight.astype(jnp.float32), step_bias.astype(jnp.float32), decay_log.astype(jnp.float32), skip_gain.astype(jnp.float32), output_weight.astype(jnp.float32))
    grads = pull_back(cot_all)
    return (outputs.reshape(MICRO, TOKENS, D), grads[0].reshape(MICRO, TOKENS, D), grads[1], grads[2], grads[3], grads[4], grads[5], grads[6], grads[7], grads[8], grads[9], grads[10])
```

```python
import functools

import jax
import jax.numpy as jnp
from jax import lax
from jax.experimental import pallas as pl
from jax.experimental.pallas import tpu as pltpu
from jax.sharding import PartitionSpec as P

epsilon = 1e-05
log2e = 1.4426950408889634
far = 1e6
chunk = 16
f32 = jnp.float32
bf16 = jnp.bfloat16
highest = lax.Precision.HIGHEST
last_dims = (((1,), (1,)), ((), ()))
first_dims = (((0,), (0,)), ((), ()))


def positions(length_row, order_row, slot_count):
    number = order_row.shape[0]
    picked = (order_row[:, None] == jnp.arange(number, dtype=jnp.int32)[None, :]).astype(jnp.int32)
    ordered = jnp.sum(picked * length_row[None, :], axis=1)
    seq_ends = jnp.cumsum(ordered)
    starts = jnp.concatenate([jnp.zeros((1,), jnp.int32), seq_ends])
    slot_ids = jnp.arange(slot_count, dtype=jnp.int32)
    seq_begin = jnp.max(jnp.where(starts[None, :] <= slot_ids[:, None], starts[None, :], 0), axis=1)
    return (slot_ids - seq_begin, (slot_ids < seq_ends[-1]).astype(jnp.float32))


def delayed(values, steps_back):
    if steps_back == 0:
        return values
    return jnp.pad(values[:, :-steps_back], ((0, 0), (steps_back, 0), (0, 0)))


def advanced(values, steps_ahead):
    if steps_ahead == 0:
        return values
    return jnp.pad(values[:, steps_ahead:], ((0, 0), (0, steps_ahead), (0, 0)))


def swapped(values, axis, bit):
    count = lax.axis_size(axis)
    return lax.ppermute(values, axis, [(i, i ^ bit) for i in range(count)])


def tensor_gather(values, axis):
    if lax.axis_size("tensor") != 2:
        return lax.all_gather(values, "tensor", axis=axis, tiled=True)
    other = swapped(values, "tensor", 1)
    mine_first = lax.axis_index("tensor") == 0
    low = jnp.where(mine_first, values, other)
    high = jnp.where(mine_first, other, values)
    return jnp.concatenate([low, high], axis=axis)


def tensor_sum(values):
    if lax.axis_size("tensor") != 2:
        return lax.psum(values, "tensor")
    return values + swapped(values, "tensor", 1)


def tensor_scatter_matmul(pairs, rows, micro):
    def product(picked):
        total = None
        for left, right, dims in pairs:
            part = left.reshape(micro, -1, left.shape[-1])
            if picked is not None:
                part = lax.dynamic_slice_in_dim(part, picked * rows, rows, 1)
            part = lax.dot_general(part.reshape(-1, part.shape[-1]), right, dims, preferred_element_type=f32)
            total = part if total is None else total + part
        return total.reshape(micro, -1, total.shape[-1])

    if lax.axis_size("tensor") != 2:
        return lax.psum_scatter(
            product(None).astype(bf16), "tensor", scatter_dimension=1, tiled=True
        ).astype(f32)
    here = lax.axis_index("tensor")
    away = swapped(product(1 - here).astype(bf16), "tensor", 1)
    return product(here) + away.astype(f32)


def moved(values, offset):
    count = lax.axis_size("dp")
    return lax.ppermute(values, "dp", [((i + 4 * offset) % count, i) for i in range(count)])


def reduce_scatter(values):
    count = lax.axis_size("dp")
    outer = count // 4
    kind = values.dtype
    here = lax.axis_index("dp")
    parts = values.reshape((outer, 2, 2, values.shape[0] // count) + values.shape[1:])
    core = here % 2
    cross = (here // 2) % 2
    place = here // 4
    kept = lax.dynamic_index_in_dim(parts, core, 2, False)
    sent = lax.dynamic_index_in_dim(parts, 1 - core, 2, False)
    parts = (kept.astype(f32) + swapped(sent, "dp", 1).astype(f32)).astype(kind)
    kept = lax.dynamic_index_in_dim(parts, cross, 1, False)
    sent = lax.dynamic_index_in_dim(parts, 1 - cross, 1, False)
    parts = (kept.astype(f32) + swapped(sent, "dp", 2).astype(f32)).astype(kind)
    total = lax.dynamic_index_in_dim(parts, place, 0, False).astype(f32)
    for offset in range(1, outer):
        sent = lax.dynamic_index_in_dim(parts, (place + outer - offset) % outer, 0, False)
        total = total + moved(sent, offset).astype(f32)
    return total


def scan_kernel(
    states,
    pre_ref,
    act_ref,
    gate_ref,
    dgated_ref,
    mask_ref,
    in_ref,
    out_ref,
    in_block_ref,
    out_block_ref,
    skip_ref,
    decay_ref,
    gated_ref,
    dgate_ref,
    dpre_ref,
    dact_ref,
    small_ref,
    decay_grad_ref,
    din_ref,
    dout_ref,
    step_s,
    drive_s,
    dscan_s,
    scanned_s,
    state_s,
    adjoint_s,
    rate_s,
    decay_s,
):
    tok, width = pre_ref.shape
    tiles = width // 128
    rows = chunk * states
    count = tok // chunk
    first = pl.program_id(1) == 0
    decay = -jnp.exp(decay_ref[...])
    decay_two = decay * log2e
    skip = skip_ref[0:1, :]
    row_ids = lax.broadcasted_iota(jnp.int32, (chunk, rows), 0)
    col_ids = lax.broadcasted_iota(jnp.int32, (chunk, rows), 1)
    ones_block = (lax.div(col_ids, states) == row_ids).astype(bf16)

    def spread(ref, at):
        one = ref[pl.ds(at, states), :]
        return jnp.concatenate([one] * tiles, axis=1) if tiles > 1 else one

    def softplus(v):
        return jnp.maximum(v, 0.0) + jnp.log1p(jnp.exp(-jnp.abs(v)))

    def forward(step, state):
        base = pl.multiple_of(step * chunk, chunk)
        cut = pl.ds(base, chunk)
        step_size = softplus(pre_ref[cut, :])
        keep = mask_ref[cut, 0:1]
        live = mask_ref[cut, 1:2]
        gate = gate_ref[cut, :]
        drive = step_size * act_ref[cut, :].astype(f32)
        dscan = dgated_ref[cut, :] * live * gate * jax.nn.sigmoid(gate)
        step_s[cut, :] = step_size + far * (1.0 - keep)
        drive_s[cut, :] = drive
        dscan_s[cut, :] = dscan
        for i in range(chunk):
            row = pl.ds(base + i, 1)
            at = pl.multiple_of((base + i) * states, states)
            factor = jnp.exp2(step_s[row, :] * decay_two)
            state = factor * state + drive_s[row, :] * spread(in_ref, at)
            state_s[pl.ds(at, states), :] = state
        start = pl.multiple_of(base * states, rows)
        low = state_s[pl.ds(start, rows), :].astype(bf16)
        scanned_s[cut, :] = jnp.dot(out_block_ref[cut, :], low, preferred_element_type=f32)
        part = lax.dot_general(dscan.astype(bf16), low, last_dims, preferred_element_type=f32)
        dout_ref[cut, :] = jnp.where(first, part, dout_ref[cut, :] + part)
        return state

    zero = jnp.zeros((states, width), f32)
    lax.fori_loop(0, count, forward, zero)
    decay_s[...] = zero

    def backward(back, carry):
        handed, skip_acc, bias_acc = carry
        step = count - 1 - back
        base = pl.multiple_of(step * chunk, chunk)
        cut = pl.ds(base, chunk)
        acc = decay_s[...]
        for i in reversed(range(chunk)):
            row = pl.ds(base + i, 1)
            at = pl.multiple_of((base + i) * states, states)
            step_row = step_s[row, :]
            adjoint = dscan_s[row, :] * spread(out_ref, at) + handed
            adjoint_s[pl.ds(i * states, states), :] = adjoint.astype(bf16)
            handed = jnp.exp2(step_row * decay_two) * adjoint
            if i == 0:
                before = pl.multiple_of(jnp.maximum(at - states, 0), states)
            else:
                before = pl.multiple_of((base + (i - 1)) * states, states)
            rate = handed * state_s[pl.ds(before, states), :] * decay
            rate_s[pl.ds(i * states, states), :] = rate.astype(bf16)
            acc = acc + rate * step_row
        decay_s[...] = acc
        low = adjoint_s[...]
        in_sum = jnp.dot(in_block_ref[cut, :], low, preferred_element_type=f32)
        rate_sum = jnp.dot(ones_block, rate_s[...], preferred_element_type=f32)
        part = lax.dot_general(drive_s[cut, :].astype(bf16), low, last_dims, preferred_element_type=f32)
        din_ref[cut, :] = jnp.where(first, part, din_ref[cut, :] + part)
        pre = pre_ref[cut, :]
        live = mask_ref[cut, 1:2]
        gate = gate_ref[cut, :]
        sig = jax.nn.sigmoid(gate)
        act = act_ref[cut, :].astype(f32)
        dscan = dscan_s[cut, :]
        dpre = ((rate_sum + in_sum * act) * jax.nn.sigmoid(pre)).astype(bf16)
        dpre_ref[cut, :] = dpre
        dact_ref[cut, :] = dscan * skip + in_sum * softplus(pre)
        branch = (scanned_s[cut, :] + skip * act) * live
        gated_ref[cut, :] = (branch * gate * sig).astype(bf16)
        dgate_ref[cut, :] = (dgated_ref[cut, :] * branch * sig * (1.0 + gate * (1.0 - sig))).astype(bf16)
        skip_acc = skip_acc + jnp.sum((dscan * act).reshape(chunk // 8, 8, width), axis=0)
        bias_acc = bias_acc + jnp.sum(dpre.astype(f32).reshape(chunk // 8, 8, width), axis=0)
        return handed, skip_acc, bias_acc

    eight = jnp.zeros((8, width), f32)
    _, skip_acc, bias_acc = lax.fori_loop(0, count, backward, (zero, eight, eight))
    decay_grad_ref[...] = decay_s[...]
    small_ref[0:8, :] = skip_acc
    small_ref[8:16, :] = bias_acc


def scan_both_ways(pre, act, gate, dgated, mask, in_cols, out_cols, skip, decay_log):
    micro, tok, chans = pre.shape
    states = decay_log.shape[0]
    rows = chunk * states
    width = min(512, chans)

    def lanes(cols):
        return jnp.broadcast_to(cols[..., None], cols.shape + (128,)).reshape(micro, tok * states, 128)

    same = jnp.arange(tok)[:, None] % chunk == jnp.arange(rows)[None, :] // states

    def blocked(cols):
        return jnp.where(same[None], jnp.tile(cols, (1, 1, chunk)), 0.0).astype(bf16)

    def whole(r, c):
        return pl.BlockSpec((None, r, c), lambda m, j: (m, 0, 0))

    def part(r):
        return pl.BlockSpec((None, r, width), lambda m, j: (m, 0, j))

    def param(r):
        return pl.BlockSpec((r, width), lambda m, j: (0, j))

    def shaped(r, c, kind):
        return jax.ShapeDtypeStruct((micro, r, c), kind)

    elements = micro * tok * chans * states
    gated, dgate, dpre, dact, small, decay_grad, din, dout = pl.pallas_call(
        functools.partial(scan_kernel, states),
        grid=(micro, chans // width),
        in_specs=[part(tok)] * 4
        + [whole(tok, 2)]
        + [whole(tok * states, 128)] * 2
        + [whole(tok, rows)] * 2
        + [param(1), param(states)],
        out_specs=[part(tok)] * 4 + [part(16), part(states), whole(tok, rows), whole(tok, rows)],
        out_shape=[shaped(tok, chans, bf16)] * 3
        + [shaped(tok, chans, f32), shaped(16, chans, f32), shaped(states, chans, f32)]
        + [shaped(tok, rows, f32)] * 2,
        scratch_shapes=[pltpu.VMEM((tok, width), f32)] * 4
        + [pltpu.VMEM((tok * states, width), f32)]
        + [pltpu.VMEM((rows, width), bf16)] * 2
        + [pltpu.VMEM((states, width), f32)],
        compiler_params=pltpu.CompilerParams(
            dimension_semantics=("arbitrary", "arbitrary"), vmem_limit_bytes=56 * 2**20
        ),
        cost_estimate=pl.CostEstimate(
            flops=30 * elements, bytes_accessed=24 * micro * tok * chans, transcendentals=2 * elements
        ),
    )(
        pre,
        act,
        gate,
        dgated,
        mask,
        lanes(in_cols),
        lanes(out_cols),
        blocked(in_cols),
        blocked(out_cols),
        skip[None],
        decay_log,
    )
    picks = (jnp.arange(rows)[:, None] % states == jnp.arange(states)[None, :]).astype(f32)

    def unblocked(full):
        return jnp.dot(jnp.where(same[None], full, 0.0), picks, precision=highest)

    skip_grad = jnp.sum(small[:, :8], axis=(0, 1))
    bias_grad = jnp.sum(small[:, 8:], axis=(0, 1))
    return gated, dgate, dpre, dact, skip_grad, bias_grad, jnp.sum(decay_grad, axis=0), unblocked(din), unblocked(dout)


def on_device(
    hidden,
    cotangent,
    lengths,
    order,
    norm_gain,
    input_weight,
    conv_weight,
    conv_bias,
    select_weight,
    step_weight,
    step_bias,
    decay_log,
    skip_gain,
    output_weight,
):
    micro, shard_rows, model_dim = hidden.shape
    count = lax.axis_size("dp")
    group_tok = shard_rows * lax.axis_size("tensor")
    tokens = micro * group_tok
    channels = input_weight.shape[2]
    taps = conv_weight.shape[0]
    states = decay_log.shape[0]
    own = conv_bias.shape[0]
    own_dim = norm_gain.shape[0]

    pieces = [norm_gain, conv_weight, conv_bias, step_bias, decay_log, skip_gain]
    packed = lax.all_gather(jnp.concatenate([v.reshape(-1) for v in pieces]), "dp", axis=0)
    full = []
    at = 0
    for v in pieces:
        part = packed[:, at : at + v.size]
        at += v.size
        if v.ndim == 2:
            part = part.reshape(count, v.shape[0], v.shape[1]).transpose(1, 0, 2).reshape(v.shape[0], -1)
        else:
            part = part.reshape(-1)
        full.append(part)
    gain_full, conv_w, conv_b, step_b, decay_lg, skip_g = full
    w_inner = lax.all_gather(input_weight[:, 0], "dp", axis=0, tiled=True)
    w_sel = lax.all_gather(select_weight, "dp", axis=0, tiled=True)
    w_step = lax.all_gather(step_weight, "dp", axis=0, tiled=True)
    w_gate = lax.all_gather(input_weight[:, 1], "dp", axis=0, tiled=True)
    w_out = lax.all_gather(output_weight.T, "dp", axis=0, tiled=True)
    rank_dim = w_step.shape[0]

    inverse_rms = lax.rsqrt(jnp.mean(hidden * hidden, axis=-1, keepdims=True) + epsilon)
    normal_rows = hidden * inverse_rms
    normed = tensor_gather((normal_rows * gain_full).astype(bf16), 1).reshape(tokens, model_dim)
    cot_full = tensor_gather(cotangent, 1).reshape(tokens, model_dim)

    position, live_mask = jax.vmap(lambda a, b: positions(a, b, group_tok))(lengths[:, 0], order[:, 0])
    mask = jnp.stack([(position > 0).astype(f32), live_mask], axis=2)

    inner = jnp.dot(normed, w_inner, preferred_element_type=f32).reshape(micro, group_tok, channels)
    tap_masks = [(position >= taps - 1 - t).astype(f32)[:, :, None] for t in range(taps)]
    convolved = jnp.zeros_like(inner) + conv_b
    for t in range(taps):
        convolved = convolved + conv_w[t] * delayed(inner, taps - 1 - t) * tap_masks[t]
    act_low = jax.nn.silu(convolved).astype(bf16)
    act_rows = act_low.reshape(tokens, channels)
    selected = tensor_sum(jnp.dot(act_rows, w_sel, preferred_element_type=f32))
    rank_low = selected[:, :rank_dim].astype(bf16)
    cols = selected[:, rank_dim:].reshape(micro, group_tok, 2 * states)
    pre_step = jnp.dot(rank_low, w_step, preferred_element_type=f32) + step_b
    gate = jnp.dot(normed, w_gate, preferred_element_type=f32)
    dgated = jnp.dot(cot_full, w_out, preferred_element_type=f32)

    def grouped(v):
        return v.reshape(micro, group_tok, channels)

    gated, dgate, dpre, dact, skip_grad, step_bias_grad, decay_grad, din, dout = scan_both_ways(
        grouped(pre_step),
        act_low,
        grouped(gate),
        grouped(dgated),
        mask,
        cols[..., :states],
        cols[..., states:],
        skip_g,
        decay_lg,
    )
    gated = gated.reshape(tokens, channels)
    dgate = dgate.reshape(tokens, channels)
    dpre = dpre.reshape(tokens, channels)

    out_grad = lax.dot_general(cot_full, gated, first_dims, preferred_element_type=f32).astype(bf16)
    out_grad = reduce_scatter(out_grad)
    gate_grad = lax.dot_general(normed, dgate, first_dims, preferred_element_type=f32).astype(bf16)
    gate_grad = reduce_scatter(gate_grad)
    layer_rows = hidden + tensor_scatter_matmul([(gated, w_out, last_dims)], shard_rows, micro)

    rank_grad = lax.dot_general(dpre, w_step, last_dims, preferred_element_type=f32)
    select_terms = jnp.concatenate(
        [rank_grad, din.reshape(tokens, states), dout.reshape(tokens, states)], axis=1
    )
    select_low = tensor_sum(select_terms).astype(bf16)
    step_weight_grad = lax.dot_general(rank_low, dpre, first_dims, preferred_element_type=f32)
    select_grad = lax.dot_general(select_low, act_rows, first_dims, preferred_element_type=f32)
    dact = dact + grouped(lax.dot_general(select_low, w_sel, last_dims, preferred_element_type=f32))
    conv_sig = jax.nn.sigmoid(convolved)
    dconv = dact * conv_sig * (1.0 + convolved * (1.0 - conv_sig))
    conv_bias_grad = jnp.sum(dconv, axis=(0, 1))
    conv_rows = []
    dinner = jnp.zeros_like(inner)
    for t in range(taps):
        masked = dconv * tap_masks[t]
        conv_rows.append(jnp.sum(masked * delayed(inner, taps - 1 - t), axis=(0, 1)))
        dinner = dinner + advanced(masked, taps - 1 - t) * conv_w[t]
    dinner = dinner.astype(bf16).reshape(tokens, channels)
    inner_grad = lax.dot_general(normed, dinner, first_dims, preferred_element_type=f32).astype(bf16)
    inner_grad = reduce_scatter(inner_grad)

    dnormed = tensor_scatter_matmul(
        [(dinner, w_inner, last_dims), (dgate, w_gate, last_dims)], shard_rows, micro
    )
    gain_part = jnp.sum(dnormed * normal_rows, axis=(0, 1))
    dnormal = dnormed * gain_full
    grad_rows = cotangent.astype(f32) + inverse_rms * (
        dnormal - normal_rows * jnp.mean(dnormal * normal_rows, axis=-1, keepdims=True)
    )

    vectors = jnp.concatenate(
        [jnp.stack(conv_rows + [conv_bias_grad, step_bias_grad, skip_grad]), decay_grad], axis=0
    )
    vectors = vectors.reshape(-1, count, own).transpose(1, 0, 2)
    vectors = reduce_scatter(vectors)[0]
    select_part = select_grad.astype(bf16).reshape(-1, count, own).transpose(1, 0, 2).reshape(count, -1)
    step_part = step_weight_grad.astype(bf16).reshape(count, -1)
    mixed = reduce_scatter(jnp.concatenate([select_part, step_part], axis=1))[0]
    gain_total = tensor_sum(reduce_scatter(gain_part.reshape(count, own_dim))[0])
    split = select_part.shape[1]
    return (
        layer_rows,
        grad_rows,
        gain_total,
        jnp.stack([inner_grad, gate_grad], axis=1),
        vectors[:taps],
        vectors[taps],
        mixed[:split].reshape(-1, own).T,
        mixed[split:].reshape(-1, channels),
        vectors[taps + 1],
        vectors[taps + 3 :],
        vectors[taps + 2],
        out_grad.T,
    )


def solution(mesh):
    in_specs = (
        P(None, ("dp", "tensor"), None),
        P(None, ("dp", "tensor"), None),
        P(None, "dp", None),
        P(None, "dp", None),
        P("dp"),
        P("dp", None, "tensor"),
        P(None, ("tensor", "dp")),
        P(("tensor", "dp")),
        P(("tensor", "dp"), None),
        P("dp", "tensor"),
        P(("tensor", "dp")),
        P(None, ("tensor", "dp")),
        P(("tensor", "dp")),
        P("tensor", "dp"),
    )
    out_specs = (
        P(None, ("dp", "tensor"), None),
        P(None, ("dp", "tensor"), None),
        P("dp"),
        P("dp", None, "tensor"),
        P(None, ("tensor", "dp")),
        P(("tensor", "dp")),
        P(("tensor", "dp"), None),
        P("dp", "tensor"),
        P(("tensor", "dp")),
        P(None, ("tensor", "dp")),
        P(("tensor", "dp")),
        P("tensor", "dp"),
    )
    return jax.shard_map(
        on_device, mesh=mesh, in_specs=in_specs, out_specs=out_specs, check_vma=False
    )
```

```python
import functools

import jax
import jax.numpy as jnp
from jax import lax
from jax.experimental import pallas as pl
from jax.experimental.pallas import tpu as pltpu
from jax.sharding import PartitionSpec as P

epsilon = 1e-05
log2e = 1.4426950408889634
far = 1e6
chunk = 16
f32 = jnp.float32
bf16 = jnp.bfloat16
highest = lax.Precision.HIGHEST
small_cost = pl.CostEstimate(flops=1, bytes_accessed=1, transcendentals=0)
last_dims = (((1,), (1,)), ((), ()))
first_dims = (((0,), (0,)), ((), ()))


def positions(length_row, order_row, slot_count):
    number = order_row.shape[0]
    picked = (order_row[:, None] == jnp.arange(number, dtype=jnp.int32)[None, :]).astype(jnp.int32)
    ordered = jnp.sum(picked * length_row[None, :], axis=1)
    seq_ends = jnp.cumsum(ordered)
    starts = jnp.concatenate([jnp.zeros((1,), jnp.int32), seq_ends])
    slot_ids = jnp.arange(slot_count, dtype=jnp.int32)
    seq_begin = jnp.max(jnp.where(starts[None, :] <= slot_ids[:, None], starts[None, :], 0), axis=1)
    return (slot_ids - seq_begin, (slot_ids < seq_ends[-1]).astype(jnp.float32))


def swapped(values, axis, bit):
    count = lax.axis_size(axis)
    return lax.ppermute(values, axis, [(i, i ^ bit) for i in range(count)])


def tensor_gather(values, axis):
    if lax.axis_size("tensor") != 2:
        return lax.all_gather(values, "tensor", axis=axis, tiled=True)
    other = swapped(values, "tensor", 1)
    mine_first = lax.axis_index("tensor") == 0
    low = jnp.where(mine_first, values, other)
    high = jnp.where(mine_first, other, values)
    return jnp.concatenate([low, high], axis=axis)


def tensor_sum(values):
    if lax.axis_size("tensor") != 2:
        return lax.psum(values, "tensor")
    return values + swapped(values, "tensor", 1)


def moved(values, offset):
    count = lax.axis_size("dp")
    return lax.ppermute(values, "dp", [((i + 4 * offset) % count, i) for i in range(count)])


def reduce_scatter(values):
    count = lax.axis_size("dp")
    outer = count // 4
    kind = values.dtype
    here = lax.axis_index("dp")
    parts = values.reshape((outer, 2, 2, values.shape[0] // count) + values.shape[1:])
    core = here % 2
    cross = (here // 2) % 2
    place = here // 4
    kept = lax.dynamic_index_in_dim(parts, core, 2, False)
    sent = lax.dynamic_index_in_dim(parts, 1 - core, 2, False)
    parts = (kept.astype(f32) + swapped(sent, "dp", 1).astype(f32)).astype(kind)
    kept = lax.dynamic_index_in_dim(parts, cross, 1, False)
    sent = lax.dynamic_index_in_dim(parts, 1 - cross, 1, False)
    parts = (kept.astype(f32) + swapped(sent, "dp", 2).astype(f32)).astype(kind)
    total = lax.dynamic_index_in_dim(parts, place, 0, False).astype(f32)
    for offset in range(1, outer):
        sent = lax.dynamic_index_in_dim(parts, (place + outer - offset) % outer, 0, False)
        total = total + moved(sent, offset).astype(f32)
    return total


def scan_kernel(
    states,
    pre_ref,
    act_ref,
    normed_ref,
    cot_ref,
    gate_weight_ref,
    out_weight_ref,
    rank_ref,
    step_weight_ref,
    mask_ref,
    in_ref,
    out_ref,
    in_block_ref,
    out_block_ref,
    skip_ref,
    decay_ref,
    gated_ref,
    dgate_ref,
    dact_ref,
    step_grad_ref,
    sums_ref,
    rank_grad_ref,
    din_ref,
    dout_ref,
    gate_s,
    dgated_s,
    step_s,
    drive_s,
    dscan_s,
    scanned_s,
    dpre_s,
    state_s,
    power_s,
    odd_s,
    even_s,
    odd_rate_s,
    even_rate_s,
    decay_s,
):
    tok, width = pre_ref.shape
    tiles = width // 128
    rows = chunk * states
    count = tok // chunk
    first = pl.program_id(1) == 0
    decay = -jnp.exp(decay_ref[...])
    decay_two = decay * log2e
    skip = skip_ref[0:1, :]
    row_ids = lax.broadcasted_iota(jnp.int32, (chunk, rows), 0)
    col_ids = lax.broadcasted_iota(jnp.int32, (chunk, rows), 1)
    ones_block = (lax.div(col_ids, states) == row_ids).astype(bf16)
    gate_s[...] = jnp.dot(normed_ref[...], gate_weight_ref[...], preferred_element_type=f32)
    dgated_s[...] = jnp.dot(cot_ref[...], out_weight_ref[...], preferred_element_type=f32)

    def spread(ref, at):
        one = ref[pl.ds(at, states), :]
        return jnp.concatenate([one] * tiles, axis=1) if tiles > 1 else one

    def softplus(v):
        return jnp.maximum(v, 0.0) + jnp.log1p(jnp.exp(-jnp.abs(v)))

    def run_forward(step, state, low_s):
        base = pl.multiple_of(step * chunk, chunk)
        cut = pl.ds(base, chunk)
        step_size = softplus(pre_ref[cut, :])
        keep = mask_ref[cut, 1:2]
        live = mask_ref[cut, 0:1]
        gate = gate_s[cut, :]
        step_s[cut, :] = step_size + far * (1.0 - keep)
        drive_s[cut, :] = step_size * act_ref[cut, :].astype(f32)
        dscan_s[cut, :] = dgated_s[cut, :] * live * gate * jax.nn.sigmoid(gate)
        for i in range(chunk):
            row = pl.ds(base + i, 1)
            at = pl.multiple_of((base + i) * states, states)
            power = step_s[row, :] * decay_two
            power_s[pl.ds(at, states), :] = power
            state = jnp.exp2(power) * state + drive_s[row, :] * spread(in_ref, at)
            state_s[pl.ds(at, states), :] = state
            low_s[pl.ds(i * states, states), :] = state.astype(bf16)
        return state

    def sum_forward(step, low_s):
        cut = pl.ds(pl.multiple_of(step * chunk, chunk), chunk)
        low = low_s[...]
        scanned_s[cut, :] = jnp.dot(out_block_ref[cut, :], low, preferred_element_type=f32)
        dout_ref[cut, :] = lax.dot_general(dscan_s[cut, :].astype(bf16), low, last_dims, preferred_element_type=f32)

    def forward(pair, state):
        sum_forward(jnp.maximum(2 * pair - 1, 0), odd_s)
        state = run_forward(2 * pair, state, even_s)
        sum_forward(2 * pair, even_s)
        return run_forward(2 * pair + 1, state, odd_s)

    zero = jnp.zeros((states, width), f32)
    odd_s[...] = jnp.zeros_like(odd_s)
    lax.fori_loop(0, count // 2, forward, zero)
    sum_forward(count - 1, odd_s)
    decay_s[...] = zero

    def run_backward(step, handed, low_s, rate_s):
        base = pl.multiple_of(step * chunk, chunk)
        acc = decay_s[...]
        for i in reversed(range(chunk)):
            row = pl.ds(base + i, 1)
            at = pl.multiple_of((base + i) * states, states)
            power = power_s[pl.ds(at, states), :]
            adjoint = dscan_s[row, :] * spread(out_ref, at) + handed
            low_s[pl.ds(i * states, states), :] = adjoint.astype(bf16)
            handed = jnp.exp2(power) * adjoint
            if i == 0:
                before = pl.multiple_of(jnp.maximum(at - states, 0), states)
            else:
                before = pl.multiple_of((base + (i - 1)) * states, states)
            rate = handed * state_s[pl.ds(before, states), :]
            rate_s[pl.ds(i * states, states), :] = (rate * decay).astype(bf16)
            acc = acc + rate * power
        decay_s[...] = acc
        return handed

    def sum_backward(step, low_s, rate_s, accs):
        skip_acc, bias_acc = accs
        cut = pl.ds(pl.multiple_of(step * chunk, chunk), chunk)
        low = low_s[...]
        in_sum = jnp.dot(in_block_ref[cut, :], low, preferred_element_type=f32)
        rate_sum = jnp.dot(ones_block, rate_s[...], preferred_element_type=f32)
        din_ref[cut, :] = lax.dot_general(drive_s[cut, :].astype(bf16), low, last_dims, preferred_element_type=f32)
        pre = pre_ref[cut, :]
        live = mask_ref[cut, 0:1]
        gate = gate_s[cut, :]
        sig = jax.nn.sigmoid(gate)
        act = act_ref[cut, :].astype(f32)
        dscan = dscan_s[cut, :]
        dpre = ((rate_sum + in_sum * act) * jax.nn.sigmoid(pre)).astype(bf16)
        dpre_s[cut, :] = dpre
        dact_ref[cut, :] = dscan * skip + in_sum * softplus(pre)
        branch = (scanned_s[cut, :] + skip * act) * live
        gated_ref[cut, :] = (branch * gate * sig).astype(bf16)
        dgate_ref[cut, :] = (dgated_s[cut, :] * branch * sig * (1.0 + gate * (1.0 - sig))).astype(bf16)
        skip_acc = skip_acc + jnp.sum((dscan * act).reshape(chunk // 8, 8, width), axis=0)
        bias_acc = bias_acc + jnp.sum(dpre.astype(f32).reshape(chunk // 8, 8, width), axis=0)
        return skip_acc, bias_acc

    eight = jnp.zeros((8, width), f32)
    last = count - 1
    handed = run_backward(last, zero, odd_s, odd_rate_s)

    def backward(pair, carry):
        handed, accs = carry
        step = last - 2 * pair
        accs = sum_backward(step, odd_s, odd_rate_s, accs)
        handed = run_backward(step - 1, handed, even_s, even_rate_s)
        accs = sum_backward(step - 1, even_s, even_rate_s, accs)
        handed = run_backward(step - 2, handed, odd_s, odd_rate_s)
        return handed, accs

    handed, accs = lax.fori_loop(0, count // 2 - 1, backward, (handed, (eight, eight)))
    accs = sum_backward(1, odd_s, odd_rate_s, accs)
    run_backward(0, handed, even_s, even_rate_s)
    skip_acc, bias_acc = sum_backward(0, even_s, even_rate_s, accs)
    rank_grad_ref[...] = lax.dot_general(dpre_s[...], step_weight_ref[...], last_dims, preferred_element_type=f32)
    step_part = lax.dot_general(rank_ref[...], dpre_s[...], first_dims, preferred_element_type=f32)
    small = jnp.concatenate(
        [jnp.sum(skip_acc, axis=0, keepdims=True), jnp.sum(bias_acc, axis=0, keepdims=True), jnp.zeros((6, width), f32)],
        axis=0,
    )

    @pl.when(first)
    def _():
        step_grad_ref[...] = step_part
        sums_ref[0:8, :] = small
        sums_ref[8:, :] = decay_s[...] * (1.0 / log2e)

    @pl.when(jnp.logical_not(first))
    def _():
        step_grad_ref[...] += step_part
        sums_ref[0:8, :] += small
        sums_ref[8:, :] += decay_s[...] * (1.0 / log2e)


def scan_both_ways(start, blocks, width, pre, act, normed, cot, weights, rank_low, step_weight, mask, tables, skip, decay_log):
    micro, tok, chans = pre.shape
    dim = normed.shape[2]
    states = decay_log.shape[0]
    rows = chunk * states
    rank = rank_low.shape[2]
    inside = start % (weights.shape[2] // width)

    def whole(r, c):
        return pl.BlockSpec((None, r, c), lambda j, m: (m, 0, 0))

    def each(r, c):
        return pl.BlockSpec((None, None, r, c), lambda j, m: (j, m, 0, 0))

    def part(r):
        return pl.BlockSpec((None, r, width), lambda j, m: (m, 0, j))

    def later(r):
        return pl.BlockSpec((None, r, width), lambda j, m: (m, 0, j + start))

    def param(r, at):
        return pl.BlockSpec((r, width), lambda j, m: (0, j + at))

    def shaped(*dims, kind=f32):
        return jax.ShapeDtypeStruct(dims, kind)

    total = blocks * width
    return pl.pallas_call(
        functools.partial(scan_kernel, states),
        grid=(blocks, micro),
        in_specs=[later(tok)] * 2
        + [whole(tok, dim)] * 2
        + [pl.BlockSpec((None, dim, width), lambda j, m, k=k: (k, 0, j + inside)) for k in range(2)]
        + [whole(tok, rank), param(rank, start), whole(tok, mask.shape[2])]
        + [whole(tok * states, 128)] * 2
        + [whole(tok, rows)] * 2
        + [param(1, start), param(states, start)],
        out_specs=[part(tok)] * 3
        + [param(rank, 0), param(8 + states, 0), each(tok, rank), each(tok, rows), each(tok, rows)],
        out_shape=[shaped(micro, tok, total, kind=bf16)] * 2
        + [shaped(micro, tok, total), shaped(rank, total), shaped(8 + states, total)]
        + [shaped(blocks, micro, tok, rank), shaped(blocks, micro, tok, rows), shaped(blocks, micro, tok, rows)],
        scratch_shapes=[pltpu.VMEM((tok, width), f32)] * 6
        + [pltpu.VMEM((tok, width), bf16)]
        + [pltpu.VMEM((tok * states, width), f32)] * 2
        + [pltpu.VMEM((rows, width), bf16)] * 4
        + [pltpu.VMEM((states, width), f32)],
        compiler_params=pltpu.CompilerParams(
            dimension_semantics=("arbitrary", "arbitrary"), vmem_limit_bytes=58 * 2**20
        ),
        cost_estimate=small_cost,
    )(pre, act, normed, cot, weights, weights, rank_low, step_weight, mask, *tables, skip[None], decay_log)


def halves(values):
    high = values.astype(bf16)
    return high, (values - high.astype(f32)).astype(bf16)


def middle_kernel(states, selected_ref, weight_ref, bias_ref, pre_ref, rank_ref, in_ref, out_ref, in_block_ref, out_block_ref):
    tokens = selected_ref.shape[0]
    rank = weight_ref.shape[0]
    rows = chunk * states
    selected = selected_ref[...]
    low = selected[:, :rank].astype(bf16)
    rank_ref[...] = low
    pre_ref[...] = jnp.dot(low, weight_ref[...], preferred_element_type=f32) + bias_ref[...]
    state_ids = lax.broadcasted_iota(jnp.int32, (states, rows), 0)
    col_ids = lax.broadcasted_iota(jnp.int32, (states, rows), 1)
    spreading = (lax.rem(col_ids, states) == state_ids).astype(bf16)
    row_ids = lax.broadcasted_iota(jnp.int32, (chunk, rows), 0)
    chunk_cols = lax.broadcasted_iota(jnp.int32, (chunk, rows), 1)
    same = lax.div(chunk_cols, states) == row_ids
    ones = jnp.ones((2 * chunk, 128), bf16)
    for at, lanes_ref, block_ref in ((rank, in_ref, in_block_ref), (rank + states, out_ref, out_block_ref)):
        tiled = [
            jnp.dot(v, spreading, preferred_element_type=f32) for v in halves(selected[:, at : at + states])
        ]
        for i in range(tokens // chunk):
            cut = slice(i * chunk, (i + 1) * chunk)
            high, rest = [jnp.where(same, v[cut], 0.0).astype(bf16) for v in tiled]
            block_ref[cut, :] = high
            lanes_ref[i * rows : (i + 1) * rows, :] = lax.dot_general(
                jnp.concatenate([high, rest], axis=0), ones, first_dims, preferred_element_type=f32
            )


def middle(selected, weight, bias, states):
    tokens, picked = selected.shape
    rank, channels = weight.shape
    rows = chunk * states
    cut = min(128, tokens)

    def fixed(r, c):
        return pl.BlockSpec((r, c), lambda i: (0, 0))

    def part(r, c):
        return pl.BlockSpec((r, c), lambda i: (i, 0))

    def shaped(r, c, kind):
        return jax.ShapeDtypeStruct((r, c), kind)

    return pl.pallas_call(
        functools.partial(middle_kernel, states),
        grid=(tokens // cut,),
        in_specs=[part(cut, picked), fixed(rank, channels), fixed(1, channels)],
        out_specs=[part(cut, channels), part(cut, rank)]
        + [part(cut * states, 128)] * 2
        + [part(cut, rows)] * 2,
        out_shape=[shaped(tokens, channels, f32), shaped(tokens, rank, bf16)]
        + [shaped(tokens * states, 128, f32)] * 2
        + [shaped(tokens, rows, bf16)] * 2,
        compiler_params=pltpu.CompilerParams(dimension_semantics=("arbitrary",), vmem_limit_bytes=48 * 2**20),
    )(selected, weight, bias[None])


def unblocked(fulls, states):
    tok, rows = fulls[0].shape[2:]
    same = jnp.arange(tok)[:, None] % chunk == jnp.arange(rows)[None, :] // states
    picks = (jnp.arange(rows)[:, None] % states == jnp.arange(states)[None, :]).astype(f32)
    full = sum(v[j] for v in fulls for j in range(v.shape[0]))
    return jnp.dot(jnp.where(same[None], full, 0.0), picks, precision=highest)


def behind(values, steps):
    return values if steps == 0 else pltpu.roll(values, steps, 0)


def ahead(values, steps):
    return values if steps == 0 else pltpu.roll(values, values.shape[0] - steps, 0)


def convolve(inner, mask_ref, weight_ref, bias_ref):
    taps = weight_ref.shape[0]
    total = bias_ref[...] + weight_ref[taps - 1 : taps, :] * inner
    for back in range(1, taps):
        tap = taps - 1 - back
        total = total + weight_ref[tap : tap + 1, :] * behind(inner, back) * mask_ref[:, back : back + 1]
    return total


def inner_kernel(normed_ref, weight_ref, mask_ref, conv_ref, bias_ref, select_ref, inner_ref, act_ref, selected_ref):
    inner = jnp.dot(normed_ref[...], weight_ref[...], preferred_element_type=f32)
    inner_ref[...] = inner
    convolved = convolve(inner, mask_ref, conv_ref, bias_ref)
    act = (convolved * jax.nn.sigmoid(convolved)).astype(bf16)
    act_ref[...] = act
    part = jnp.dot(act, select_ref[...], preferred_element_type=f32)
    selected_ref[...] = jnp.where(pl.program_id(0) == 0, part, selected_ref[...] + part)


def inner_forward(normed, weight, mask, conv_w, conv_b, select):
    tokens, dim = normed.shape
    channels = weight.shape[1]
    width = min(256, channels)
    taps = conv_w.shape[0]
    picked = select.shape[1]

    def fixed(r, c):
        return pl.BlockSpec((r, c), lambda j: (0, 0))

    def part(r):
        return pl.BlockSpec((r, width), lambda j: (0, j))

    return pl.pallas_call(
        inner_kernel,
        grid=(channels // width,),
        in_specs=[
            fixed(tokens, dim),
            part(dim),
            fixed(tokens, mask.shape[1]),
            part(taps),
            part(1),
            pl.BlockSpec((width, picked), lambda j: (j, 0)),
        ],
        out_specs=[part(tokens), part(tokens), fixed(tokens, picked)],
        out_shape=[
            jax.ShapeDtypeStruct((tokens, channels), f32),
            jax.ShapeDtypeStruct((tokens, channels), bf16),
            jax.ShapeDtypeStruct((tokens, picked), f32),
        ],
        compiler_params=pltpu.CompilerParams(dimension_semantics=("arbitrary",), vmem_limit_bytes=48 * 2**20),
        cost_estimate=small_cost,
    )(normed, weight, mask, conv_w, conv_b[None], select)


def inner_back_kernel(bounds, places_ref, *refs):
    *dact_refs, dsel_ref, select_ref, inner_ref, act_ref, mask_ref, conv_ref, bias_ref, left_ref = refs[:-6]
    dinner_ref, sums_ref, select_grad_ref, sent_ref, kept_ref, dact_s = refs[-6:]
    taps = conv_ref.shape[0]
    tile = pl.program_id(0)
    for ref, low, high in zip(dact_refs, bounds[:-1], bounds[1:]):

        @pl.when(jnp.logical_and(tile >= low, tile < high))
        def _(ref=ref):
            dact_s[...] = ref[...]

    inner = inner_ref[...]
    dsel = dsel_ref[...]
    convolved = convolve(inner, mask_ref, conv_ref, bias_ref)
    sig = jax.nn.sigmoid(convolved)
    dact = dact_s[...] + lax.dot_general(dsel, select_ref[...], last_dims, preferred_element_type=f32)
    dconv = dact * sig * (1.0 + convolved * (1.0 - sig))
    dinner = conv_ref[taps - 1 : taps, :] * dconv
    sums_ref[taps : taps + 1, :] = jnp.sum(dconv, axis=0, keepdims=True)
    sums_ref[taps - 1 : taps, :] = jnp.sum(dconv * inner, axis=0, keepdims=True)
    for back in range(1, taps):
        tap = taps - 1 - back
        masked = dconv * mask_ref[:, back : back + 1]
        sums_ref[tap : tap + 1, :] = jnp.sum(masked * behind(inner, back), axis=0, keepdims=True)
        dinner = dinner + conv_ref[tap : tap + 1, :] * ahead(masked, back)
    low = dinner.astype(bf16)
    dinner_ref[...] = low
    select_grad_ref[...] = lax.dot_general(
        dsel, act_ref[...], first_dims, preferred_element_type=f32
    ).astype(bf16)
    outer, own = kept_ref.shape[1], kept_ref.shape[3]
    for core, out_ref in ((1, sent_ref), (0, kept_ref)):
        for cross in range(2):
            at = (2 * core + cross) * outer
            rows = [
                left_ref[pl.ds(pl.multiple_of(places_ref[at + j] * own, own), own), :] for j in range(outer)
            ]
            full = jnp.dot(jnp.concatenate(rows, axis=0), low, preferred_element_type=f32).astype(bf16)
            for j in range(outer):
                out_ref[cross, j, 0] = full[j * own : (j + 1) * own]


def inner_backward(places, dacts, dsel, select, inner, act, mask, conv_w, conv_b, left):
    tokens, channels = inner.shape
    count = places.shape[0]
    outer, own = count // 4, left.shape[0] // count
    width = min([256] + [v.shape[1] for v in dacts])
    taps = conv_w.shape[0]
    picked = select.shape[1]
    bounds = [0]
    for v in dacts:
        bounds.append(bounds[-1] + v.shape[1] // width)

    def fixed(r, c):
        return pl.BlockSpec((r, c), lambda j, _: (0, 0))

    def part(r):
        return pl.BlockSpec((r, width), lambda j, _: (0, j))

    def held(low, high):
        return pl.BlockSpec((tokens, width), lambda j, _: (0, jnp.clip(j - low, 0, high - low - 1)))

    parts = pl.BlockSpec((2, outer, 1, own, width), lambda j, _: (0, 0, 0, 0, j))
    return pl.pallas_call(
        functools.partial(inner_back_kernel, tuple(bounds)),
        grid_spec=pltpu.PrefetchScalarGridSpec(
            num_scalar_prefetch=1,
            grid=(channels // width,),
            in_specs=[held(low, high) for low, high in zip(bounds[:-1], bounds[1:])]
            + [
                fixed(tokens, picked),
                pl.BlockSpec((width, picked), lambda j, _: (j, 0)),
                part(tokens),
                part(tokens),
                fixed(tokens, mask.shape[1]),
                part(taps),
                part(1),
                fixed(*left.shape),
            ],
            out_specs=[part(tokens), part(8), part(picked), parts, parts],
            scratch_shapes=[pltpu.VMEM((tokens, width), f32)],
        ),
        out_shape=[
            jax.ShapeDtypeStruct((tokens, channels), bf16),
            jax.ShapeDtypeStruct((8, channels), f32),
            jax.ShapeDtypeStruct((picked, channels), bf16),
        ]
        + [jax.ShapeDtypeStruct((2, outer, 1, own, channels), bf16)] * 2,
        compiler_params=pltpu.CompilerParams(dimension_semantics=("arbitrary",), vmem_limit_bytes=52 * 2**20),
        cost_estimate=small_cost,
    )(places, *dacts, dsel, select, inner, act, mask, conv_w, conv_b[None], left)


def project_kernel(micro, count, where_ref, *refs):
    lefts, rights = refs[:count], refs[count : 2 * count]
    here_ref, away_ref, total_s = refs[2 * count :]
    total = None
    for left, right in zip(lefts, rights):
        part = lax.dot_general(left[...], right[...], last_dims, preferred_element_type=f32)
        total = part if total is None else total + part
    total_s[...] = total
    group = total.shape[0] // micro
    rows = here_ref.shape[1]
    here = where_ref[0] * rows
    for m in range(micro):
        here_ref[m] = total_s[pl.ds(pl.multiple_of(m * group + here, rows), rows), :]
        away_ref[m] = total_s[pl.ds(pl.multiple_of(m * group + (group - rows) - here, rows), rows), :].astype(bf16)


def project(lefts, rights, places, micro, shard_rows):
    tokens = lefts[0].shape[0]
    dim = rights[0].shape[1]
    width = min(256, dim)
    where = lax.axis_index("tensor").astype(jnp.int32)[None]

    def column(plane, at, wide):
        return pl.BlockSpec((None, width, wide), lambda i, _: (plane, i, at))

    return pl.pallas_call(
        functools.partial(project_kernel, micro, len(lefts)),
        grid_spec=pltpu.PrefetchScalarGridSpec(
            num_scalar_prefetch=1,
            grid=(dim // width,),
            in_specs=[pl.BlockSpec(v.shape, lambda i, _: (0, 0)) for v in lefts]
            + [column(*at, v.shape[1]) for at, v in zip(places, lefts)],
            out_specs=[pl.BlockSpec((micro, shard_rows, width), lambda i, _: (0, 0, i))] * 2,
            scratch_shapes=[pltpu.VMEM((tokens, width), f32)],
        ),
        out_shape=[
            jax.ShapeDtypeStruct((micro, shard_rows, dim), f32),
            jax.ShapeDtypeStruct((micro, shard_rows, dim), bf16),
        ],
        compiler_params=pltpu.CompilerParams(dimension_semantics=("arbitrary",), vmem_limit_bytes=48 * 2**20),
        cost_estimate=small_cost,
    )(where, *lefts, *rights)


def spread_sum(lefts, rights, places, micro, shard_rows):
    if lax.axis_size("tensor") == 2:
        here, away = project(lefts, rights, places, micro, shard_rows)
        return here, swapped(away, "tensor", 1)
    total = 0.0
    for left, right, (plane, at) in zip(lefts, rights, places):
        wide = left.shape[1]
        total = total + lax.dot_general(
            left, right[plane, :, at * wide : (at + 1) * wide], last_dims, preferred_element_type=f32
        )
    total = total.reshape(micro, -1, total.shape[1])
    away = lax.psum_scatter(total.astype(bf16), "tensor", scatter_dimension=1, tiled=True)
    return jnp.zeros(away.shape, f32), away


def parts_kernel(kinds, outer, places_ref, *refs):
    out_ref = refs[-1]
    own = refs[0].shape[0]
    for kind in range(kinds):
        left = jnp.concatenate([r[...] for r in refs[kind * outer : (kind + 1) * outer]], axis=0)
        full = jnp.dot(left, refs[kinds * outer + kind][...], preferred_element_type=f32).astype(bf16)
        for j in range(outer):
            out_ref[j, kind] = full[j * own : (j + 1) * own]


def grad_parts(places, near, lefts, rights):
    kinds = len(lefts)
    count = places.shape[0]
    outer = count // 4
    own = lefts[0].shape[0] // count
    tokens = lefts[0].shape[1]
    width = rights[0].shape[1]
    offset = 0 if near else 2 * outer

    def left_spec(j):
        return pl.BlockSpec((own, tokens), lambda q, where: (where[offset + q * outer + j], 0))

    return pl.pallas_call(
        functools.partial(parts_kernel, kinds, outer),
        grid_spec=pltpu.PrefetchScalarGridSpec(
            num_scalar_prefetch=1,
            grid=(2,),
            in_specs=[left_spec(j) for _ in range(kinds) for j in range(outer)]
            + [pl.BlockSpec(v.shape, lambda q, where: (0, 0)) for v in rights],
            out_specs=pl.BlockSpec((None, outer, kinds, own, width), lambda q, where: (q, 0, 0, 0, 0)),
        ),
        out_shape=jax.ShapeDtypeStruct((2, outer, kinds, own, width), bf16),
        compiler_params=pltpu.CompilerParams(dimension_semantics=("arbitrary",), vmem_limit_bytes=48 * 2**20),
        cost_estimate=small_cost,
    )(places, *[v for v in lefts for _ in range(outer)], *rights)


def join(*trees):
    return lax.optimization_barrier(trees)


def summed(first, second, *more):
    total = first.astype(f32) + second.astype(f32)
    for v in more:
        total = total + v.astype(f32)
    return total


def sums_kernel(crosses, alongs, outer, *refs):
    given = iter(refs[: 2 * crosses + 3 * alongs])
    outs = iter(refs[2 * crosses + 3 * alongs :])
    for _ in range(crosses):
        kept, got = next(given), next(given)
        next(outs)[...] = (kept[...].astype(f32) + got[...].astype(f32)).astype(bf16)
    for _ in range(alongs):
        kept, got, across = next(given), next(given), next(given)
        next(outs)[...] = kept[0].astype(f32) + got[0].astype(f32) + across[0].astype(f32)
        for j in range(1, outer):
            next(outs)[...] = (kept[j].astype(f32) + got[j].astype(f32) + across[j].astype(f32)).astype(bf16)


def step_sums(crosses, alongs):
    cuts = 4
    in_specs, out_specs, out_shape, given = [], [], [], []
    outer = (crosses + alongs)[0][0].shape[1]

    def taken(shape, first, at, wide):
        block = (None,) + shape[1:-2] + (shape[-2] // cuts, wide)
        return pl.BlockSpec(block, lambda i: (first,) + (0,) * (len(shape) - 3) + (i, at))

    def plain(shape):
        return pl.BlockSpec(shape[:-2] + (shape[-2] // cuts, shape[-1]), lambda i: (0,) * (len(shape) - 2) + (i, 0))

    for kept, got, (at, wide) in crosses:
        shape = kept.shape
        in_specs += [taken(shape, 1, at, wide)] * 2
        given += [kept, got]
        out = shape[1:-1] + (wide,)
        out_specs.append(plain(out))
        out_shape.append(jax.ShapeDtypeStruct(out, bf16))
    for kept, got, across, (at, wide) in alongs:
        shape = kept.shape
        in_specs += [taken(shape, 0, at, wide)] * 2 + [plain(across.shape)]
        given += [kept, got, across]
        out = shape[2:-1] + (wide,)
        out_specs += [plain(out)] * outer
        out_shape += [jax.ShapeDtypeStruct(out, f32 if j == 0 else bf16) for j in range(outer)]
    outs = pl.pallas_call(
        functools.partial(sums_kernel, len(crosses), len(alongs), outer),
        grid=(cuts,),
        in_specs=in_specs,
        out_specs=out_specs,
        out_shape=out_shape,
        compiler_params=pltpu.CompilerParams(dimension_semantics=("arbitrary",), vmem_limit_bytes=48 * 2**20),
        cost_estimate=small_cost,
    )(*given)
    outs = list(outs)
    first, rest = outs[: len(crosses)], outs[len(crosses) :]
    return first, [rest[i * outer : (i + 1) * outer] for i in range(len(alongs))]


def along_moves(rows):
    count = lax.axis_size("dp")
    return rows[:1] + [
        lax.ppermute(v, "dp", [(i, (i + 4 * (j + 1)) % count) for i in range(count)])
        for j, v in enumerate(rows[1:])
    ]


def final_kernel(kinds, *refs):
    *terms, out_ref = refs[: len(refs) - kinds + 1]
    outs = (out_ref,) + refs[len(refs) - kinds + 1 :]
    total = terms[0][...]
    for ref in terms[1:]:
        total = total + ref[...].astype(f32)
    outs[0][...] = total[0]
    if kinds == 2:
        outs[1][...] = total[1].T


def final_sum(terms):
    kinds, own, width = terms[0].shape
    return pl.pallas_call(
        functools.partial(final_kernel, kinds),
        out_shape=[jax.ShapeDtypeStruct((own, width), f32), jax.ShapeDtypeStruct((width, own), f32)][:kinds],
        compiler_params=pltpu.CompilerParams(vmem_limit_bytes=48 * 2**20),
        cost_estimate=small_cost,
    )(*terms)


def doubled(values):
    count = lax.axis_size("dp")
    here = lax.axis_index("dp")
    values = values[None]
    bit = 1
    while bit < count:
        other = swapped(values, "dp", bit)
        low = (here & bit) == 0
        values = jnp.concatenate([jnp.where(low, values, other), jnp.where(low, other, values)], axis=0)
        bit *= 2
    return values


def on_device(
    hidden,
    cotangent,
    lengths,
    order,
    norm_gain,
    input_weight,
    conv_weight,
    conv_bias,
    select_weight,
    step_weight,
    step_bias,
    decay_log,
    skip_gain,
    output_weight,
):
    micro, shard_rows, model_dim = hidden.shape
    count = lax.axis_size("dp")
    outer = count // 4
    group_tok = shard_rows * lax.axis_size("tensor")
    tokens = micro * group_tok
    channels = input_weight.shape[2]
    taps = conv_weight.shape[0]
    states = decay_log.shape[0]
    own = conv_bias.shape[0]
    own_dim = norm_gain.shape[0]
    half = channels // 2
    quarter = channels // 4
    here = lax.axis_index("dp")
    ids = jnp.arange(count, dtype=jnp.int32)
    place, cross, core = here // 4, (here // 2) % 2, here % 2
    places = ((place + ids % outer) % outer) * 4 + (cross ^ (ids // outer) % 2) * 2 + (core ^ ids // (2 * outer))
    places = places.astype(jnp.int32)

    pieces = [norm_gain, conv_weight, conv_bias, step_bias, decay_log, skip_gain]
    packed = doubled(jnp.concatenate([v.reshape(-1) for v in pieces]))
    picked = select_weight.shape[1]
    narrow, packed = join(jnp.concatenate([select_weight.T, step_weight.reshape(-1, own)], axis=0), packed)
    full = []
    at = 0
    for v in pieces:
        part = packed[:, at : at + v.size]
        at += v.size
        if v.ndim == 2:
            part = part.reshape(count, v.shape[0], v.shape[1]).transpose(1, 0, 2).reshape(v.shape[0], -1)
        else:
            part = part.reshape(-1)
        full.append(part)
    gain_full, conv_w, conv_b, step_b, decay_lg, skip_g = full
    narrow = doubled(narrow)
    w_sel = narrow[:, :picked].transpose(0, 2, 1).reshape(channels, picked)
    w_step = narrow[:, picked:].reshape(-1, channels)

    w_inner = lax.all_gather(input_weight[:, 0], "dp", axis=0, tiled=True)
    out_shard = output_weight.T
    weights = []
    for number in range(2):
        cut = slice(number * half, (number + 1) * half)
        both = jnp.stack([input_weight[:, 1, cut], out_shard[:, cut]])
        weights.append(lax.all_gather(both, "dp", axis=1, tiled=True))

    inverse_rms = lax.rsqrt(jnp.mean(hidden * hidden, axis=-1, keepdims=True) + epsilon)
    normal_rows = hidden * inverse_rms
    normed = tensor_gather((normal_rows * gain_full).astype(bf16), 1).reshape(tokens, model_dim)
    normed, cot_rows = join(normed, cotangent)
    cot_full = tensor_gather(cot_rows, 1).reshape(tokens, model_dim)

    position, live_mask = jax.vmap(lambda a, b: positions(a, b, group_tok))(lengths[:, 0], order[:, 0])
    mask = jnp.stack([live_mask] + [(position >= back).astype(f32) for back in range(1, taps)], axis=2)
    flat_mask = mask.reshape(tokens, taps)

    def grouped(v):
        return v.reshape(micro, group_tok, v.shape[-1])

    inner, act, selected = inner_forward(normed, w_inner, flat_mask, conv_w, conv_b, w_sel)
    selected = tensor_sum(selected)
    lefts = (normed.T, cot_full.T)
    pre_step, rank_low, *tables = middle(selected, w_step, step_b, states)
    tables = tuple(grouped(v) if v.shape[0] == tokens else v.reshape(micro, -1, v.shape[-1]) for v in tables)
    rank_rows = grouped(rank_low)

    gated, dgate, dact, step_grads, sums, rank_grads, dins, douts = [[] for _ in range(8)]
    rows_now = (grouped(normed), grouped(cot_full))
    kept, got, across, total = {}, {}, {}, {}
    stages = ((0, 2), (2, 1), (3, 1))

    def whole(piece):
        return kept[piece], got[piece], (0, kept[piece].shape[-1])

    def whole_across(piece):
        return kept[piece], got[piece], across[piece], (0, kept[piece].shape[-1])

    for number, (start, blocks) in enumerate(stages):
        cross, along = (), ()
        if number > 0:
            cross, along = step_sums(
                [whole(number - 1)], [whole_across(number - 2)] if number > 1 else []
            )
        rows_now, cross, along = join(rows_now, cross, along)
        cross = [swapped(v, "dp", 2) for v in cross]
        along = [along_moves(v) for v in along]
        results = scan_both_ways(
            start,
            blocks,
            quarter,
            grouped(pre_step),
            grouped(act),
            *rows_now,
            weights[start // 2],
            rank_rows,
            w_step,
            mask,
            tables,
            skip_g,
            decay_lg,
        )
        results, cross, along = join(results, cross, along)
        if number > 0:
            across[number - 1] = cross[0]
        if number > 1:
            total[number - 2] = along[0]
        for held, v in zip((gated, dgate, dact), results[:3]):
            held.append(v.reshape(tokens, -1))
        for held, v in zip((step_grads, sums, rank_grads, dins, douts), results[3:]):
            held.append(v)
        if number == 2:
            break
        rights = (dgate[number], gated[number])
        sent = grad_parts(places, False, lefts, rights)
        sent, lefts = join(sent, lefts)
        got[number] = swapped(sent, "dp", 1)
        kept[number] = grad_parts(places, True, lefts, rights)
        rows_now, kept[number] = join(rows_now, kept[number])

    rank_grad = sum(v[j] for v in rank_grads for j in range(v.shape[0]))
    select_terms = jnp.concatenate([rank_grad, unblocked(dins, states), unblocked(douts, states)], axis=2)
    select_terms = select_terms.reshape(tokens, -1)
    select_terms, gated[2], dgate[2], lefts = join(select_terms, gated[2], dgate[2], lefts)
    select_terms = tensor_sum(select_terms)
    sent = grad_parts(places, False, lefts, (dgate[2], gated[2]))
    sent, lefts = join(sent, lefts)
    got[2] = swapped(sent, "dp", 1)
    kept[2] = grad_parts(places, True, lefts, (dgate[2], gated[2]))
    got[2], kept[2], select_terms = join(got[2], kept[2], select_terms)
    select_low = select_terms.astype(bf16)
    cross, along = step_sums([whole(2)], [whole_across(1)])
    cross, along, select_low = join(cross, along, select_low)
    across[2] = swapped(cross[0], "dp", 2)
    along = along_moves(along[0])
    dinner, conv_sums, select_grad, sent, kept[3] = inner_backward(
        places, dact, select_low, w_sel, inner, act, flat_mask, conv_w, conv_b, lefts[0]
    )
    across[2], along, dinner, conv_sums, select_grad, sent, kept[3] = join(
        across[2], along, dinner, conv_sums, select_grad, sent, kept[3]
    )
    total[1] = along

    got[3] = swapped(sent, "dp", 1)
    mixed_select = select_grad.reshape(-1, count, own).transpose(1, 0, 2).reshape(count, own_dim, -1)
    mixed_step = jnp.concatenate(step_grads, axis=1).astype(bf16).reshape(count, own_dim, -1)
    split = mixed_select.shape[2]
    mixed = jnp.take(jnp.concatenate([mixed_select, mixed_step], axis=2), places, axis=0)
    mixed = mixed.reshape((2, 2, outer, 1) + mixed.shape[1:])
    kept[4] = mixed[0]
    got[4] = swapped(mixed[1], "dp", 1)
    _, along = step_sums([], [whole_across(2)])
    got[3], along, kept[4], got[4] = join(got[3], along, kept[4], got[4])
    along = along_moves(along[0])
    cross, _ = step_sums([(kept[3], got[3], (0, half)), (kept[3], got[3], (1, half)), whole(4)], [])
    first, second = swapped(cross[0], "dp", 2), cross[1]
    across[4] = swapped(cross[2], "dp", 2)
    norm_here, norm_away = spread_sum(
        dgate + [dinner],
        [weights[0], weights[1], weights[1], w_inner[None]],
        [(0, 0), (0, 0), (0, 1), (0, 0)],
        micro,
        shard_rows,
    )
    first, across[4], along, second, norm_here = join(first, across[4], along, second, norm_here)
    total[2] = along
    _, along = step_sums([], [(kept[3], got[3], first, (0, half)), whole_across(4)])
    second, along, gated = join(second, along, gated)
    second = swapped(second, "dp", 2)
    along = [along_moves(v) for v in along]
    layer_here, layer_away = spread_sum(
        gated, [weights[0], weights[1], weights[1]], [(1, 0), (1, 0), (1, 1)], micro, shard_rows
    )
    dnormed = norm_here + norm_away.astype(f32)
    gain_part = jnp.sum(dnormed * normal_rows, axis=(0, 1))
    vectors = jnp.concatenate([conv_sums[: taps + 1], jnp.concatenate(sums, axis=1)], axis=0)
    vectors = vectors.reshape(-1, count, own).transpose(1, 0, 2).reshape(count, -1)
    vectors = jnp.concatenate([gain_part.reshape(count, own_dim), vectors], axis=1)
    second, along, layer_here, vectors = join(second, along, layer_here, vectors)
    total[3], total[4] = along
    _, along = step_sums([], [(kept[3], got[3], second, (1, half))])
    along, vectors = join(along, vectors)
    total[5] = along_moves(along[0])
    vectors = reduce_scatter(vectors)[0]
    gain_total = tensor_sum(vectors[:own_dim])
    vectors = vectors[own_dim:].reshape(-1, own)

    layer_rows = hidden + (layer_here + layer_away.astype(f32))
    dnormal = dnormed * gain_full
    grad_rows = cotangent.astype(f32) + inverse_rms * (
        dnormal - normal_rows * jnp.mean(dnormal * normal_rows, axis=-1, keepdims=True)
    )
    sums_of = [final_sum(total[n]) for n in range(6)]
    gate_grad = jnp.concatenate([v[0] for v in sums_of[:3]], axis=1)
    out_grad = jnp.concatenate([v[1] for v in sums_of[:3]], axis=0)
    inner_grad = jnp.concatenate([sums_of[3][0], sums_of[5][0]], axis=1)
    mixed = sums_of[4][0]
    return (
        layer_rows,
        grad_rows,
        gain_total,
        jnp.stack([inner_grad, gate_grad], axis=1),
        vectors[:taps],
        vectors[taps],
        mixed[:, :split].reshape(-1, own).T,
        mixed[:, split:].reshape(-1, channels),
        vectors[taps + 2],
        vectors[taps + 9 :],
        vectors[taps + 1],
        out_grad,
    )


def solution(mesh):
    in_specs = (
        P(None, ("dp", "tensor"), None),
        P(None, ("dp", "tensor"), None),
        P(None, "dp", None),
        P(None, "dp", None),
        P("dp"),
        P("dp", None, "tensor"),
        P(None, ("tensor", "dp")),
        P(("tensor", "dp")),
        P(("tensor", "dp"), None),
        P("dp", "tensor"),
        P(("tensor", "dp")),
        P(None, ("tensor", "dp")),
        P(("tensor", "dp")),
        P("tensor", "dp"),
    )
    out_specs = (
        P(None, ("dp", "tensor"), None),
        P(None, ("dp", "tensor"), None),
        P("dp"),
        P("dp", None, "tensor"),
        P(None, ("tensor", "dp")),
        P(("tensor", "dp")),
        P(("tensor", "dp"), None),
        P("dp", "tensor"),
        P(("tensor", "dp")),
        P(None, ("tensor", "dp")),
        P(("tensor", "dp")),
        P("tensor", "dp"),
    )
    return jax.shard_map(
        on_device, mesh=mesh, in_specs=in_specs, out_specs=out_specs, check_vma=False
    )
```

```python
import functools

import jax
import jax.numpy as jnp
from jax import lax
from jax.experimental import pallas as pl
from jax.experimental.pallas import tpu as pltpu
from jax.sharding import PartitionSpec as P

epsilon = 1e-05
log2e = 1.4426950408889634
far = 1e6
chunk = 16
f32 = jnp.float32
bf16 = jnp.bfloat16
highest = lax.Precision.HIGHEST
small_cost = pl.CostEstimate(flops=1, bytes_accessed=1, transcendentals=0)
last_dims = (((1,), (1,)), ((), ()))
first_dims = (((0,), (0,)), ((), ()))


def positions(length_row, order_row, slot_count):
    number = order_row.shape[0]
    picked = (order_row[:, None] == jnp.arange(number, dtype=jnp.int32)[None, :]).astype(jnp.int32)
    ordered = jnp.sum(picked * length_row[None, :], axis=1)
    seq_ends = jnp.cumsum(ordered)
    starts = jnp.concatenate([jnp.zeros((1,), jnp.int32), seq_ends])
    slot_ids = jnp.arange(slot_count, dtype=jnp.int32)
    seq_begin = jnp.max(jnp.where(starts[None, :] <= slot_ids[:, None], starts[None, :], 0), axis=1)
    return (slot_ids - seq_begin, (slot_ids < seq_ends[-1]).astype(jnp.float32))


def swapped(values, axis, bit):
    count = lax.axis_size(axis)
    return lax.ppermute(values, axis, [(i, i ^ bit) for i in range(count)])


def tensor_gather(values, axis):
    if lax.axis_size("tensor") != 2:
        return lax.all_gather(values, "tensor", axis=axis, tiled=True)
    other = swapped(values, "tensor", 1)
    mine_first = lax.axis_index("tensor") == 0
    low = jnp.where(mine_first, values, other)
    high = jnp.where(mine_first, other, values)
    return jnp.concatenate([low, high], axis=axis)


def tensor_sum(values, kind=f32):
    if lax.axis_size("tensor") != 2:
        return lax.psum(values, "tensor")
    return values + swapped(values.astype(kind), "tensor", 1).astype(f32)


def moved(values, offset):
    count = lax.axis_size("dp")
    return lax.ppermute(values, "dp", [((i + 4 * offset) % count, i) for i in range(count)])


def reduce_scatter(values):
    count = lax.axis_size("dp")
    outer = count // 4
    kind = values.dtype
    here = lax.axis_index("dp")
    parts = values.reshape((outer, 2, 2, values.shape[0] // count) + values.shape[1:])
    core = here % 2
    cross = (here // 2) % 2
    place = here // 4
    kept = lax.dynamic_index_in_dim(parts, core, 2, False)
    sent = lax.dynamic_index_in_dim(parts, 1 - core, 2, False)
    parts = (kept.astype(f32) + swapped(sent, "dp", 1).astype(f32)).astype(kind)
    kept = lax.dynamic_index_in_dim(parts, cross, 1, False)
    sent = lax.dynamic_index_in_dim(parts, 1 - cross, 1, False)
    parts = (kept.astype(f32) + swapped(sent, "dp", 2).astype(f32)).astype(kind)
    total = lax.dynamic_index_in_dim(parts, place, 0, False).astype(f32)
    for offset in range(1, outer):
        sent = lax.dynamic_index_in_dim(parts, (place + outer - offset) % outer, 0, False)
        total = total + moved(sent, offset).astype(f32)
    return total


def scan_kernel(
    states,
    pre_ref,
    act_ref,
    normed_ref,
    cot_ref,
    gate_weight_ref,
    out_weight_ref,
    rank_ref,
    step_weight_ref,
    mask_ref,
    in_ref,
    out_ref,
    in_block_ref,
    out_block_ref,
    skip_ref,
    decay_ref,
    gated_ref,
    dgate_ref,
    dact_ref,
    step_grad_ref,
    sums_ref,
    rank_grad_ref,
    din_ref,
    dout_ref,
    gate_s,
    dgated_s,
    step_s,
    drive_s,
    dscan_s,
    scanned_s,
    dpre_s,
    state_s,
    power_s,
    odd_s,
    even_s,
    odd_rate_s,
    even_rate_s,
    decay_s,
):
    tok, width = pre_ref.shape
    tiles = width // 128
    rows = chunk * states
    count = tok // chunk
    first = pl.program_id(1) == 0
    decay = -jnp.exp(decay_ref[...])
    decay_two = decay * log2e
    skip = skip_ref[0:1, :]
    row_ids = lax.broadcasted_iota(jnp.int32, (chunk, rows), 0)
    col_ids = lax.broadcasted_iota(jnp.int32, (chunk, rows), 1)
    ones_block = (lax.div(col_ids, states) == row_ids).astype(bf16)
    gate_s[...] = jnp.dot(normed_ref[...], gate_weight_ref[...], preferred_element_type=f32)
    dgated_s[...] = jnp.dot(cot_ref[...], out_weight_ref[...], preferred_element_type=f32)

    def spread(ref, at):
        one = ref[pl.ds(at, states), :]
        return jnp.concatenate([one] * tiles, axis=1) if tiles > 1 else one

    def softplus(v):
        return jnp.maximum(v, 0.0) + jnp.log1p(jnp.exp(-jnp.abs(v)))

    def run_forward(step, state, low_s):
        base = pl.multiple_of(step * chunk, chunk)
        cut = pl.ds(base, chunk)
        step_size = softplus(pre_ref[cut, :])
        keep = mask_ref[cut, 1:2]
        live = mask_ref[cut, 0:1]
        gate = gate_s[cut, :]
        step_s[cut, :] = step_size + far * (1.0 - keep)
        drive_s[cut, :] = step_size * act_ref[cut, :].astype(f32)
        dscan_s[cut, :] = dgated_s[cut, :] * live * gate * jax.nn.sigmoid(gate)
        for i in range(chunk):
            row = pl.ds(base + i, 1)
            at = pl.multiple_of((base + i) * states, states)
            power = step_s[row, :] * decay_two
            power_s[pl.ds(at, states), :] = power
            state = jnp.exp2(power) * state + drive_s[row, :] * spread(in_ref, at)
            state_s[pl.ds(at, states), :] = state
            low_s[pl.ds(i * states, states), :] = state.astype(bf16)
        return state

    def sum_forward(step, low_s):
        cut = pl.ds(pl.multiple_of(step * chunk, chunk), chunk)
        low = low_s[...]
        scanned_s[cut, :] = jnp.dot(out_block_ref[cut, :], low, preferred_element_type=f32)
        dout_ref[cut, :] = lax.dot_general(dscan_s[cut, :].astype(bf16), low, last_dims, preferred_element_type=f32)

    def forward(pair, state):
        sum_forward(jnp.maximum(2 * pair - 1, 0), odd_s)
        state = run_forward(2 * pair, state, even_s)
        sum_forward(2 * pair, even_s)
        return run_forward(2 * pair + 1, state, odd_s)

    zero = jnp.zeros((states, width), f32)
    odd_s[...] = jnp.zeros_like(odd_s)
    lax.fori_loop(0, count // 2, forward, zero)
    sum_forward(count - 1, odd_s)
    decay_s[...] = zero

    def run_backward(step, handed, low_s, rate_s):
        base = pl.multiple_of(step * chunk, chunk)
        acc = decay_s[...]
        for i in reversed(range(chunk)):
            row = pl.ds(base + i, 1)
            at = pl.multiple_of((base + i) * states, states)
            power = power_s[pl.ds(at, states), :]
            adjoint = dscan_s[row, :] * spread(out_ref, at) + handed
            low_s[pl.ds(i * states, states), :] = adjoint.astype(bf16)
            handed = jnp.exp2(power) * adjoint
            if i == 0:
                before = pl.multiple_of(jnp.maximum(at - states, 0), states)
            else:
                before = pl.multiple_of((base + (i - 1)) * states, states)
            rate = handed * state_s[pl.ds(before, states), :]
            rate_s[pl.ds(i * states, states), :] = (rate * decay).astype(bf16)
            acc = acc + rate * power
        decay_s[...] = acc
        return handed

    def sum_backward(step, low_s, rate_s, accs):
        skip_acc, bias_acc = accs
        cut = pl.ds(pl.multiple_of(step * chunk, chunk), chunk)
        low = low_s[...]
        in_sum = jnp.dot(in_block_ref[cut, :], low, preferred_element_type=f32)
        rate_sum = jnp.dot(ones_block, rate_s[...], preferred_element_type=f32)
        din_ref[cut, :] = lax.dot_general(drive_s[cut, :].astype(bf16), low, last_dims, preferred_element_type=f32)
        pre = pre_ref[cut, :]
        live = mask_ref[cut, 0:1]
        gate = gate_s[cut, :]
        sig = jax.nn.sigmoid(gate)
        act = act_ref[cut, :].astype(f32)
        dscan = dscan_s[cut, :]
        dpre = ((rate_sum + in_sum * act) * jax.nn.sigmoid(pre)).astype(bf16)
        dpre_s[cut, :] = dpre
        dact_ref[cut, :] = dscan * skip + in_sum * softplus(pre)
        branch = (scanned_s[cut, :] + skip * act) * live
        gated_ref[cut, :] = (branch * gate * sig).astype(bf16)
        dgate_ref[cut, :] = (dgated_s[cut, :] * branch * sig * (1.0 + gate * (1.0 - sig))).astype(bf16)
        skip_acc = skip_acc + jnp.sum((dscan * act).reshape(chunk // 8, 8, width), axis=0)
        bias_acc = bias_acc + jnp.sum(dpre.astype(f32).reshape(chunk // 8, 8, width), axis=0)
        return skip_acc, bias_acc

    eight = jnp.zeros((8, width), f32)
    last = count - 1
    handed = run_backward(last, zero, odd_s, odd_rate_s)

    def backward(pair, carry):
        handed, accs = carry
        step = last - 2 * pair
        accs = sum_backward(step, odd_s, odd_rate_s, accs)
        handed = run_backward(step - 1, handed, even_s, even_rate_s)
        accs = sum_backward(step - 1, even_s, even_rate_s, accs)
        handed = run_backward(step - 2, handed, odd_s, odd_rate_s)
        return handed, accs

    handed, accs = lax.fori_loop(0, count // 2 - 1, backward, (handed, (eight, eight)))
    accs = sum_backward(1, odd_s, odd_rate_s, accs)
    run_backward(0, handed, even_s, even_rate_s)
    skip_acc, bias_acc = sum_backward(0, even_s, even_rate_s, accs)
    rank_grad_ref[...] = lax.dot_general(dpre_s[...], step_weight_ref[...], last_dims, preferred_element_type=f32)
    step_part = lax.dot_general(rank_ref[...], dpre_s[...], first_dims, preferred_element_type=f32)
    small = jnp.concatenate(
        [jnp.sum(skip_acc, axis=0, keepdims=True), jnp.sum(bias_acc, axis=0, keepdims=True), jnp.zeros((6, width), f32)],
        axis=0,
    )

    @pl.when(first)
    def _():
        step_grad_ref[...] = step_part
        sums_ref[0:8, :] = small
        sums_ref[8:, :] = decay_s[...] * (1.0 / log2e)

    @pl.when(jnp.logical_not(first))
    def _():
        step_grad_ref[...] += step_part
        sums_ref[0:8, :] += small
        sums_ref[8:, :] += decay_s[...] * (1.0 / log2e)


def scan_both_ways(start, blocks, width, pre, act, normed, cot, weights, rank_low, step_weight, mask, tables, skip, decay_log):
    micro, tok, chans = pre.shape
    dim = normed.shape[2]
    states = decay_log.shape[0]
    rows = chunk * states
    rank = rank_low.shape[2]

    def whole(r, c):
        return pl.BlockSpec((None, r, c), lambda j, m: (m, 0, 0))

    def each(r, c):
        return pl.BlockSpec((None, None, r, c), lambda j, m: (j, m, 0, 0))

    def part(r):
        return pl.BlockSpec((None, r, width), lambda j, m: (m, 0, j))

    def later(r):
        return pl.BlockSpec((None, r, width), lambda j, m: (m, 0, j + start))

    def param(r, at):
        return pl.BlockSpec((r, width), lambda j, m: (0, j + at))

    def shaped(*dims, kind=f32):
        return jax.ShapeDtypeStruct(dims, kind)

    total = blocks * width
    return pl.pallas_call(
        functools.partial(scan_kernel, states),
        grid=(blocks, micro),
        in_specs=[later(tok)] * 2
        + [whole(tok, dim)] * 2
        + [pl.BlockSpec((None, dim, width), lambda j, m, k=k, at=at: (k, 0, j + at)) for _, k, at in weights]
        + [whole(tok, rank), param(rank, start), whole(tok, mask.shape[2])]
        + [whole(tok * states, 128)] * 2
        + [whole(tok, rows)] * 2
        + [param(1, start), param(states, start)],
        out_specs=[part(tok)] * 3
        + [param(rank, 0), param(8 + states, 0), each(tok, rank), each(tok, rows), each(tok, rows)],
        out_shape=[shaped(micro, tok, total, kind=bf16)] * 2
        + [shaped(micro, tok, total), shaped(rank, total), shaped(8 + states, total)]
        + [shaped(blocks, micro, tok, rank), shaped(blocks, micro, tok, rows), shaped(blocks, micro, tok, rows)],
        scratch_shapes=[pltpu.VMEM((tok, width), f32)] * 6
        + [pltpu.VMEM((tok, width), bf16)]
        + [pltpu.VMEM((tok * states, width), f32)] * 2
        + [pltpu.VMEM((rows, width), bf16)] * 4
        + [pltpu.VMEM((states, width), f32)],
        compiler_params=pltpu.CompilerParams(
            dimension_semantics=("arbitrary", "arbitrary"), vmem_limit_bytes=58 * 2**20
        ),
        cost_estimate=small_cost,
    )(pre, act, normed, cot, *[v for v, _, _ in weights], rank_low, step_weight, mask, *tables, skip[None], decay_log)


def halves(values):
    high = values.astype(bf16)
    return high, (values - high.astype(f32)).astype(bf16)


def middle_kernel(states, selected_ref, weight_ref, bias_ref, pre_ref, rank_ref, in_ref, out_ref, in_block_ref, out_block_ref):
    tokens = selected_ref.shape[0]
    rank = weight_ref.shape[0]
    rows = chunk * states
    selected = selected_ref[...]
    low = selected[:, :rank].astype(bf16)
    rank_ref[...] = low
    pre_ref[...] = jnp.dot(low, weight_ref[...], preferred_element_type=f32) + bias_ref[...]
    state_ids = lax.broadcasted_iota(jnp.int32, (states, rows), 0)
    col_ids = lax.broadcasted_iota(jnp.int32, (states, rows), 1)
    spreading = (lax.rem(col_ids, states) == state_ids).astype(bf16)
    row_ids = lax.broadcasted_iota(jnp.int32, (chunk, rows), 0)
    chunk_cols = lax.broadcasted_iota(jnp.int32, (chunk, rows), 1)
    same = lax.div(chunk_cols, states) == row_ids
    ones = jnp.ones((2 * chunk, 128), bf16)
    for at, lanes_ref, block_ref in ((rank, in_ref, in_block_ref), (rank + states, out_ref, out_block_ref)):
        tiled = [
            jnp.dot(v, spreading, preferred_element_type=f32) for v in halves(selected[:, at : at + states])
        ]
        for i in range(tokens // chunk):
            cut = slice(i * chunk, (i + 1) * chunk)
            high, rest = [jnp.where(same, v[cut], 0.0).astype(bf16) for v in tiled]
            block_ref[cut, :] = high
            lanes_ref[i * rows : (i + 1) * rows, :] = lax.dot_general(
                jnp.concatenate([high, rest], axis=0), ones, first_dims, preferred_element_type=f32
            )


def middle(selected, weight, bias, states):
    tokens, picked = selected.shape
    rank, channels = weight.shape
    rows = chunk * states
    cut = min(128, tokens)

    def fixed(r, c):
        return pl.BlockSpec((r, c), lambda i: (0, 0))

    def part(r, c):
        return pl.BlockSpec((r, c), lambda i: (i, 0))

    def shaped(r, c, kind):
        return jax.ShapeDtypeStruct((r, c), kind)

    return pl.pallas_call(
        functools.partial(middle_kernel, states),
        grid=(tokens // cut,),
        in_specs=[part(cut, picked), fixed(rank, channels), fixed(1, channels)],
        out_specs=[part(cut, channels), part(cut, rank)]
        + [part(cut * states, 128)] * 2
        + [part(cut, rows)] * 2,
        out_shape=[shaped(tokens, channels, f32), shaped(tokens, rank, bf16)]
        + [shaped(tokens * states, 128, f32)] * 2
        + [shaped(tokens, rows, bf16)] * 2,
        compiler_params=pltpu.CompilerParams(dimension_semantics=("arbitrary",), vmem_limit_bytes=48 * 2**20),
    )(selected, weight, bias[None])


def unblocked(fulls, states):
    tok, rows = fulls[0].shape[2:]
    same = jnp.arange(tok)[:, None] % chunk == jnp.arange(rows)[None, :] // states
    picks = (jnp.arange(rows)[:, None] % states == jnp.arange(states)[None, :]).astype(f32)
    full = sum(v[j] for v in fulls for j in range(v.shape[0]))
    return jnp.dot(jnp.where(same[None], full, 0.0), picks, precision=highest)


def behind(values, steps):
    return values if steps == 0 else pltpu.roll(values, steps, 0)


def ahead(values, steps):
    return values if steps == 0 else pltpu.roll(values, values.shape[0] - steps, 0)


def convolve(inner, mask_ref, weight_ref, bias_ref):
    taps = weight_ref.shape[0]
    total = bias_ref[...] + weight_ref[taps - 1 : taps, :] * inner
    for back in range(1, taps):
        tap = taps - 1 - back
        total = total + weight_ref[tap : tap + 1, :] * behind(inner, back) * mask_ref[:, back : back + 1]
    return total


def inner_kernel(bounds, normed_ref, *refs):
    *weight_refs, mask_ref, conv_ref, bias_ref, select_ref, inner_ref, act_ref, selected_ref = refs
    tile = pl.program_id(0)
    for ref, low, high in zip(weight_refs, bounds[:-1], bounds[1:]):

        @pl.when(jnp.logical_and(tile >= low, tile < high))
        def _(ref=ref):
            inner_ref[...] = jnp.dot(normed_ref[...], ref[...], preferred_element_type=f32)

    convolved = convolve(inner_ref[...], mask_ref, conv_ref, bias_ref)
    act = (convolved * jax.nn.sigmoid(convolved)).astype(bf16)
    act_ref[...] = act
    part = jnp.dot(act, select_ref[...], preferred_element_type=f32)
    selected_ref[...] = jnp.where(tile == 0, part, selected_ref[...] + part)


def inner_forward(normed, weights, mask, conv_w, conv_b, select):
    tokens, dim = normed.shape
    channels = sum(v.shape[1] for v in weights)
    width = min([256] + [v.shape[1] for v in weights])
    taps = conv_w.shape[0]
    picked = select.shape[1]
    bounds = [0]
    for v in weights:
        bounds.append(bounds[-1] + v.shape[1] // width)

    def fixed(r, c):
        return pl.BlockSpec((r, c), lambda j: (0, 0))

    def part(r):
        return pl.BlockSpec((r, width), lambda j: (0, j))

    def held(low, high):
        return pl.BlockSpec((dim, width), lambda j: (0, jnp.clip(j - low, 0, high - low - 1)))

    return pl.pallas_call(
        functools.partial(inner_kernel, tuple(bounds)),
        grid=(channels // width,),
        in_specs=[fixed(tokens, dim)]
        + [held(low, high) for low, high in zip(bounds[:-1], bounds[1:])]
        + [
            fixed(tokens, mask.shape[1]),
            part(taps),
            part(1),
            pl.BlockSpec((width, picked), lambda j: (j, 0)),
        ],
        out_specs=[part(tokens), part(tokens), fixed(tokens, picked)],
        out_shape=[
            jax.ShapeDtypeStruct((tokens, channels), f32),
            jax.ShapeDtypeStruct((tokens, channels), bf16),
            jax.ShapeDtypeStruct((tokens, picked), f32),
        ],
        compiler_params=pltpu.CompilerParams(dimension_semantics=("arbitrary",), vmem_limit_bytes=48 * 2**20),
        cost_estimate=small_cost,
    )(normed, *weights, mask, conv_w, conv_b[None], select)


def assemble_kernel(outer, places_ref, *refs):
    *groups, out_ref = refs
    for i, ref in enumerate(groups):

        @pl.when(lax.div(pl.program_id(0), outer) == i)
        def _(ref=ref):
            out_ref[...] = ref[...]


def assemble(groups, places):
    count = places.shape[0]
    outer = count // len(groups)
    rows, width = groups[0].shape
    own = rows // outer

    def held(i):
        return pl.BlockSpec((own, width), lambda r, _: (jnp.clip(r - i * outer, 0, outer - 1), 0))

    return pl.pallas_call(
        functools.partial(assemble_kernel, outer),
        grid_spec=pltpu.PrefetchScalarGridSpec(
            num_scalar_prefetch=1,
            grid=(count,),
            in_specs=[held(i) for i in range(len(groups))],
            out_specs=pl.BlockSpec((own, width), lambda r, where: (where[r], 0)),
        ),
        out_shape=jax.ShapeDtypeStruct((rows * len(groups), width), groups[0].dtype),
        compiler_params=pltpu.CompilerParams(dimension_semantics=("arbitrary",), vmem_limit_bytes=48 * 2**20),
        cost_estimate=small_cost,
    )(places, *groups)


def inner_back_kernel(bounds, places_ref, *refs):
    *dact_refs, dsel_ref, select_ref, inner_ref, act_ref, mask_ref, conv_ref, bias_ref, left_ref = refs[:-6]
    dinner_ref, sums_ref, select_grad_ref, sent_ref, kept_ref, dact_s = refs[-6:]
    taps = conv_ref.shape[0]
    tile = pl.program_id(0)
    for ref, low, high in zip(dact_refs, bounds[:-1], bounds[1:]):

        @pl.when(jnp.logical_and(tile >= low, tile < high))
        def _(ref=ref):
            dact_s[...] = ref[...]

    inner = inner_ref[...]
    dsel = dsel_ref[...]
    convolved = convolve(inner, mask_ref, conv_ref, bias_ref)
    sig = jax.nn.sigmoid(convolved)
    dact = dact_s[...] + lax.dot_general(dsel, select_ref[...], last_dims, preferred_element_type=f32)
    dconv = dact * sig * (1.0 + convolved * (1.0 - sig))
    dinner = conv_ref[taps - 1 : taps, :] * dconv
    sums_ref[taps : taps + 1, :] = jnp.sum(dconv, axis=0, keepdims=True)
    sums_ref[taps - 1 : taps, :] = jnp.sum(dconv * inner, axis=0, keepdims=True)
    for back in range(1, taps):
        tap = taps - 1 - back
        masked = dconv * mask_ref[:, back : back + 1]
        sums_ref[tap : tap + 1, :] = jnp.sum(masked * behind(inner, back), axis=0, keepdims=True)
        dinner = dinner + conv_ref[tap : tap + 1, :] * ahead(masked, back)
    low = dinner.astype(bf16)
    dinner_ref[...] = low
    select_grad_ref[...] = lax.dot_general(dsel, act_ref[...], first_dims, preferred_element_type=f32)
    outer, own = kept_ref.shape[1], kept_ref.shape[3]
    for core, out_ref in ((1, sent_ref), (0, kept_ref)):
        for cross in range(2):
            at = (2 * core + cross) * outer
            rows = [
                left_ref[pl.ds(pl.multiple_of(places_ref[at + j] * own, own), own), :] for j in range(outer)
            ]
            full = jnp.dot(jnp.concatenate(rows, axis=0), low, preferred_element_type=f32).astype(bf16)
            for j in range(outer):
                out_ref[cross, j, 0] = full[j * own : (j + 1) * own]


def inner_backward(places, dacts, dsel, select, inner, act, mask, conv_w, conv_b, left):
    tokens, channels = inner.shape
    count = places.shape[0]
    outer, own = count // 4, left.shape[0] // count
    width = min([256] + [v.shape[1] for v in dacts])
    taps = conv_w.shape[0]
    picked = select.shape[1]
    bounds = [0]
    for v in dacts:
        bounds.append(bounds[-1] + v.shape[1] // width)

    def fixed(r, c):
        return pl.BlockSpec((r, c), lambda j, _: (0, 0))

    def part(r):
        return pl.BlockSpec((r, width), lambda j, _: (0, j))

    def held(low, high):
        return pl.BlockSpec((tokens, width), lambda j, _: (0, jnp.clip(j - low, 0, high - low - 1)))

    parts = pl.BlockSpec((2, outer, 1, own, width), lambda j, _: (0, 0, 0, 0, j))
    return pl.pallas_call(
        functools.partial(inner_back_kernel, tuple(bounds)),
        grid_spec=pltpu.PrefetchScalarGridSpec(
            num_scalar_prefetch=1,
            grid=(channels // width,),
            in_specs=[held(low, high) for low, high in zip(bounds[:-1], bounds[1:])]
            + [
                fixed(tokens, picked),
                pl.BlockSpec((width, picked), lambda j, _: (j, 0)),
                part(tokens),
                part(tokens),
                fixed(tokens, mask.shape[1]),
                part(taps),
                part(1),
                fixed(*left.shape),
            ],
            out_specs=[part(tokens), part(8), part(picked), parts, parts],
            scratch_shapes=[pltpu.VMEM((tokens, width), f32)],
        ),
        out_shape=[
            jax.ShapeDtypeStruct((tokens, channels), bf16),
            jax.ShapeDtypeStruct((8, channels), f32),
            jax.ShapeDtypeStruct((picked, channels), f32),
        ]
        + [jax.ShapeDtypeStruct((2, outer, 1, own, channels), bf16)] * 2,
        compiler_params=pltpu.CompilerParams(dimension_semantics=("arbitrary",), vmem_limit_bytes=52 * 2**20),
        cost_estimate=small_cost,
    )(places, *dacts, dsel, select, inner, act, mask, conv_w, conv_b[None], left)


def project_kernel(count, where_ref, *refs):
    lefts, rights, out_ref = refs[:count], refs[count:-1], refs[-1]
    total = None
    for left, right in zip(lefts, rights):
        rows = jnp.concatenate([left[m] for m in range(left.shape[0])], axis=0)
        part = lax.dot_general(rows, right[...], last_dims, preferred_element_type=f32)
        total = part if total is None else total + part
    rows = out_ref.shape[1]
    for m in range(out_ref.shape[0]):
        out_ref[m] = total[m * rows : (m + 1) * rows].astype(out_ref.dtype)


def project(terms, where, shard_rows, kind):
    micro = terms[0][0].shape[0]
    dim = terms[0][3].shape[1]
    width = min(256, dim)

    def column(plane, at, wide):
        return pl.BlockSpec((None, width, wide), lambda i, _: (plane, i, at))

    def left_rows(at, wide):
        return pl.BlockSpec((micro, shard_rows, wide), lambda i, who: (0, who[0], at))

    return pl.pallas_call(
        functools.partial(project_kernel, len(terms)),
        grid_spec=pltpu.PrefetchScalarGridSpec(
            num_scalar_prefetch=1,
            grid=(dim // width,),
            in_specs=[left_rows(at, wide) for _, at, wide, _, _, _ in terms]
            + [column(plane, at, wide) for _, _, wide, _, plane, at in terms],
            out_specs=pl.BlockSpec((micro, shard_rows, width), lambda i, _: (0, 0, i)),
        ),
        out_shape=jax.ShapeDtypeStruct((micro, shard_rows, dim), kind),
        compiler_params=pltpu.CompilerParams(dimension_semantics=("arbitrary",), vmem_limit_bytes=48 * 2**20),
        cost_estimate=small_cost,
    )(where, *[t[0] for t in terms], *[t[3] for t in terms])


def project_all(terms):
    total = 0.0
    for left, left_at, wide, right, plane, at in terms:
        total = total + jnp.einsum(
            "mgc,dc->mgd",
            left[..., left_at * wide : (left_at + 1) * wide],
            right[plane, :, at * wide : (at + 1) * wide],
            preferred_element_type=f32,
        )
    return lax.psum_scatter(total.astype(bf16), "tensor", scatter_dimension=1, tiled=True)


def parts_kernel(kinds, outer, places_ref, *refs):
    out_ref = refs[-1]
    own = refs[0].shape[0]
    for kind in range(kinds):
        left = jnp.concatenate([r[...] for r in refs[kind * outer : (kind + 1) * outer]], axis=0)
        full = jnp.dot(left, refs[kinds * outer + kind][...], preferred_element_type=f32).astype(bf16)
        for j in range(outer):
            out_ref[j, kind] = full[j * own : (j + 1) * own]


def grad_parts(places, near, lefts, rights):
    kinds = len(lefts)
    count = places.shape[0]
    outer = count // 4
    own = lefts[0].shape[0] // count
    tokens = lefts[0].shape[1]
    width = rights[0].shape[1]
    offset = 0 if near else 2 * outer

    def left_spec(j):
        return pl.BlockSpec((own, tokens), lambda q, where: (where[offset + q * outer + j], 0))

    return pl.pallas_call(
        functools.partial(parts_kernel, kinds, outer),
        grid_spec=pltpu.PrefetchScalarGridSpec(
            num_scalar_prefetch=1,
            grid=(2,),
            in_specs=[left_spec(j) for _ in range(kinds) for j in range(outer)]
            + [pl.BlockSpec(v.shape, lambda q, where: (0, 0)) for v in rights],
            out_specs=pl.BlockSpec((None, outer, kinds, own, width), lambda q, where: (q, 0, 0, 0, 0)),
        ),
        out_shape=jax.ShapeDtypeStruct((2, outer, kinds, own, width), bf16),
        compiler_params=pltpu.CompilerParams(dimension_semantics=("arbitrary",), vmem_limit_bytes=48 * 2**20),
        cost_estimate=small_cost,
    )(places, *[v for v in lefts for _ in range(outer)], *rights)


def join(*trees):
    return lax.optimization_barrier(trees)


def summed(first, second, *more):
    total = first.astype(f32) + second.astype(f32)
    for v in more:
        total = total + v.astype(f32)
    return total


def sums_kernel(crosses, alongs, outer, *refs):
    ins = 2 * sum(crosses) + 3 * sum(alongs)
    given, outs = iter(refs[:ins]), iter(refs[ins:])
    for sources in crosses:
        out, at = next(outs), 0
        for _ in range(sources):
            kept, got = next(given), next(given)
            total = (kept[...].astype(f32) + got[...].astype(f32)).astype(bf16)
            out[..., at : at + total.shape[-1]] = total
            at += total.shape[-1]
    for sources in alongs:
        out, at = [next(outs) for _ in range(outer)], 0
        for _ in range(sources):
            kept, got, across = next(given), next(given), next(given)
            wide = kept.shape[-1]
            for j in range(outer):
                total = kept[j].astype(f32) + got[j].astype(f32) + across[j].astype(f32)
                out[j][..., at : at + wide] = total.astype(out[j].dtype)
            at += wide


def step_sums(crosses, alongs):
    cuts = 4
    in_specs, out_specs, out_shape, given = [], [], [], []
    outer = (crosses + alongs)[0][0][0].shape[1]

    def taken(shape, first, at, wide):
        block = (None,) + shape[1:-2] + (shape[-2] // cuts, wide)
        return pl.BlockSpec(block, lambda i: (first,) + (0,) * (len(shape) - 3) + (i, at))

    def plain(shape, at=0):
        return pl.BlockSpec(
            shape[:-2] + (shape[-2] // cuts, shape[-1]), lambda i: (0,) * (len(shape) - 2) + (i, at)
        )

    for sources in crosses:
        for kept, got, at, wide in sources:
            in_specs += [taken(kept.shape, 1, at, wide)] * 2
            given += [kept, got]
        out = sources[0][0].shape[1:-1] + (sum(v[3] for v in sources),)
        out_specs.append(plain(out))
        out_shape.append(jax.ShapeDtypeStruct(out, bf16))
    for sources in alongs:
        for kept, got, at, wide, across, across_at in sources:
            in_specs += [taken(kept.shape, 0, at, wide)] * 2 + [plain(across.shape[:-1] + (wide,), across_at)]
            given += [kept, got, across]
        out = sources[0][0].shape[2:-1] + (sum(v[3] for v in sources),)
        out_specs += [plain(out)] * outer
        out_shape += [jax.ShapeDtypeStruct(out, f32 if j == 0 else bf16) for j in range(outer)]
    outs = pl.pallas_call(
        functools.partial(
            sums_kernel, tuple(len(v) for v in crosses), tuple(len(v) for v in alongs), outer
        ),
        grid=(cuts,),
        in_specs=in_specs,
        out_specs=out_specs,
        out_shape=out_shape,
        compiler_params=pltpu.CompilerParams(dimension_semantics=("arbitrary",), vmem_limit_bytes=48 * 2**20),
        cost_estimate=small_cost,
    )(*given)
    outs = list(outs)
    first, rest = outs[: len(crosses)], outs[len(crosses) :]
    return first, [rest[i * outer : (i + 1) * outer] for i in range(len(alongs))]


def along_moves(rows):
    count = lax.axis_size("dp")
    return rows[:1] + [
        lax.ppermute(v, "dp", [(i, (i + 4 * (j + 1)) % count) for i in range(count)])
        for j, v in enumerate(rows[1:])
    ]


def final_kernel(turned, *refs):
    terms, outs = refs[: len(refs) - len(turned)], refs[len(refs) - len(turned) :]
    total = terms[0][...]
    for ref in terms[1:]:
        total = total + ref[...].astype(f32)
    for i, turn in enumerate(turned):
        outs[i][...] = total[i].T if turn else total[i]


def final_sum(terms, turned):
    kinds, own, width = terms[0].shape
    return pl.pallas_call(
        functools.partial(final_kernel, turned),
        out_shape=[jax.ShapeDtypeStruct((width, own) if turn else (own, width), f32) for turn in turned],
        compiler_params=pltpu.CompilerParams(vmem_limit_bytes=48 * 2**20),
        cost_estimate=small_cost,
    )(*terms)


def doubled(values):
    count = lax.axis_size("dp")
    here = lax.axis_index("dp")
    values = values[None]
    bit = 1
    while bit < count:
        other = swapped(values, "dp", bit)
        low = (here & bit) == 0
        values = jnp.concatenate([jnp.where(low, values, other), jnp.where(low, other, values)], axis=0)
        bit *= 2
    return values


def finish_kernel(hidden_ref, cot_ref, gain_ref, layer_ref, layer_away_ref, here_ref, away_ref, layer_out, grad_out):
    hidden = hidden_ref[...]
    scale = lax.rsqrt(jnp.mean(hidden * hidden, axis=-1, keepdims=True) + epsilon)
    normal = hidden * scale
    layer_out[...] = hidden + (layer_ref[...] + layer_away_ref[...].astype(f32))
    dnormed = here_ref[...] + away_ref[...].astype(f32)
    dnormal = dnormed * gain_ref[...]
    middle = jnp.mean(dnormal * normal, axis=-1, keepdims=True)
    grad_out[...] = cot_ref[...].astype(f32) + scale * (dnormal - normal * middle)


def finish(hidden, cotangent, gain, layer_here, layer_away, here, away):
    micro, rows, dim = hidden.shape
    total = micro * rows
    cut = min(64, total)

    def part():
        return pl.BlockSpec((cut, dim), lambda i: (i, 0))

    layer, grad = pl.pallas_call(
        finish_kernel,
        grid=(total // cut,),
        in_specs=[part(), part(), pl.BlockSpec((1, dim), lambda i: (0, 0))] + [part()] * 4,
        out_specs=[part(), part()],
        out_shape=[jax.ShapeDtypeStruct((total, dim), f32)] * 2,
        compiler_params=pltpu.CompilerParams(dimension_semantics=("arbitrary",), vmem_limit_bytes=48 * 2**20),
        cost_estimate=small_cost,
    )(*[v.reshape(-1, dim) for v in (hidden, cotangent, gain, layer_here, layer_away, here, away)])
    return layer.reshape(hidden.shape), grad.reshape(hidden.shape)


def on_device(
    hidden,
    cotangent,
    lengths,
    order,
    norm_gain,
    input_weight,
    conv_weight,
    conv_bias,
    select_weight,
    step_weight,
    step_bias,
    decay_log,
    skip_gain,
    output_weight,
):
    micro, shard_rows, model_dim = hidden.shape
    count = lax.axis_size("dp")
    outer = count // 4
    group_tok = shard_rows * lax.axis_size("tensor")
    tokens = micro * group_tok
    channels = input_weight.shape[2]
    taps = conv_weight.shape[0]
    states = decay_log.shape[0]
    own = conv_bias.shape[0]
    own_dim = norm_gain.shape[0]
    half = channels // 2
    quarter = channels // 4
    here = lax.axis_index("dp")
    ids = jnp.arange(count, dtype=jnp.int32)
    place, cross, core = here // 4, (here // 2) % 2, here % 2
    places = ((place + ids % outer) % outer) * 4 + (cross ^ (ids // outer) % 2) * 2 + (core ^ ids // (2 * outer))
    ranks = ((core ^ ids % 2) * 2 + (cross ^ (ids // 2) % 2)) * outer + (ids // 4 - place) % outer
    places, ranks = places.astype(jnp.int32), ranks.astype(jnp.int32)

    w_inner = lax.all_gather(input_weight[:, 0], "dp", axis=0, tiled=True)
    out_shard = output_weight.T
    weights = []
    for low, high in ((0, half), (half, channels)):
        both = jnp.stack([input_weight[:, 1, low:high], out_shard[:, low:high]])
        both = lax.all_gather(both, "dp", axis=1, tiled=True)
        weights += [((both, 0, at), (both, 1, at)) for at in range(1 if low == 0 else 2)]

    pieces = [norm_gain, conv_weight, conv_bias, step_bias, decay_log, skip_gain]
    packed = doubled(jnp.concatenate([v.reshape(-1) for v in pieces]))
    narrow, packed = join(jnp.concatenate([select_weight.T, step_weight.reshape(-1, own)], axis=0), packed)
    full = []
    at = 0
    for v in pieces:
        part = packed[:, at : at + v.size]
        at += v.size
        if v.ndim == 2:
            part = part.reshape(count, v.shape[0], v.shape[1]).transpose(1, 0, 2).reshape(v.shape[0], -1)
        else:
            part = part.reshape(-1)
        full.append(part)
    gain_full, conv_w, conv_b, step_b, decay_lg, skip_g = full
    picked = select_weight.shape[1]
    narrow = jnp.stack([narrow] + [moved(narrow, j) for j in range(1, outer)])
    narrow = jnp.stack([narrow, swapped(narrow, "dp", 2)])
    narrow = jnp.stack([narrow, swapped(narrow, "dp", 1)]).reshape((count,) + narrow.shape[2:])
    narrow = jnp.take(narrow, ranks, axis=0)
    w_sel = narrow[:, :picked].transpose(0, 2, 1).reshape(channels, picked)
    w_step = narrow[:, picked:].reshape(-1, channels)
    rank_dim = w_step.shape[0]

    inverse_rms = lax.rsqrt(jnp.mean(hidden * hidden, axis=-1, keepdims=True) + epsilon)
    normal_rows = hidden * inverse_rms
    normed = tensor_gather((normal_rows * gain_full).astype(bf16), 1).reshape(tokens, model_dim)
    normed, cot_rows = join(normed, cotangent)
    cot_full = tensor_gather(cot_rows, 1).reshape(tokens, model_dim)

    position, live_mask = jax.vmap(lambda a, b: positions(a, b, group_tok))(lengths[:, 0], order[:, 0])
    mask = jnp.stack([live_mask] + [(position >= back).astype(f32) for back in range(1, taps)], axis=2)
    flat_mask = mask.reshape(tokens, taps)

    def grouped(v):
        return v.reshape(micro, group_tok, v.shape[-1])

    inner, act, selected = inner_forward(normed, [w_inner], flat_mask, conv_w, conv_b, w_sel)
    selected = tensor_sum(selected)
    lefts = (normed.T, cot_full.T)
    pre_step, rank_low, *tables = middle(selected, w_step, step_b, states)
    tables = tuple(grouped(v) if v.shape[0] == tokens else v.reshape(micro, -1, v.shape[-1]) for v in tables)
    rank_rows = grouped(rank_low)

    gated, dgate, dact, step_grads, sums, rank_grads, dins, douts = [[] for _ in range(8)]
    kept, got, across, total = {}, {}, {}, {}
    rows = (grouped(normed), grouped(cot_full))

    def scanned(number, skip_now):
        return scan_both_ways(
            (0, 2, 3)[number],
            (2, 1, 1)[number],
            quarter,
            grouped(pre_step),
            grouped(act),
            *rows,
            weights[number],
            rank_rows,
            w_step,
            mask,
            tables,
            skip_now,
            decay_lg,
        )

    def hold(results):
        for held, v in zip((gated, dgate, dact), results[:3]):
            held.append(v.reshape(tokens, -1))
        for held, v in zip((step_grads, sums, rank_grads, dins, douts), results[3:]):
            held.append(v)

    def source(piece, at=0, wide=None):
        return kept[piece], got[piece], at, wide or kept[piece].shape[-1]

    hold(scanned(0, skip_g))
    places_now = places
    for piece, left, right in (("gate", lefts[0], dgate[0]), ("out", lefts[1], gated[0])):
        sent = grad_parts(places_now, False, (left,), (right,))
        sent, places_now = join(sent, places_now)
        got[piece] = swapped(sent, "dp", 1)
        kept[piece] = grad_parts(places_now, True, (left,), (right,))
    cross, _ = step_sums(
        [[source("gate"), source("out", 0, quarter)], [source("out", 1, quarter)]], []
    )
    skip_now, cross = join(skip_g, cross)
    across["zero"], across["rest"] = [swapped(v, "dp", 2) for v in cross]

    results = scanned(1, skip_now)
    results, across["zero"] = join(results, across["zero"])
    hold(results)
    sent = grad_parts(places_now, False, lefts, (dgate[1], gated[1]))
    sent, places_now = join(sent, places_now)
    got["second"] = swapped(sent, "dp", 1)
    kept["second"] = grad_parts(places_now, True, lefts, (dgate[1], gated[1]))
    kept["second"], across["rest"], got["second"] = join(kept["second"], across["rest"], got["second"])
    cross, along = step_sums([[source("second")]], [[source("gate") + (across["zero"], 0)]])
    skip_now, cross, along = join(skip_now, cross, along)
    total["gate"] = along_moves(along[0])
    across["second"] = swapped(cross[0], "dp", 2)

    results = scanned(2, skip_now)
    results, total["gate"], across["second"] = join(results, total["gate"], across["second"])
    hold(results)
    rank_grad = sum(v[j] for v in rank_grads for j in range(v.shape[0]))
    select_terms = jnp.concatenate([rank_grad, unblocked(dins, states), unblocked(douts, states)], axis=2)
    _, along = step_sums(
        [], [[source("out", 0, quarter) + (across["zero"], 2), source("out", 1, quarter) + (across["rest"], 0)]]
    )
    two = lax.axis_size("tensor") == 2
    where = lax.axis_index("tensor").astype(jnp.int32)[None]
    select_terms, places_now, along = join(select_terms.reshape(tokens, -1), places_now, along)
    select_terms = tensor_sum(select_terms, bf16)
    total["out"] = along_moves(along[0])
    sent = grad_parts(places_now, False, lefts, (dgate[2], gated[2]))
    sent, places_now = join(sent, places_now)
    got["third"] = swapped(sent, "dp", 1)
    kept["third"] = grad_parts(places_now, True, lefts, (dgate[2], gated[2]))
    kept["third"], where = join(kept["third"], where)
    out_terms = [(grouped(v), 0, v.shape[1]) + w[1] for v, w in zip(gated, weights)]
    layer_away = project(out_terms, 1 - where, shard_rows, bf16) if two else project_all(out_terms)
    select_terms, kept["third"], got["third"], total["out"], layer_away = join(
        select_terms, kept["third"], got["third"], total["out"], layer_away
    )
    select_low = select_terms.astype(bf16)
    cross, along = step_sums([[source("third")]], [[source("second") + (across["second"], 0)]])
    cross, along, select_low, layer_away = join(cross, along, select_low, layer_away)
    across["third"] = swapped(cross[0], "dp", 2)
    total["second"] = along_moves(along[0])
    if two:
        layer_away = swapped(layer_away, "tensor", 1)
    dinner, conv_sums, select_grad, sent, kept["inner"] = inner_backward(
        places_now, dact, select_low, w_sel, inner, act, flat_mask, conv_w, conv_b, lefts[0]
    )
    across["third"], total["second"], dinner, conv_sums, select_grad, sent, kept["inner"], where, layer_away = join(
        across["third"], total["second"], dinner, conv_sums, select_grad, sent, kept["inner"], where, layer_away
    )
    norm_terms = [(grouped(v), 0, v.shape[1]) + w[0] for v, w in zip(dgate, weights)]
    norm_terms.append((grouped(dinner), 0, channels, w_inner[None], 0, 0))
    got["inner"] = swapped(sent, "dp", 1)
    if two:
        norm_away = project(norm_terms, 1 - where, shard_rows, bf16)
    else:
        norm_away = project_all(norm_terms)
    got["inner"], norm_away, where = join(got["inner"], norm_away, where)
    cross, along = step_sums(
        [[source("inner", 0, half)], [source("inner", 1, half)]], [[source("third") + (across["third"], 0)]]
    )
    cross, along, where, norm_away, select_grad = join(cross, along, where, norm_away, select_grad)
    across["first"] = swapped(cross[0], "dp", 2)
    total["third"] = along_moves(along[0])
    if two:
        norm_away = swapped(norm_away, "tensor", 1)
        norm_here = project(norm_terms, where, shard_rows, f32)
        layer_here = project(out_terms, where, shard_rows, f32)
    else:
        norm_here, layer_here = [jnp.zeros(v.shape, f32) for v in (norm_away, layer_away)]
    across["first"], total["third"], cross[1], norm_here, layer_here, norm_away = join(
        across["first"], total["third"], cross[1], norm_here, layer_here, norm_away
    )
    step_grad = jnp.concatenate(step_grads, axis=1)
    step_grad = step_grad.reshape(count, rank_dim // count, count, own).transpose(1, 2, 0, 3)
    small = jnp.concatenate(
        [select_grad, step_grad.reshape(rank_dim, channels), conv_sums, jnp.concatenate(sums, axis=1)], axis=0
    )
    small = lax.psum_scatter(small, "dp", scatter_dimension=1, tiled=True)
    _, along = step_sums([], [[source("inner", 0, half) + (across["first"], 0)]])
    cross[1], along, norm_here = join(cross[1], along, norm_here)
    across["last"] = swapped(cross[1], "dp", 2)
    total["first"] = along_moves(along[0])
    norm_here, total["first"][1] = join(norm_here, total["first"][1])
    layer_rows, grad_rows = finish(hidden, cotangent, gain_full, layer_here, layer_away, norm_here, norm_away)
    gates, outs = [], []
    total["gate"], layer_rows = join(total["gate"], layer_rows)
    gates += final_sum(total["gate"], (False,))
    outs += final_sum(total["out"], (True,))
    for name in ("second", "third"):
        one, other = final_sum(total[name], (False, True))
        gates.append(one)
        outs.append(other)
    across["last"], total["first"], gates, outs, layer_rows, grad_rows = join(
        across["last"], total["first"], gates, outs, layer_rows, grad_rows
    )
    _, along = step_sums([], [[source("inner", 1, half) + (across["last"], 0)]])
    total["last"] = along_moves(along[0])
    gate_grad = jnp.concatenate(gates, axis=1)
    (first,) = final_sum(total["first"], (False,))
    own_input = input_weight.astype(f32)
    most = jnp.sum(own_input[:, 0, :half] * first, axis=1) + jnp.sum(own_input[:, 1] * gate_grad, axis=1)
    (last,) = final_sum(total["last"], (False,))
    gain_total = tensor_sum(most + jnp.sum(own_input[:, 0, half:] * last, axis=1)) / norm_gain
    at = picked + rank_dim
    return (
        layer_rows,
        grad_rows,
        gain_total,
        jnp.stack([jnp.concatenate([first, last], axis=1), gate_grad], axis=1),
        small[at : at + taps],
        small[at + taps],
        small[:picked].T,
        small[picked:at].reshape(-1, channels),
        small[at + 9],
        small[at + 16 :],
        small[at + 8],
        jnp.concatenate(outs, axis=0),
    )


def solution(mesh):
    in_specs = (
        P(None, ("dp", "tensor"), None),
        P(None, ("dp", "tensor"), None),
        P(None, "dp", None),
        P(None, "dp", None),
        P("dp"),
        P("dp", None, "tensor"),
        P(None, ("tensor", "dp")),
        P(("tensor", "dp")),
        P(("tensor", "dp"), None),
        P("dp", "tensor"),
        P(("tensor", "dp")),
        P(None, ("tensor", "dp")),
        P(("tensor", "dp")),
        P("tensor", "dp"),
    )
    out_specs = (
        P(None, ("dp", "tensor"), None),
        P(None, ("dp", "tensor"), None),
        P("dp"),
        P("dp", None, "tensor"),
        P(None, ("tensor", "dp")),
        P(("tensor", "dp")),
        P(("tensor", "dp"), None),
        P("dp", "tensor"),
        P(("tensor", "dp")),
        P(None, ("tensor", "dp")),
        P(("tensor", "dp")),
        P("tensor", "dp"),
    )
    return jax.shard_map(
        on_device, mesh=mesh, in_specs=in_specs, out_specs=out_specs, check_vma=False
    )
```

```python
import functools

import jax
import jax.numpy as jnp
from jax import lax
from jax.experimental import pallas as pl
from jax.experimental.pallas import tpu as pltpu
from jax.sharding import PartitionSpec as P

epsilon = 1e-05
log2e = 1.4426950408889634
far = 1e6
chunk = 16
f32 = jnp.float32
bf16 = jnp.bfloat16
highest = lax.Precision.HIGHEST
small_cost = pl.CostEstimate(flops=1, bytes_accessed=1, transcendentals=0)
last_dims = (((1,), (1,)), ((), ()))
first_dims = (((0,), (0,)), ((), ()))


def positions(length_row, order_row, slot_count):
    number = order_row.shape[0]
    picked = (order_row[:, None] == jnp.arange(number, dtype=jnp.int32)[None, :]).astype(jnp.int32)
    ordered = jnp.sum(picked * length_row[None, :], axis=1)
    seq_ends = jnp.cumsum(ordered)
    starts = jnp.concatenate([jnp.zeros((1,), jnp.int32), seq_ends])
    slot_ids = jnp.arange(slot_count, dtype=jnp.int32)
    seq_begin = jnp.max(jnp.where(starts[None, :] <= slot_ids[:, None], starts[None, :], 0), axis=1)
    return (slot_ids - seq_begin, (slot_ids < seq_ends[-1]).astype(jnp.float32))


def swapped(values, axis, bit):
    count = lax.axis_size(axis)
    return lax.ppermute(values, axis, [(i, i ^ bit) for i in range(count)])


def tensor_gather(values, axis):
    if lax.axis_size("tensor") != 2:
        return lax.all_gather(values, "tensor", axis=axis, tiled=True)
    other = swapped(values, "tensor", 1)
    mine_first = lax.axis_index("tensor") == 0
    low = jnp.where(mine_first, values, other)
    high = jnp.where(mine_first, other, values)
    return jnp.concatenate([low, high], axis=axis)


def tensor_sum(values, kind=f32):
    if lax.axis_size("tensor") != 2:
        return lax.psum(values, "tensor")
    return values + swapped(values.astype(kind), "tensor", 1).astype(f32)


def moved(values, offset):
    count = lax.axis_size("dp")
    return lax.ppermute(values, "dp", [((i + 4 * offset) % count, i) for i in range(count)])


def reduce_scatter(values):
    count = lax.axis_size("dp")
    outer = count // 4
    kind = values.dtype
    here = lax.axis_index("dp")
    parts = values.reshape((outer, 2, 2, values.shape[0] // count) + values.shape[1:])
    core = here % 2
    cross = (here // 2) % 2
    place = here // 4
    kept = lax.dynamic_index_in_dim(parts, core, 2, False)
    sent = lax.dynamic_index_in_dim(parts, 1 - core, 2, False)
    parts = (kept.astype(f32) + swapped(sent, "dp", 1).astype(f32)).astype(kind)
    kept = lax.dynamic_index_in_dim(parts, cross, 1, False)
    sent = lax.dynamic_index_in_dim(parts, 1 - cross, 1, False)
    parts = (kept.astype(f32) + swapped(sent, "dp", 2).astype(f32)).astype(kind)
    total = lax.dynamic_index_in_dim(parts, place, 0, False).astype(f32)
    for offset in range(1, outer):
        sent = lax.dynamic_index_in_dim(parts, (place + outer - offset) % outer, 0, False)
        total = total + moved(sent, offset).astype(f32)
    return total


def scan_kernel(
    states,
    pre_ref,
    act_ref,
    normed_ref,
    cot_ref,
    gate_weight_ref,
    out_weight_ref,
    rank_ref,
    step_weight_ref,
    mask_ref,
    in_ref,
    out_ref,
    in_block_ref,
    out_block_ref,
    skip_ref,
    decay_ref,
    gated_ref,
    dgate_ref,
    dact_ref,
    step_grad_ref,
    sums_ref,
    rank_grad_ref,
    din_ref,
    dout_ref,
    gate_s,
    dgated_s,
    step_s,
    drive_s,
    dscan_s,
    scanned_s,
    dpre_s,
    state_s,
    power_s,
    odd_s,
    even_s,
    odd_rate_s,
    even_rate_s,
    decay_s,
):
    tok, width = pre_ref.shape
    tiles = width // 128
    rows = chunk * states
    count = tok // chunk
    first = pl.program_id(1) == 0
    decay = -jnp.exp(decay_ref[...])
    decay_two = decay * log2e
    skip = skip_ref[0:1, :]
    row_ids = lax.broadcasted_iota(jnp.int32, (chunk, rows), 0)
    col_ids = lax.broadcasted_iota(jnp.int32, (chunk, rows), 1)
    ones_block = (lax.div(col_ids, states) == row_ids).astype(bf16)
    gate_s[...] = jnp.dot(normed_ref[...], gate_weight_ref[...], preferred_element_type=f32)
    dgated_s[...] = jnp.dot(cot_ref[...], out_weight_ref[...], preferred_element_type=f32)

    def spread(ref, at):
        one = ref[pl.ds(at, states), :]
        return jnp.concatenate([one] * tiles, axis=1) if tiles > 1 else one

    def softplus(v):
        return jnp.maximum(v, 0.0) + jnp.log1p(jnp.exp(-jnp.abs(v)))

    def run_forward(step, state, low_s):
        base = pl.multiple_of(step * chunk, chunk)
        cut = pl.ds(base, chunk)
        step_size = softplus(pre_ref[cut, :])
        keep = mask_ref[cut, 1:2]
        live = mask_ref[cut, 0:1]
        gate = gate_s[cut, :]
        step_s[cut, :] = step_size + far * (1.0 - keep)
        drive_s[cut, :] = step_size * act_ref[cut, :].astype(f32)
        dscan_s[cut, :] = dgated_s[cut, :] * live * gate * jax.nn.sigmoid(gate)
        for i in range(chunk):
            row = pl.ds(base + i, 1)
            at = pl.multiple_of((base + i) * states, states)
            power = step_s[row, :] * decay_two
            power_s[pl.ds(at, states), :] = power
            state = jnp.exp2(power) * state + drive_s[row, :] * spread(in_ref, at)
            state_s[pl.ds(at, states), :] = state
            low_s[pl.ds(i * states, states), :] = state.astype(bf16)
        return state

    def sum_forward(step, low_s):
        cut = pl.ds(pl.multiple_of(step * chunk, chunk), chunk)
        low = low_s[...]
        scanned_s[cut, :] = jnp.dot(out_block_ref[cut, :], low, preferred_element_type=f32)
        dout_ref[cut, :] = lax.dot_general(dscan_s[cut, :].astype(bf16), low, last_dims, preferred_element_type=f32)

    def forward(pair, state):
        sum_forward(jnp.maximum(2 * pair - 1, 0), odd_s)
        state = run_forward(2 * pair, state, even_s)
        sum_forward(2 * pair, even_s)
        return run_forward(2 * pair + 1, state, odd_s)

    zero = jnp.zeros((states, width), f32)
    odd_s[...] = jnp.zeros_like(odd_s)
    lax.fori_loop(0, count // 2, forward, zero)
    sum_forward(count - 1, odd_s)
    decay_s[...] = zero

    def run_backward(step, handed, low_s, rate_s):
        base = pl.multiple_of(step * chunk, chunk)
        acc = decay_s[...]
        for i in reversed(range(chunk)):
            row = pl.ds(base + i, 1)
            at = pl.multiple_of((base + i) * states, states)
            power = power_s[pl.ds(at, states), :]
            adjoint = dscan_s[row, :] * spread(out_ref, at) + handed
            low_s[pl.ds(i * states, states), :] = adjoint.astype(bf16)
            handed = jnp.exp2(power) * adjoint
            if i == 0:
                before = pl.multiple_of(jnp.maximum(at - states, 0), states)
            else:
                before = pl.multiple_of((base + (i - 1)) * states, states)
            rate = handed * state_s[pl.ds(before, states), :]
            rate_s[pl.ds(i * states, states), :] = (rate * decay).astype(bf16)
            acc = acc + rate * power
        decay_s[...] = acc
        return handed

    def sum_backward(step, low_s, rate_s, accs):
        skip_acc, bias_acc = accs
        cut = pl.ds(pl.multiple_of(step * chunk, chunk), chunk)
        low = low_s[...]
        in_sum = jnp.dot(in_block_ref[cut, :], low, preferred_element_type=f32)
        rate_sum = jnp.dot(ones_block, rate_s[...], preferred_element_type=f32)
        din_ref[cut, :] = lax.dot_general(drive_s[cut, :].astype(bf16), low, last_dims, preferred_element_type=f32)
        pre = pre_ref[cut, :]
        live = mask_ref[cut, 0:1]
        gate = gate_s[cut, :]
        sig = jax.nn.sigmoid(gate)
        act = act_ref[cut, :].astype(f32)
        dscan = dscan_s[cut, :]
        dpre = ((rate_sum + in_sum * act) * jax.nn.sigmoid(pre)).astype(bf16)
        dpre_s[cut, :] = dpre
        dact_ref[cut, :] = dscan * skip + in_sum * softplus(pre)
        branch = (scanned_s[cut, :] + skip * act) * live
        gated_ref[cut, :] = (branch * gate * sig).astype(bf16)
        dgate_ref[cut, :] = (dgated_s[cut, :] * branch * sig * (1.0 + gate * (1.0 - sig))).astype(bf16)
        skip_acc = skip_acc + jnp.sum((dscan * act).reshape(chunk // 8, 8, width), axis=0)
        bias_acc = bias_acc + jnp.sum(dpre.astype(f32).reshape(chunk // 8, 8, width), axis=0)
        return skip_acc, bias_acc

    eight = jnp.zeros((8, width), f32)
    last = count - 1
    handed = run_backward(last, zero, odd_s, odd_rate_s)

    def backward(pair, carry):
        handed, accs = carry
        step = last - 2 * pair
        accs = sum_backward(step, odd_s, odd_rate_s, accs)
        handed = run_backward(step - 1, handed, even_s, even_rate_s)
        accs = sum_backward(step - 1, even_s, even_rate_s, accs)
        handed = run_backward(step - 2, handed, odd_s, odd_rate_s)
        return handed, accs

    handed, accs = lax.fori_loop(0, count // 2 - 1, backward, (handed, (eight, eight)))
    accs = sum_backward(1, odd_s, odd_rate_s, accs)
    run_backward(0, handed, even_s, even_rate_s)
    skip_acc, bias_acc = sum_backward(0, even_s, even_rate_s, accs)
    rank_grad_ref[...] = lax.dot_general(dpre_s[...], step_weight_ref[...], last_dims, preferred_element_type=f32)
    step_part = lax.dot_general(rank_ref[...], dpre_s[...], first_dims, preferred_element_type=f32)
    small = jnp.concatenate(
        [jnp.sum(skip_acc, axis=0, keepdims=True), jnp.sum(bias_acc, axis=0, keepdims=True), jnp.zeros((6, width), f32)],
        axis=0,
    )

    @pl.when(first)
    def _():
        step_grad_ref[...] = step_part
        sums_ref[0:8, :] = small
        sums_ref[8:, :] = decay_s[...] * (1.0 / log2e)

    @pl.when(jnp.logical_not(first))
    def _():
        step_grad_ref[...] += step_part
        sums_ref[0:8, :] += small
        sums_ref[8:, :] += decay_s[...] * (1.0 / log2e)


def scan_both_ways(start, blocks, width, pre, act, normed, cot, weights, rank_low, step_weight, mask, tables, skip, decay_log):
    micro, tok, chans = pre.shape
    dim = normed.shape[2]
    states = decay_log.shape[0]
    rows = chunk * states
    rank = rank_low.shape[2]

    def whole(r, c):
        return pl.BlockSpec((None, r, c), lambda j, m: (m, 0, 0))

    def each(r, c):
        return pl.BlockSpec((None, None, r, c), lambda j, m: (j, m, 0, 0))

    def part(r):
        return pl.BlockSpec((None, r, width), lambda j, m: (m, 0, j))

    def later(r):
        return pl.BlockSpec((None, r, width), lambda j, m: (m, 0, j + start))

    def param(r, at):
        return pl.BlockSpec((r, width), lambda j, m: (0, j + at))

    def shaped(*dims, kind=f32):
        return jax.ShapeDtypeStruct(dims, kind)

    total = blocks * width
    return pl.pallas_call(
        functools.partial(scan_kernel, states),
        grid=(blocks, micro),
        in_specs=[later(tok)] * 2
        + [whole(tok, dim)] * 2
        + [pl.BlockSpec((None, dim, width), lambda j, m, k=k, at=at: (k, 0, j + at)) for _, k, at in weights]
        + [whole(tok, rank), param(rank, start), whole(tok, mask.shape[2])]
        + [whole(tok * states, 128)] * 2
        + [whole(tok, rows)] * 2
        + [param(1, start), param(states, start)],
        out_specs=[part(tok)] * 3
        + [param(rank, 0), param(8 + states, 0), each(tok, rank), each(tok, rows), each(tok, rows)],
        out_shape=[shaped(micro, tok, total, kind=bf16)] * 2
        + [shaped(micro, tok, total), shaped(rank, total), shaped(8 + states, total)]
        + [shaped(blocks, micro, tok, rank), shaped(blocks, micro, tok, rows), shaped(blocks, micro, tok, rows)],
        scratch_shapes=[pltpu.VMEM((tok, width), f32)] * 6
        + [pltpu.VMEM((tok, width), bf16)]
        + [pltpu.VMEM((tok * states, width), f32)] * 2
        + [pltpu.VMEM((rows, width), bf16)] * 4
        + [pltpu.VMEM((states, width), f32)],
        compiler_params=pltpu.CompilerParams(
            dimension_semantics=("arbitrary", "arbitrary"), vmem_limit_bytes=58 * 2**20
        ),
        cost_estimate=small_cost,
    )(pre, act, normed, cot, *[v for v, _, _ in weights], rank_low, step_weight, mask, *tables, skip[None], decay_log)


def halves(values):
    high = values.astype(bf16)
    return high, (values - high.astype(f32)).astype(bf16)


def middle_kernel(states, selected_ref, weight_ref, bias_ref, pre_ref, rank_ref, in_ref, out_ref, in_block_ref, out_block_ref):
    tokens = selected_ref.shape[0]
    rank = weight_ref.shape[0]
    rows = chunk * states
    selected = selected_ref[...]
    low = selected[:, :rank].astype(bf16)
    rank_ref[...] = low
    pre_ref[...] = jnp.dot(low, weight_ref[...], preferred_element_type=f32) + bias_ref[...]
    state_ids = lax.broadcasted_iota(jnp.int32, (states, rows), 0)
    col_ids = lax.broadcasted_iota(jnp.int32, (states, rows), 1)
    spreading = (lax.rem(col_ids, states) == state_ids).astype(bf16)
    row_ids = lax.broadcasted_iota(jnp.int32, (chunk, rows), 0)
    chunk_cols = lax.broadcasted_iota(jnp.int32, (chunk, rows), 1)
    same = lax.div(chunk_cols, states) == row_ids
    ones = jnp.ones((2 * chunk, 128), bf16)
    for at, lanes_ref, block_ref in ((rank, in_ref, in_block_ref), (rank + states, out_ref, out_block_ref)):
        tiled = [
            jnp.dot(v, spreading, preferred_element_type=f32) for v in halves(selected[:, at : at + states])
        ]
        for i in range(tokens // chunk):
            cut = slice(i * chunk, (i + 1) * chunk)
            high, rest = [jnp.where(same, v[cut], 0.0).astype(bf16) for v in tiled]
            block_ref[cut, :] = high
            lanes_ref[i * rows : (i + 1) * rows, :] = lax.dot_general(
                jnp.concatenate([high, rest], axis=0), ones, first_dims, preferred_element_type=f32
            )


def middle(selected, weight, bias, states):
    tokens, picked = selected.shape
    rank, channels = weight.shape
    rows = chunk * states
    cut = min(128, tokens)

    def fixed(r, c):
        return pl.BlockSpec((r, c), lambda i: (0, 0))

    def part(r, c):
        return pl.BlockSpec((r, c), lambda i: (i, 0))

    def shaped(r, c, kind):
        return jax.ShapeDtypeStruct((r, c), kind)

    return pl.pallas_call(
        functools.partial(middle_kernel, states),
        grid=(tokens // cut,),
        in_specs=[part(cut, picked), fixed(rank, channels), fixed(1, channels)],
        out_specs=[part(cut, channels), part(cut, rank)]
        + [part(cut * states, 128)] * 2
        + [part(cut, rows)] * 2,
        out_shape=[shaped(tokens, channels, f32), shaped(tokens, rank, bf16)]
        + [shaped(tokens * states, 128, f32)] * 2
        + [shaped(tokens, rows, bf16)] * 2,
        compiler_params=pltpu.CompilerParams(dimension_semantics=("arbitrary",), vmem_limit_bytes=48 * 2**20),
    )(selected, weight, bias[None])


def unblocked(fulls, states):
    tok, rows = fulls[0].shape[2:]
    same = jnp.arange(tok)[:, None] % chunk == jnp.arange(rows)[None, :] // states
    picks = (jnp.arange(rows)[:, None] % states == jnp.arange(states)[None, :]).astype(f32)
    full = sum(v[j] for v in fulls for j in range(v.shape[0]))
    return jnp.dot(jnp.where(same[None], full, 0.0), picks, precision=highest)


def behind(values, steps):
    return values if steps == 0 else pltpu.roll(values, steps, 0)


def ahead(values, steps):
    return values if steps == 0 else pltpu.roll(values, values.shape[0] - steps, 0)


def convolve(inner, mask_ref, weight_ref, bias_ref):
    taps = weight_ref.shape[0]
    total = bias_ref[...] + weight_ref[taps - 1 : taps, :] * inner
    for back in range(1, taps):
        tap = taps - 1 - back
        total = total + weight_ref[tap : tap + 1, :] * behind(inner, back) * mask_ref[:, back : back + 1]
    return total


def inner_kernel(bounds, normed_ref, *refs):
    *weight_refs, mask_ref, conv_ref, bias_ref, select_ref, inner_ref, act_ref, selected_ref = refs
    tile = pl.program_id(0)
    for ref, low, high in zip(weight_refs, bounds[:-1], bounds[1:]):

        @pl.when(jnp.logical_and(tile >= low, tile < high))
        def _(ref=ref):
            inner_ref[...] = jnp.dot(normed_ref[...], ref[...], preferred_element_type=f32)

    convolved = convolve(inner_ref[...], mask_ref, conv_ref, bias_ref)
    act = (convolved * jax.nn.sigmoid(convolved)).astype(bf16)
    act_ref[...] = act
    part = jnp.dot(act, select_ref[...], preferred_element_type=f32)
    selected_ref[...] = jnp.where(tile == 0, part, selected_ref[...] + part)


def inner_forward(normed, weights, mask, conv_w, conv_b, select):
    tokens, dim = normed.shape
    channels = sum(v.shape[1] for v in weights)
    width = min([256] + [v.shape[1] for v in weights])
    taps = conv_w.shape[0]
    picked = select.shape[1]
    bounds = [0]
    for v in weights:
        bounds.append(bounds[-1] + v.shape[1] // width)

    def fixed(r, c):
        return pl.BlockSpec((r, c), lambda j: (0, 0))

    def part(r):
        return pl.BlockSpec((r, width), lambda j: (0, j))

    def held(low, high):
        return pl.BlockSpec((dim, width), lambda j: (0, jnp.clip(j - low, 0, high - low - 1)))

    return pl.pallas_call(
        functools.partial(inner_kernel, tuple(bounds)),
        grid=(channels // width,),
        in_specs=[fixed(tokens, dim)]
        + [held(low, high) for low, high in zip(bounds[:-1], bounds[1:])]
        + [
            fixed(tokens, mask.shape[1]),
            part(taps),
            part(1),
            pl.BlockSpec((width, picked), lambda j: (j, 0)),
        ],
        out_specs=[part(tokens), part(tokens), fixed(tokens, picked)],
        out_shape=[
            jax.ShapeDtypeStruct((tokens, channels), f32),
            jax.ShapeDtypeStruct((tokens, channels), bf16),
            jax.ShapeDtypeStruct((tokens, picked), f32),
        ],
        compiler_params=pltpu.CompilerParams(dimension_semantics=("arbitrary",), vmem_limit_bytes=48 * 2**20),
        cost_estimate=small_cost,
    )(normed, *weights, mask, conv_w, conv_b[None], select)


def assemble_kernel(outer, places_ref, *refs):
    *groups, out_ref = refs
    for i, ref in enumerate(groups):

        @pl.when(lax.div(pl.program_id(0), outer) == i)
        def _(ref=ref):
            out_ref[...] = ref[...]


def assemble(groups, places):
    count = places.shape[0]
    outer = count // len(groups)
    rows, width = groups[0].shape
    own = rows // outer

    def held(i):
        return pl.BlockSpec((own, width), lambda r, _: (jnp.clip(r - i * outer, 0, outer - 1), 0))

    return pl.pallas_call(
        functools.partial(assemble_kernel, outer),
        grid_spec=pltpu.PrefetchScalarGridSpec(
            num_scalar_prefetch=1,
            grid=(count,),
            in_specs=[held(i) for i in range(len(groups))],
            out_specs=pl.BlockSpec((own, width), lambda r, where: (where[r], 0)),
        ),
        out_shape=jax.ShapeDtypeStruct((rows * len(groups), width), groups[0].dtype),
        compiler_params=pltpu.CompilerParams(dimension_semantics=("arbitrary",), vmem_limit_bytes=48 * 2**20),
        cost_estimate=small_cost,
    )(places, *groups)


def inner_back_kernel(bounds, places_ref, *refs):
    *dact_refs, dsel_ref, select_ref, inner_ref, act_ref, mask_ref, conv_ref, bias_ref, left_ref = refs[:-6]
    dinner_ref, sums_ref, select_grad_ref, sent_ref, kept_ref, dact_s = refs[-6:]
    taps = conv_ref.shape[0]
    tile = pl.program_id(0)
    for ref, low, high in zip(dact_refs, bounds[:-1], bounds[1:]):

        @pl.when(jnp.logical_and(tile >= low, tile < high))
        def _(ref=ref):
            dact_s[...] = ref[...]

    inner = inner_ref[...]
    dsel = dsel_ref[...]
    convolved = convolve(inner, mask_ref, conv_ref, bias_ref)
    sig = jax.nn.sigmoid(convolved)
    dact = dact_s[...] + lax.dot_general(dsel, select_ref[...], last_dims, preferred_element_type=f32)
    dconv = dact * sig * (1.0 + convolved * (1.0 - sig))
    dinner = conv_ref[taps - 1 : taps, :] * dconv
    sums_ref[taps : taps + 1, :] = jnp.sum(dconv, axis=0, keepdims=True)
    sums_ref[taps - 1 : taps, :] = jnp.sum(dconv * inner, axis=0, keepdims=True)
    for back in range(1, taps):
        tap = taps - 1 - back
        masked = dconv * mask_ref[:, back : back + 1]
        sums_ref[tap : tap + 1, :] = jnp.sum(masked * behind(inner, back), axis=0, keepdims=True)
        dinner = dinner + conv_ref[tap : tap + 1, :] * ahead(masked, back)
    low = dinner.astype(bf16)
    dinner_ref[...] = low
    select_grad_ref[...] = lax.dot_general(dsel, act_ref[...], first_dims, preferred_element_type=f32)
    outer, own = kept_ref.shape[1], kept_ref.shape[3]
    for core, out_ref in ((1, sent_ref), (0, kept_ref)):
        for cross in range(2):
            at = (2 * core + cross) * outer
            rows = [
                left_ref[pl.ds(pl.multiple_of(places_ref[at + j] * own, own), own), :] for j in range(outer)
            ]
            full = jnp.dot(jnp.concatenate(rows, axis=0), low, preferred_element_type=f32).astype(bf16)
            for j in range(outer):
                out_ref[cross, j, 0] = full[j * own : (j + 1) * own]


def inner_backward(places, dacts, dsel, select, inner, act, mask, conv_w, conv_b, left):
    tokens, channels = inner.shape
    count = places.shape[0]
    outer, own = count // 4, left.shape[0] // count
    width = min([256] + [v.shape[1] for v in dacts])
    taps = conv_w.shape[0]
    picked = select.shape[1]
    bounds = [0]
    for v in dacts:
        bounds.append(bounds[-1] + v.shape[1] // width)

    def fixed(r, c):
        return pl.BlockSpec((r, c), lambda j, _: (0, 0))

    def part(r):
        return pl.BlockSpec((r, width), lambda j, _: (0, j))

    def held(low, high):
        return pl.BlockSpec((tokens, width), lambda j, _: (0, jnp.clip(j - low, 0, high - low - 1)))

    parts = pl.BlockSpec((2, outer, 1, own, width), lambda j, _: (0, 0, 0, 0, j))
    return pl.pallas_call(
        functools.partial(inner_back_kernel, tuple(bounds)),
        grid_spec=pltpu.PrefetchScalarGridSpec(
            num_scalar_prefetch=1,
            grid=(channels // width,),
            in_specs=[held(low, high) for low, high in zip(bounds[:-1], bounds[1:])]
            + [
                fixed(tokens, picked),
                pl.BlockSpec((width, picked), lambda j, _: (j, 0)),
                part(tokens),
                part(tokens),
                fixed(tokens, mask.shape[1]),
                part(taps),
                part(1),
                fixed(*left.shape),
            ],
            out_specs=[part(tokens), part(8), part(picked), parts, parts],
            scratch_shapes=[pltpu.VMEM((tokens, width), f32)],
        ),
        out_shape=[
            jax.ShapeDtypeStruct((tokens, channels), bf16),
            jax.ShapeDtypeStruct((8, channels), f32),
            jax.ShapeDtypeStruct((picked, channels), f32),
        ]
        + [jax.ShapeDtypeStruct((2, outer, 1, own, channels), bf16)] * 2,
        compiler_params=pltpu.CompilerParams(dimension_semantics=("arbitrary",), vmem_limit_bytes=52 * 2**20),
        cost_estimate=small_cost,
    )(places, *dacts, dsel, select, inner, act, mask, conv_w, conv_b[None], left)


def project_kernel(count, where_ref, *refs):
    lefts, rights, out_ref = refs[:count], refs[count:-1], refs[-1]
    total = None
    for left, right in zip(lefts, rights):
        rows = jnp.concatenate([left[m] for m in range(left.shape[0])], axis=0)
        part = lax.dot_general(rows, right[...], last_dims, preferred_element_type=f32)
        total = part if total is None else total + part
    rows = out_ref.shape[1]
    for m in range(out_ref.shape[0]):
        out_ref[m] = total[m * rows : (m + 1) * rows].astype(out_ref.dtype)


def project(terms, where, shard_rows, kind):
    micro = terms[0][0].shape[0]
    dim = terms[0][3].shape[1]
    width = min(256, dim)

    def column(plane, at, wide):
        return pl.BlockSpec((None, width, wide), lambda i, _: (plane, i, at))

    def left_rows(at, wide):
        return pl.BlockSpec((micro, shard_rows, wide), lambda i, who: (0, who[0], at))

    return pl.pallas_call(
        functools.partial(project_kernel, len(terms)),
        grid_spec=pltpu.PrefetchScalarGridSpec(
            num_scalar_prefetch=1,
            grid=(dim // width,),
            in_specs=[left_rows(at, wide) for _, at, wide, _, _, _ in terms]
            + [column(plane, at, wide) for _, _, wide, _, plane, at in terms],
            out_specs=pl.BlockSpec((micro, shard_rows, width), lambda i, _: (0, 0, i)),
        ),
        out_shape=jax.ShapeDtypeStruct((micro, shard_rows, dim), kind),
        compiler_params=pltpu.CompilerParams(dimension_semantics=("arbitrary",), vmem_limit_bytes=48 * 2**20),
        cost_estimate=small_cost,
    )(where, *[t[0] for t in terms], *[t[3] for t in terms])


def project_all(terms):
    total = 0.0
    for left, left_at, wide, right, plane, at in terms:
        total = total + jnp.einsum(
            "mgc,dc->mgd",
            left[..., left_at * wide : (left_at + 1) * wide],
            right[plane, :, at * wide : (at + 1) * wide],
            preferred_element_type=f32,
        )
    return lax.psum_scatter(total.astype(bf16), "tensor", scatter_dimension=1, tiled=True)


def parts_kernel(kinds, outer, places_ref, *refs):
    out_ref = refs[-1]
    own = refs[0].shape[0]
    for kind in range(kinds):
        left = jnp.concatenate([r[...] for r in refs[kind * outer : (kind + 1) * outer]], axis=0)
        full = jnp.dot(left, refs[kinds * outer + kind][...], preferred_element_type=f32).astype(bf16)
        for j in range(outer):
            out_ref[j, kind] = full[j * own : (j + 1) * own]


def grad_parts(places, near, lefts, rights):
    kinds = len(lefts)
    count = places.shape[0]
    outer = count // 4
    own = lefts[0].shape[0] // count
    tokens = lefts[0].shape[1]
    width = rights[0].shape[1]
    offset = 0 if near else 2 * outer

    def left_spec(j):
        return pl.BlockSpec((own, tokens), lambda q, where: (where[offset + q * outer + j], 0))

    return pl.pallas_call(
        functools.partial(parts_kernel, kinds, outer),
        grid_spec=pltpu.PrefetchScalarGridSpec(
            num_scalar_prefetch=1,
            grid=(2,),
            in_specs=[left_spec(j) for _ in range(kinds) for j in range(outer)]
            + [pl.BlockSpec(v.shape, lambda q, where: (0, 0)) for v in rights],
            out_specs=pl.BlockSpec((None, outer, kinds, own, width), lambda q, where: (q, 0, 0, 0, 0)),
        ),
        out_shape=jax.ShapeDtypeStruct((2, outer, kinds, own, width), bf16),
        compiler_params=pltpu.CompilerParams(dimension_semantics=("arbitrary",), vmem_limit_bytes=48 * 2**20),
        cost_estimate=small_cost,
    )(places, *[v for v in lefts for _ in range(outer)], *rights)


def join(*trees):
    return lax.optimization_barrier(trees)


def summed(first, second, *more):
    total = first.astype(f32) + second.astype(f32)
    for v in more:
        total = total + v.astype(f32)
    return total


def sums_kernel(crosses, alongs, outer, *refs):
    ins = 2 * sum(crosses) + 3 * sum(alongs)
    given, outs = iter(refs[:ins]), iter(refs[ins:])
    for sources in crosses:
        out, at = next(outs), 0
        for _ in range(sources):
            kept, got = next(given), next(given)
            total = (kept[...].astype(f32) + got[...].astype(f32)).astype(bf16)
            out[..., at : at + total.shape[-1]] = total
            at += total.shape[-1]
    for sources in alongs:
        out, at = [next(outs) for _ in range(outer)], 0
        for _ in range(sources):
            kept, got, across = next(given), next(given), next(given)
            wide = kept.shape[-1]
            for j in range(outer):
                total = kept[j].astype(f32) + got[j].astype(f32) + across[j].astype(f32)
                out[j][..., at : at + wide] = total.astype(out[j].dtype)
            at += wide


def step_sums(crosses, alongs):
    cuts = 4
    in_specs, out_specs, out_shape, given = [], [], [], []
    outer = (crosses + alongs)[0][0][0].shape[1]

    def taken(shape, first, at, wide):
        block = (None,) + shape[1:-2] + (shape[-2] // cuts, wide)
        return pl.BlockSpec(block, lambda i: (first,) + (0,) * (len(shape) - 3) + (i, at))

    def plain(shape, at=0):
        return pl.BlockSpec(
            shape[:-2] + (shape[-2] // cuts, shape[-1]), lambda i: (0,) * (len(shape) - 2) + (i, at)
        )

    for sources in crosses:
        for kept, got, at, wide in sources:
            in_specs += [taken(kept.shape, 1, at, wide)] * 2
            given += [kept, got]
        out = sources[0][0].shape[1:-1] + (sum(v[3] for v in sources),)
        out_specs.append(plain(out))
        out_shape.append(jax.ShapeDtypeStruct(out, bf16))
    for sources in alongs:
        for kept, got, at, wide, across, across_at in sources:
            in_specs += [taken(kept.shape, 0, at, wide)] * 2 + [plain(across.shape[:-1] + (wide,), across_at)]
            given += [kept, got, across]
        out = sources[0][0].shape[2:-1] + (sum(v[3] for v in sources),)
        out_specs += [plain(out)] * outer
        out_shape += [jax.ShapeDtypeStruct(out, f32 if j == 0 else bf16) for j in range(outer)]
    outs = pl.pallas_call(
        functools.partial(
            sums_kernel, tuple(len(v) for v in crosses), tuple(len(v) for v in alongs), outer
        ),
        grid=(cuts,),
        in_specs=in_specs,
        out_specs=out_specs,
        out_shape=out_shape,
        compiler_params=pltpu.CompilerParams(dimension_semantics=("arbitrary",), vmem_limit_bytes=48 * 2**20),
        cost_estimate=small_cost,
    )(*given)
    outs = list(outs)
    first, rest = outs[: len(crosses)], outs[len(crosses) :]
    return first, [rest[i * outer : (i + 1) * outer] for i in range(len(alongs))]


def along_moves(rows):
    count = lax.axis_size("dp")
    return rows[:1] + [
        lax.ppermute(v, "dp", [(i, (i + 4 * (j + 1)) % count) for i in range(count)])
        for j, v in enumerate(rows[1:])
    ]


def final_kernel(turned, *refs):
    terms, outs = refs[: len(refs) - len(turned)], refs[len(refs) - len(turned) :]
    total = terms[0][...]
    for ref in terms[1:]:
        total = total + ref[...].astype(f32)
    for i, turn in enumerate(turned):
        outs[i][...] = total[i].T if turn else total[i]


def final_sum(terms, turned):
    kinds, own, width = terms[0].shape
    return pl.pallas_call(
        functools.partial(final_kernel, turned),
        out_shape=[jax.ShapeDtypeStruct((width, own) if turn else (own, width), f32) for turn in turned],
        compiler_params=pltpu.CompilerParams(vmem_limit_bytes=48 * 2**20),
        cost_estimate=small_cost,
    )(*terms)


def doubled(values):
    count = lax.axis_size("dp")
    here = lax.axis_index("dp")
    values = values[None]
    bit = 1
    while bit < count:
        other = swapped(values, "dp", bit)
        low = (here & bit) == 0
        values = jnp.concatenate([jnp.where(low, values, other), jnp.where(low, other, values)], axis=0)
        bit *= 2
    return values


def finish_kernel(hidden_ref, cot_ref, gain_ref, layer_ref, layer_away_ref, here_ref, away_ref, layer_out, grad_out):
    hidden = hidden_ref[...]
    scale = lax.rsqrt(jnp.mean(hidden * hidden, axis=-1, keepdims=True) + epsilon)
    normal = hidden * scale
    layer_out[...] = hidden + (layer_ref[...] + layer_away_ref[...].astype(f32))
    dnormed = here_ref[...] + away_ref[...].astype(f32)
    dnormal = dnormed * gain_ref[...]
    middle = jnp.mean(dnormal * normal, axis=-1, keepdims=True)
    grad_out[...] = cot_ref[...].astype(f32) + scale * (dnormal - normal * middle)


def finish(hidden, cotangent, gain, layer_here, layer_away, here, away):
    micro, rows, dim = hidden.shape
    total = micro * rows
    cut = min(64, total)

    def part():
        return pl.BlockSpec((cut, dim), lambda i: (i, 0))

    layer, grad = pl.pallas_call(
        finish_kernel,
        grid=(total // cut,),
        in_specs=[part(), part(), pl.BlockSpec((1, dim), lambda i: (0, 0))] + [part()] * 4,
        out_specs=[part(), part()],
        out_shape=[jax.ShapeDtypeStruct((total, dim), f32)] * 2,
        compiler_params=pltpu.CompilerParams(dimension_semantics=("arbitrary",), vmem_limit_bytes=48 * 2**20),
        cost_estimate=small_cost,
    )(*[v.reshape(-1, dim) for v in (hidden, cotangent, gain, layer_here, layer_away, here, away)])
    return layer.reshape(hidden.shape), grad.reshape(hidden.shape)


def on_device(
    hidden,
    cotangent,
    lengths,
    order,
    norm_gain,
    input_weight,
    conv_weight,
    conv_bias,
    select_weight,
    step_weight,
    step_bias,
    decay_log,
    skip_gain,
    output_weight,
):
    micro, shard_rows, model_dim = hidden.shape
    count = lax.axis_size("dp")
    outer = count // 4
    group_tok = shard_rows * lax.axis_size("tensor")
    tokens = micro * group_tok
    channels = input_weight.shape[2]
    taps = conv_weight.shape[0]
    states = decay_log.shape[0]
    own = conv_bias.shape[0]
    own_dim = norm_gain.shape[0]
    half = channels // 2
    quarter = channels // 4
    here = lax.axis_index("dp")
    ids = jnp.arange(count, dtype=jnp.int32)
    place, cross, core = here // 4, (here // 2) % 2, here % 2
    places = ((place + ids % outer) % outer) * 4 + (cross ^ (ids // outer) % 2) * 2 + (core ^ ids // (2 * outer))
    ranks = ((core ^ ids % 2) * 2 + (cross ^ (ids // 2) % 2)) * outer + (ids // 4 - place) % outer
    places, ranks = places.astype(jnp.int32), ranks.astype(jnp.int32)

    w_inner = lax.all_gather(input_weight[:, 0], "dp", axis=0, tiled=True)
    out_shard = output_weight.T
    weights = []
    for low, high in ((0, half), (half, channels)):
        both = jnp.stack([input_weight[:, 1, low:high], out_shard[:, low:high]])
        both = lax.all_gather(both, "dp", axis=1, tiled=True)
        weights.append(((both, 0, 0), (both, 1, 0)))

    pieces = [norm_gain, conv_weight, conv_bias, step_bias, decay_log, skip_gain]
    packed = doubled(jnp.concatenate([v.reshape(-1) for v in pieces]))
    narrow, packed = join(jnp.concatenate([select_weight.T, step_weight.reshape(-1, own)], axis=0), packed)
    full = []
    at = 0
    for v in pieces:
        part = packed[:, at : at + v.size]
        at += v.size
        if v.ndim == 2:
            part = part.reshape(count, v.shape[0], v.shape[1]).transpose(1, 0, 2).reshape(v.shape[0], -1)
        else:
            part = part.reshape(-1)
        full.append(part)
    gain_full, conv_w, conv_b, step_b, decay_lg, skip_g = full
    picked = select_weight.shape[1]
    narrow = jnp.stack([narrow] + [moved(narrow, j) for j in range(1, outer)])
    narrow = jnp.stack([narrow, swapped(narrow, "dp", 2)])
    narrow = jnp.stack([narrow, swapped(narrow, "dp", 1)]).reshape((count,) + narrow.shape[2:])
    narrow = jnp.take(narrow, ranks, axis=0)
    w_sel = narrow[:, :picked].transpose(0, 2, 1).reshape(channels, picked)
    w_step = narrow[:, picked:].reshape(-1, channels)
    rank_dim = w_step.shape[0]

    inverse_rms = lax.rsqrt(jnp.mean(hidden * hidden, axis=-1, keepdims=True) + epsilon)
    normal_rows = hidden * inverse_rms
    normed = tensor_gather((normal_rows * gain_full).astype(bf16), 1).reshape(tokens, model_dim)
    normed, cot_rows = join(normed, cotangent)
    cot_full = tensor_gather(cot_rows, 1).reshape(tokens, model_dim)

    position, live_mask = jax.vmap(lambda a, b: positions(a, b, group_tok))(lengths[:, 0], order[:, 0])
    mask = jnp.stack([live_mask] + [(position >= back).astype(f32) for back in range(1, taps)], axis=2)
    flat_mask = mask.reshape(tokens, taps)

    def grouped(v):
        return v.reshape(micro, group_tok, v.shape[-1])

    inner, act, selected = inner_forward(normed, [w_inner], flat_mask, conv_w, conv_b, w_sel)
    selected = tensor_sum(selected)
    lefts = (normed.T, cot_full.T)
    pre_step, rank_low, *tables = middle(selected, w_step, step_b, states)
    tables = tuple(grouped(v) if v.shape[0] == tokens else v.reshape(micro, -1, v.shape[-1]) for v in tables)
    rank_rows = grouped(rank_low)

    gated, dgate, dact, step_grads, sums, rank_grads, dins, douts = [[] for _ in range(8)]
    kept, got, across, total = {}, {}, {}, {}
    rows = (grouped(normed), grouped(cot_full))

    def scanned(number, skip_now):
        return scan_both_ways(
            2 * number,
            2,
            quarter,
            grouped(pre_step),
            grouped(act),
            *rows,
            weights[number],
            rank_rows,
            w_step,
            mask,
            tables,
            skip_now,
            decay_lg,
        )

    def hold(results):
        for held, v in zip((gated, dgate, dact), results[:3]):
            held.append(v.reshape(tokens, -1))
        for held, v in zip((step_grads, sums, rank_grads, dins, douts), results[3:]):
            held.append(v)

    def source(piece, at=0, wide=None):
        return kept[piece], got[piece], at, wide or kept[piece].shape[-1]

    def last_step(piece, name, at=0):
        return [source(piece) + (across[name], at)]

    hold(scanned(0, skip_g))
    places_now = places
    for piece, left, right in (("gate", lefts[0], dgate[0]), ("out", lefts[1], gated[0])):
        sent = grad_parts(places_now, False, (left,), (right,))
        sent, places_now = join(sent, places_now)
        got[piece] = swapped(sent, "dp", 1)
        kept[piece] = grad_parts(places_now, True, (left,), (right,))
    cross, _ = step_sums([[source("gate"), source("out")]], [])
    skip_now, cross = join(skip_g, cross)
    across["early"] = swapped(cross[0], "dp", 2)

    results = scanned(1, skip_now)
    results, across["early"] = join(results, across["early"])
    hold(results)
    _, along = step_sums([], [last_step("gate", "early"), last_step("out", "early", 1)])
    along, places_now, rank_grads = join(along, places_now, rank_grads)
    total["gate"] = along_moves(along[0])
    for piece, left, right in (("gate_late", lefts[0], dgate[1]), ("out_late", lefts[1], gated[1])):
        sent = grad_parts(places_now, False, (left,), (right,))
        sent, places_now = join(sent, places_now)
        got[piece] = swapped(sent, "dp", 1)
    rank_grad = sum(v[j] for v in rank_grads for j in range(v.shape[0]))
    select_terms = jnp.concatenate([rank_grad, unblocked(dins, states), unblocked(douts, states)], axis=2)
    select_terms, places_now = join(select_terms.reshape(tokens, -1), places_now)
    select_terms = tensor_sum(select_terms, bf16)
    places_now, total["gate"][1] = join(places_now, total["gate"][1])
    for piece, left, right in (("gate_late", lefts[0], dgate[1]), ("out_late", lefts[1], gated[1])):
        kept[piece] = grad_parts(places_now, True, (left,), (right,))
    two = lax.axis_size("tensor") == 2
    where = lax.axis_index("tensor").astype(jnp.int32)[None]
    kept["out_late"], where = join(kept["out_late"], where)
    out_terms = [(grouped(v), 0, v.shape[1]) + w[1] for v, w in zip(gated, weights)]
    layer_away = project(out_terms, 1 - where, shard_rows, bf16) if two else project_all(out_terms)
    names = ("gate_late", "out_late")
    select_terms, late_kept, late_got, total["gate"], layer_away = join(
        select_terms, [kept[n] for n in names], [got[n] for n in names], total["gate"], layer_away
    )
    for n, one, other in zip(names, late_kept, late_got):
        kept[n], got[n] = one, other
    select_low = select_terms.astype(bf16)
    cross, _ = step_sums([[source("gate_late")], [source("out_late")]], [])
    cross, select_low, layer_away, along[1] = join(cross, select_low, layer_away, along[1])
    across["gate_late"] = swapped(cross[0], "dp", 2)
    total["out"] = along_moves(along[1])
    if two:
        layer_away = swapped(layer_away, "tensor", 1)
    dinner, conv_sums, select_grad, sent, kept["inner"] = inner_backward(
        places_now, dact, select_low, w_sel, inner, act, flat_mask, conv_w, conv_b, lefts[0]
    )
    across["gate_late"], total["out"], dinner, conv_sums, select_grad, sent, kept["inner"], where, layer_away, cross[1] = join(
        across["gate_late"],
        total["out"],
        dinner,
        conv_sums,
        select_grad,
        sent,
        kept["inner"],
        where,
        layer_away,
        cross[1],
    )
    norm_terms = [(grouped(v), 0, v.shape[1]) + w[0] for v, w in zip(dgate, weights)]
    norm_terms.append((grouped(dinner), 0, channels, w_inner[None], 0, 0))
    got["inner"] = swapped(sent, "dp", 1)
    across["out_late"] = swapped(cross[1], "dp", 2)
    _, along = step_sums([], [last_step("gate_late", "gate_late")])
    along, where = join(along, where)
    total["gate_late"] = along_moves(along[0])
    if two:
        norm_away = project(norm_terms, 1 - where, shard_rows, bf16)
    else:
        norm_away = project_all(norm_terms)
    got["inner"], norm_away, where, total["gate_late"], across["out_late"] = join(
        got["inner"], norm_away, where, total["gate_late"], across["out_late"]
    )
    cross, along = step_sums(
        [[source("inner", 0, half)], [source("inner", 1, half)]], [last_step("out_late", "out_late")]
    )
    cross, along, where, norm_away, select_grad = join(cross, along, where, norm_away, select_grad)
    across["first"] = swapped(cross[0], "dp", 2)
    total["out_late"] = along_moves(along[0])
    if two:
        norm_away = swapped(norm_away, "tensor", 1)
        norm_here = project(norm_terms, where, shard_rows, f32)
        layer_here = project(out_terms, where, shard_rows, f32)
    else:
        norm_here, layer_here = [jnp.zeros(v.shape, f32) for v in (norm_away, layer_away)]
    across["first"], total["out_late"], cross[1], norm_here, layer_here, norm_away = join(
        across["first"], total["out_late"], cross[1], norm_here, layer_here, norm_away
    )
    step_grad = jnp.concatenate(step_grads, axis=1)
    step_grad = step_grad.reshape(count, rank_dim // count, count, own).transpose(1, 2, 0, 3)
    small = jnp.concatenate(
        [select_grad, step_grad.reshape(rank_dim, channels), conv_sums, jnp.concatenate(sums, axis=1)], axis=0
    )
    small = lax.psum_scatter(small, "dp", scatter_dimension=1, tiled=True)
    _, along = step_sums([], [[source("inner", 0, half) + (across["first"], 0)]])
    cross[1], along, norm_here = join(cross[1], along, norm_here)
    across["last"] = swapped(cross[1], "dp", 2)
    total["first"] = along_moves(along[0])
    norm_here, total["first"][1] = join(norm_here, total["first"][1])
    layer_rows, grad_rows = finish(hidden, cotangent, gain_full, layer_here, layer_away, norm_here, norm_away)
    total["gate"], layer_rows = join(total["gate"], layer_rows)
    gates = [final_sum(total[n], (False,))[0] for n in ("gate", "gate_late")]
    outs = [final_sum(total[n], (True,))[0] for n in ("out", "out_late")]
    across["last"], total["first"], gates, outs, layer_rows, grad_rows = join(
        across["last"], total["first"], gates, outs, layer_rows, grad_rows
    )
    _, along = step_sums([], [[source("inner", 1, half) + (across["last"], 0)]])
    total["last"] = along_moves(along[0])
    gate_grad = jnp.concatenate(gates, axis=1)
    (first,) = final_sum(total["first"], (False,))
    own_input = input_weight.astype(f32)
    most = jnp.sum(own_input[:, 0, :half] * first, axis=1) + jnp.sum(own_input[:, 1] * gate_grad, axis=1)
    (last,) = final_sum(total["last"], (False,))
    gain_total = tensor_sum(most + jnp.sum(own_input[:, 0, half:] * last, axis=1)) / norm_gain
    at = picked + rank_dim
    return (
        layer_rows,
        grad_rows,
        gain_total,
        jnp.stack([jnp.concatenate([first, last], axis=1), gate_grad], axis=1),
        small[at : at + taps],
        small[at + taps],
        small[:picked].T,
        small[picked:at].reshape(-1, channels),
        small[at + 9],
        small[at + 16 :],
        small[at + 8],
        jnp.concatenate(outs, axis=0),
    )


def solution(mesh):
    in_specs = (
        P(None, ("dp", "tensor"), None),
        P(None, ("dp", "tensor"), None),
        P(None, "dp", None),
        P(None, "dp", None),
        P("dp"),
        P("dp", None, "tensor"),
        P(None, ("tensor", "dp")),
        P(("tensor", "dp")),
        P(("tensor", "dp"), None),
        P("dp", "tensor"),
        P(("tensor", "dp")),
        P(None, ("tensor", "dp")),
        P(("tensor", "dp")),
        P("tensor", "dp"),
    )
    out_specs = (
        P(None, ("dp", "tensor"), None),
        P(None, ("dp", "tensor"), None),
        P("dp"),
        P("dp", None, "tensor"),
        P(None, ("tensor", "dp")),
        P(("tensor", "dp")),
        P(("tensor", "dp"), None),
        P("dp", "tensor"),
        P(("tensor", "dp")),
        P(None, ("tensor", "dp")),
        P(("tensor", "dp")),
        P("tensor", "dp"),
    )
    return jax.shard_map(
        on_device, mesh=mesh, in_specs=in_specs, out_specs=out_specs, check_vma=False
    )
```

```python
import functools

import jax
import jax.numpy as jnp
from jax import lax
from jax.experimental import pallas as pl
from jax.experimental.pallas import tpu as pltpu
from jax.sharding import PartitionSpec as P

epsilon = 1e-05
log2e = 1.4426950408889634
far = 1e6
chunk = 16
f32 = jnp.float32
bf16 = jnp.bfloat16
highest = lax.Precision.HIGHEST
small_cost = pl.CostEstimate(flops=1, bytes_accessed=1, transcendentals=0)
last_dims = (((1,), (1,)), ((), ()))
first_dims = (((0,), (0,)), ((), ()))


def positions(length_row, order_row, slot_count):
    number = order_row.shape[0]
    picked = (order_row[:, None] == jnp.arange(number, dtype=jnp.int32)[None, :]).astype(jnp.int32)
    ordered = jnp.sum(picked * length_row[None, :], axis=1)
    seq_ends = jnp.cumsum(ordered)
    starts = jnp.concatenate([jnp.zeros((1,), jnp.int32), seq_ends])
    slot_ids = jnp.arange(slot_count, dtype=jnp.int32)
    seq_begin = jnp.max(jnp.where(starts[None, :] <= slot_ids[:, None], starts[None, :], 0), axis=1)
    return (slot_ids - seq_begin, (slot_ids < seq_ends[-1]).astype(jnp.float32))


def swapped(values, axis, bit):
    count = lax.axis_size(axis)
    return lax.ppermute(values, axis, [(i, i ^ bit) for i in range(count)])


def tensor_gather(values, axis):
    if lax.axis_size("tensor") != 2:
        return lax.all_gather(values, "tensor", axis=axis, tiled=True)
    other = swapped(values, "tensor", 1)
    mine_first = lax.axis_index("tensor") == 0
    low = jnp.where(mine_first, values, other)
    high = jnp.where(mine_first, other, values)
    return jnp.concatenate([low, high], axis=axis)


def tensor_sum(values, kind=f32):
    if lax.axis_size("tensor") != 2:
        return lax.psum(values, "tensor")
    return values + swapped(values.astype(kind), "tensor", 1).astype(f32)


def moved(values, offset):
    count = lax.axis_size("dp")
    return lax.ppermute(values, "dp", [((i + 4 * offset) % count, i) for i in range(count)])


def reduce_scatter(values):
    count = lax.axis_size("dp")
    outer = count // 4
    kind = values.dtype
    here = lax.axis_index("dp")
    parts = values.reshape((outer, 2, 2, values.shape[0] // count) + values.shape[1:])
    core = here % 2
    cross = (here // 2) % 2
    place = here // 4
    kept = lax.dynamic_index_in_dim(parts, core, 2, False)
    sent = lax.dynamic_index_in_dim(parts, 1 - core, 2, False)
    parts = (kept.astype(f32) + swapped(sent, "dp", 1).astype(f32)).astype(kind)
    kept = lax.dynamic_index_in_dim(parts, cross, 1, False)
    sent = lax.dynamic_index_in_dim(parts, 1 - cross, 1, False)
    parts = (kept.astype(f32) + swapped(sent, "dp", 2).astype(f32)).astype(kind)
    total = lax.dynamic_index_in_dim(parts, place, 0, False).astype(f32)
    for offset in range(1, outer):
        sent = lax.dynamic_index_in_dim(parts, (place + outer - offset) % outer, 0, False)
        total = total + moved(sent, offset).astype(f32)
    return total


def scan_kernel(
    states,
    pre_ref,
    act_ref,
    normed_ref,
    cot_ref,
    gate_weight_ref,
    out_weight_ref,
    rank_ref,
    step_weight_ref,
    mask_ref,
    in_ref,
    out_ref,
    in_block_ref,
    out_block_ref,
    skip_ref,
    decay_ref,
    gated_ref,
    dgate_ref,
    dact_ref,
    step_grad_ref,
    sums_ref,
    rank_grad_ref,
    din_ref,
    dout_ref,
    gate_s,
    dgated_s,
    step_s,
    drive_s,
    dscan_s,
    scanned_s,
    dpre_s,
    state_s,
    power_s,
    odd_s,
    even_s,
    odd_rate_s,
    even_rate_s,
    decay_s,
):
    tok, width = pre_ref.shape
    tiles = width // 128
    rows = chunk * states
    count = tok // chunk
    first = pl.program_id(1) == 0
    decay = -jnp.exp(decay_ref[...])
    decay_two = decay * log2e
    skip = skip_ref[0:1, :]
    row_ids = lax.broadcasted_iota(jnp.int32, (chunk, rows), 0)
    col_ids = lax.broadcasted_iota(jnp.int32, (chunk, rows), 1)
    ones_block = (lax.div(col_ids, states) == row_ids).astype(bf16)
    gate_s[...] = jnp.dot(normed_ref[...], gate_weight_ref[...], preferred_element_type=f32)
    dgated_s[...] = jnp.dot(cot_ref[...], out_weight_ref[...], preferred_element_type=f32)

    def spread(ref, at):
        one = ref[pl.ds(at, states), :]
        return jnp.concatenate([one] * tiles, axis=1) if tiles > 1 else one

    def softplus(v):
        return jnp.maximum(v, 0.0) + jnp.log1p(jnp.exp(-jnp.abs(v)))

    def run_forward(step, state, low_s):
        base = pl.multiple_of(step * chunk, chunk)
        cut = pl.ds(base, chunk)
        step_size = softplus(pre_ref[cut, :])
        keep = mask_ref[cut, 1:2]
        live = mask_ref[cut, 0:1]
        gate = gate_s[cut, :]
        step_s[cut, :] = step_size + far * (1.0 - keep)
        drive_s[cut, :] = step_size * act_ref[cut, :].astype(f32)
        dscan_s[cut, :] = dgated_s[cut, :] * live * gate * jax.nn.sigmoid(gate)
        for i in range(chunk):
            row = pl.ds(base + i, 1)
            at = pl.multiple_of((base + i) * states, states)
            power = step_s[row, :] * decay_two
            power_s[pl.ds(at, states), :] = power
            state = jnp.exp2(power) * state + drive_s[row, :] * spread(in_ref, at)
            state_s[pl.ds(at, states), :] = state
            low_s[pl.ds(i * states, states), :] = state.astype(bf16)
        return state

    def sum_forward(step, low_s):
        cut = pl.ds(pl.multiple_of(step * chunk, chunk), chunk)
        low = low_s[...]
        scanned_s[cut, :] = jnp.dot(out_block_ref[cut, :], low, preferred_element_type=f32)
        dout_ref[cut, :] = lax.dot_general(dscan_s[cut, :].astype(bf16), low, last_dims, preferred_element_type=f32)

    def forward(pair, state):
        sum_forward(jnp.maximum(2 * pair - 1, 0), odd_s)
        state = run_forward(2 * pair, state, even_s)
        sum_forward(2 * pair, even_s)
        return run_forward(2 * pair + 1, state, odd_s)

    zero = jnp.zeros((states, width), f32)
    odd_s[...] = jnp.zeros_like(odd_s)
    lax.fori_loop(0, count // 2, forward, zero)
    sum_forward(count - 1, odd_s)
    decay_s[...] = zero

    def run_backward(step, handed, low_s, rate_s):
        base = pl.multiple_of(step * chunk, chunk)
        acc = decay_s[...]
        for i in reversed(range(chunk)):
            row = pl.ds(base + i, 1)
            at = pl.multiple_of((base + i) * states, states)
            power = power_s[pl.ds(at, states), :]
            adjoint = dscan_s[row, :] * spread(out_ref, at) + handed
            low_s[pl.ds(i * states, states), :] = adjoint.astype(bf16)
            handed = jnp.exp2(power) * adjoint
            if i == 0:
                before = pl.multiple_of(jnp.maximum(at - states, 0), states)
            else:
                before = pl.multiple_of((base + (i - 1)) * states, states)
            rate = handed * state_s[pl.ds(before, states), :]
            rate_s[pl.ds(i * states, states), :] = (rate * decay).astype(bf16)
            acc = acc + rate * power
        decay_s[...] = acc
        return handed

    def sum_backward(step, low_s, rate_s, accs):
        skip_acc, bias_acc = accs
        cut = pl.ds(pl.multiple_of(step * chunk, chunk), chunk)
        low = low_s[...]
        in_sum = jnp.dot(in_block_ref[cut, :], low, preferred_element_type=f32)
        rate_sum = jnp.dot(ones_block, rate_s[...], preferred_element_type=f32)
        din_ref[cut, :] = lax.dot_general(drive_s[cut, :].astype(bf16), low, last_dims, preferred_element_type=f32)
        pre = pre_ref[cut, :]
        live = mask_ref[cut, 0:1]
        gate = gate_s[cut, :]
        sig = jax.nn.sigmoid(gate)
        act = act_ref[cut, :].astype(f32)
        dscan = dscan_s[cut, :]
        dpre = ((rate_sum + in_sum * act) * jax.nn.sigmoid(pre)).astype(bf16)
        dpre_s[cut, :] = dpre
        dact_ref[cut, :] = dscan * skip + in_sum * softplus(pre)
        branch = (scanned_s[cut, :] + skip * act) * live
        gated_ref[cut, :] = (branch * gate * sig).astype(bf16)
        dgate_ref[cut, :] = (dgated_s[cut, :] * branch * sig * (1.0 + gate * (1.0 - sig))).astype(bf16)
        skip_acc = skip_acc + jnp.sum((dscan * act).reshape(chunk // 8, 8, width), axis=0)
        bias_acc = bias_acc + jnp.sum(dpre.astype(f32).reshape(chunk // 8, 8, width), axis=0)
        return skip_acc, bias_acc

    eight = jnp.zeros((8, width), f32)
    last = count - 1
    handed = run_backward(last, zero, odd_s, odd_rate_s)

    def backward(pair, carry):
        handed, accs = carry
        step = last - 2 * pair
        accs = sum_backward(step, odd_s, odd_rate_s, accs)
        handed = run_backward(step - 1, handed, even_s, even_rate_s)
        accs = sum_backward(step - 1, even_s, even_rate_s, accs)
        handed = run_backward(step - 2, handed, odd_s, odd_rate_s)
        return handed, accs

    handed, accs = lax.fori_loop(0, count // 2 - 1, backward, (handed, (eight, eight)))
    accs = sum_backward(1, odd_s, odd_rate_s, accs)
    run_backward(0, handed, even_s, even_rate_s)
    skip_acc, bias_acc = sum_backward(0, even_s, even_rate_s, accs)
    rank_grad_ref[...] = lax.dot_general(dpre_s[...], step_weight_ref[...], last_dims, preferred_element_type=f32)
    step_part = lax.dot_general(rank_ref[...], dpre_s[...], first_dims, preferred_element_type=f32)
    small = jnp.concatenate(
        [jnp.sum(skip_acc, axis=0, keepdims=True), jnp.sum(bias_acc, axis=0, keepdims=True), jnp.zeros((6, width), f32)],
        axis=0,
    )

    @pl.when(first)
    def _():
        step_grad_ref[...] = step_part
        sums_ref[0:8, :] = small
        sums_ref[8:, :] = decay_s[...] * (1.0 / log2e)

    @pl.when(jnp.logical_not(first))
    def _():
        step_grad_ref[...] += step_part
        sums_ref[0:8, :] += small
        sums_ref[8:, :] += decay_s[...] * (1.0 / log2e)


def scan_both_ways(start, blocks, width, pre, act, normed, cot, weights, rank_low, step_weight, mask, tables, skip, decay_log):
    micro, tok, chans = pre.shape
    dim = normed.shape[2]
    states = decay_log.shape[0]
    rows = chunk * states
    rank = rank_low.shape[2]

    def whole(r, c):
        return pl.BlockSpec((None, r, c), lambda j, m: (m, 0, 0))

    def each(r, c):
        return pl.BlockSpec((None, None, r, c), lambda j, m: (j, m, 0, 0))

    def part(r):
        return pl.BlockSpec((None, r, width), lambda j, m: (m, 0, j))

    def later(r):
        return pl.BlockSpec((None, r, width), lambda j, m: (m, 0, j + start))

    def param(r, at):
        return pl.BlockSpec((r, width), lambda j, m: (0, j + at))

    def shaped(*dims, kind=f32):
        return jax.ShapeDtypeStruct(dims, kind)

    total = blocks * width
    return pl.pallas_call(
        functools.partial(scan_kernel, states),
        grid=(blocks, micro),
        in_specs=[later(tok)] * 2
        + [whole(tok, dim)] * 2
        + [pl.BlockSpec((None, dim, width), lambda j, m, k=k, at=at: (k, 0, j + at)) for _, k, at in weights]
        + [whole(tok, rank), param(rank, start), whole(tok, mask.shape[2])]
        + [whole(tok * states, 128)] * 2
        + [whole(tok, rows)] * 2
        + [param(1, start), param(states, start)],
        out_specs=[part(tok)] * 3
        + [param(rank, 0), param(8 + states, 0), each(tok, rank), each(tok, rows), each(tok, rows)],
        out_shape=[shaped(micro, tok, total, kind=bf16)] * 2
        + [shaped(micro, tok, total), shaped(rank, total), shaped(8 + states, total)]
        + [shaped(blocks, micro, tok, rank), shaped(blocks, micro, tok, rows), shaped(blocks, micro, tok, rows)],
        scratch_shapes=[pltpu.VMEM((tok, width), f32)] * 6
        + [pltpu.VMEM((tok, width), bf16)]
        + [pltpu.VMEM((tok * states, width), f32)] * 2
        + [pltpu.VMEM((rows, width), bf16)] * 4
        + [pltpu.VMEM((states, width), f32)],
        compiler_params=pltpu.CompilerParams(
            dimension_semantics=("arbitrary", "arbitrary"), vmem_limit_bytes=58 * 2**20
        ),
        cost_estimate=small_cost,
    )(pre, act, normed, cot, *[v for v, _, _ in weights], rank_low, step_weight, mask, *tables, skip[None], decay_log)


def halves(values):
    high = values.astype(bf16)
    return high, (values - high.astype(f32)).astype(bf16)


def middle_kernel(states, selected_ref, weight_ref, bias_ref, pre_ref, rank_ref, in_ref, out_ref, in_block_ref, out_block_ref):
    tokens = selected_ref.shape[0]
    rank = weight_ref.shape[0]
    rows = chunk * states
    selected = selected_ref[...]
    low = selected[:, :rank].astype(bf16)
    rank_ref[...] = low
    pre_ref[...] = jnp.dot(low, weight_ref[...], preferred_element_type=f32) + bias_ref[...]
    state_ids = lax.broadcasted_iota(jnp.int32, (states, rows), 0)
    col_ids = lax.broadcasted_iota(jnp.int32, (states, rows), 1)
    spreading = (lax.rem(col_ids, states) == state_ids).astype(bf16)
    row_ids = lax.broadcasted_iota(jnp.int32, (chunk, rows), 0)
    chunk_cols = lax.broadcasted_iota(jnp.int32, (chunk, rows), 1)
    same = lax.div(chunk_cols, states) == row_ids
    ones = jnp.ones((2 * chunk, 128), bf16)
    for at, lanes_ref, block_ref in ((rank, in_ref, in_block_ref), (rank + states, out_ref, out_block_ref)):
        tiled = [
            jnp.dot(v, spreading, preferred_element_type=f32) for v in halves(selected[:, at : at + states])
        ]
        for i in range(tokens // chunk):
            cut = slice(i * chunk, (i + 1) * chunk)
            high, rest = [jnp.where(same, v[cut], 0.0).astype(bf16) for v in tiled]
            block_ref[cut, :] = high
            lanes_ref[i * rows : (i + 1) * rows, :] = lax.dot_general(
                jnp.concatenate([high, rest], axis=0), ones, first_dims, preferred_element_type=f32
            )


def middle(selected, weight, bias, states):
    tokens, picked = selected.shape
    rank, channels = weight.shape
    rows = chunk * states
    cut = min(128, tokens)

    def fixed(r, c):
        return pl.BlockSpec((r, c), lambda i: (0, 0))

    def part(r, c):
        return pl.BlockSpec((r, c), lambda i: (i, 0))

    def shaped(r, c, kind):
        return jax.ShapeDtypeStruct((r, c), kind)

    return pl.pallas_call(
        functools.partial(middle_kernel, states),
        grid=(tokens // cut,),
        in_specs=[part(cut, picked), fixed(rank, channels), fixed(1, channels)],
        out_specs=[part(cut, channels), part(cut, rank)]
        + [part(cut * states, 128)] * 2
        + [part(cut, rows)] * 2,
        out_shape=[shaped(tokens, channels, f32), shaped(tokens, rank, bf16)]
        + [shaped(tokens * states, 128, f32)] * 2
        + [shaped(tokens, rows, bf16)] * 2,
        compiler_params=pltpu.CompilerParams(dimension_semantics=("arbitrary",), vmem_limit_bytes=48 * 2**20),
    )(selected, weight, bias[None])


def unblocked(fulls, states):
    tok, rows = fulls[0].shape[2:]
    same = jnp.arange(tok)[:, None] % chunk == jnp.arange(rows)[None, :] // states
    picks = (jnp.arange(rows)[:, None] % states == jnp.arange(states)[None, :]).astype(f32)
    full = sum(v[j] for v in fulls for j in range(v.shape[0]))
    return jnp.dot(jnp.where(same[None], full, 0.0), picks, precision=highest)


def behind(values, steps):
    return values if steps == 0 else pltpu.roll(values, steps, 0)


def ahead(values, steps):
    return values if steps == 0 else pltpu.roll(values, values.shape[0] - steps, 0)


def convolve(inner, mask_ref, weight_ref, bias_ref):
    taps = weight_ref.shape[0]
    total = bias_ref[...] + weight_ref[taps - 1 : taps, :] * inner
    for back in range(1, taps):
        tap = taps - 1 - back
        total = total + weight_ref[tap : tap + 1, :] * behind(inner, back) * mask_ref[:, back : back + 1]
    return total


def inner_kernel(bounds, normed_ref, *refs):
    *weight_refs, mask_ref, conv_ref, bias_ref, select_ref, inner_ref, convolved_ref, act_ref, selected_ref = refs
    tile = pl.program_id(0)
    for ref, low, high in zip(weight_refs, bounds[:-1], bounds[1:]):

        @pl.when(jnp.logical_and(tile >= low, tile < high))
        def _(ref=ref):
            inner_ref[...] = jnp.dot(normed_ref[...], ref[...], preferred_element_type=f32)

    convolved = convolve(inner_ref[...], mask_ref, conv_ref, bias_ref)
    convolved_ref[...] = convolved
    act = (convolved * jax.nn.sigmoid(convolved)).astype(bf16)
    act_ref[...] = act
    part = jnp.dot(act, select_ref[...], preferred_element_type=f32)
    selected_ref[...] = jnp.where(tile == 0, part, selected_ref[...] + part)


def inner_forward(normed, weights, mask, conv_w, conv_b, select):
    tokens, dim = normed.shape
    channels = sum(v.shape[1] for v in weights)
    width = min([256] + [v.shape[1] for v in weights])
    taps = conv_w.shape[0]
    picked = select.shape[1]
    bounds = [0]
    for v in weights:
        bounds.append(bounds[-1] + v.shape[1] // width)

    def fixed(r, c):
        return pl.BlockSpec((r, c), lambda j: (0, 0))

    def part(r):
        return pl.BlockSpec((r, width), lambda j: (0, j))

    def held(low, high):
        return pl.BlockSpec((dim, width), lambda j: (0, jnp.clip(j - low, 0, high - low - 1)))

    return pl.pallas_call(
        functools.partial(inner_kernel, tuple(bounds)),
        grid=(channels // width,),
        in_specs=[fixed(tokens, dim)]
        + [held(low, high) for low, high in zip(bounds[:-1], bounds[1:])]
        + [
            fixed(tokens, mask.shape[1]),
            part(taps),
            part(1),
            pl.BlockSpec((width, picked), lambda j: (j, 0)),
        ],
        out_specs=[part(tokens)] * 3 + [fixed(tokens, picked)],
        out_shape=[
            jax.ShapeDtypeStruct((tokens, channels), f32),
            jax.ShapeDtypeStruct((tokens, channels), f32),
            jax.ShapeDtypeStruct((tokens, channels), bf16),
            jax.ShapeDtypeStruct((tokens, picked), f32),
        ],
        compiler_params=pltpu.CompilerParams(dimension_semantics=("arbitrary",), vmem_limit_bytes=48 * 2**20),
        cost_estimate=small_cost,
    )(normed, *weights, mask, conv_w, conv_b[None], select)


def assemble_kernel(outer, places_ref, *refs):
    *groups, out_ref = refs
    for i, ref in enumerate(groups):

        @pl.when(lax.div(pl.program_id(0), outer) == i)
        def _(ref=ref):
            out_ref[...] = ref[...]


def assemble(groups, places):
    count = places.shape[0]
    outer = count // len(groups)
    rows, width = groups[0].shape
    own = rows // outer

    def held(i):
        return pl.BlockSpec((own, width), lambda r, _: (jnp.clip(r - i * outer, 0, outer - 1), 0))

    return pl.pallas_call(
        functools.partial(assemble_kernel, outer),
        grid_spec=pltpu.PrefetchScalarGridSpec(
            num_scalar_prefetch=1,
            grid=(count,),
            in_specs=[held(i) for i in range(len(groups))],
            out_specs=pl.BlockSpec((own, width), lambda r, where: (where[r], 0)),
        ),
        out_shape=jax.ShapeDtypeStruct((rows * len(groups), width), groups[0].dtype),
        compiler_params=pltpu.CompilerParams(dimension_semantics=("arbitrary",), vmem_limit_bytes=48 * 2**20),
        cost_estimate=small_cost,
    )(places, *groups)


def inner_back_kernel(bounds, places_ref, *refs):
    *dact_refs, dsel_ref, select_ref, inner_ref, convolved_ref, act_ref, mask_ref, conv_ref, left_ref = refs[:-6]
    dinner_ref, sums_ref, select_grad_ref, sent_ref, kept_ref, dact_s = refs[-6:]
    taps = conv_ref.shape[0]
    tile = pl.program_id(0)
    for ref, low, high in zip(dact_refs, bounds[:-1], bounds[1:]):

        @pl.when(jnp.logical_and(tile >= low, tile < high))
        def _(ref=ref):
            dact_s[...] = ref[...]

    inner = inner_ref[...]
    dsel = dsel_ref[...]
    convolved = convolved_ref[...]
    sig = jax.nn.sigmoid(convolved)
    dact = dact_s[...] + lax.dot_general(dsel, select_ref[...], last_dims, preferred_element_type=f32)
    dconv = dact * sig * (1.0 + convolved * (1.0 - sig))
    dinner = conv_ref[taps - 1 : taps, :] * dconv
    sums_ref[taps : taps + 1, :] = jnp.sum(dconv, axis=0, keepdims=True)
    sums_ref[taps - 1 : taps, :] = jnp.sum(dconv * inner, axis=0, keepdims=True)
    for back in range(1, taps):
        tap = taps - 1 - back
        moved = ahead(dconv * mask_ref[:, back : back + 1], back)
        sums_ref[tap : tap + 1, :] = jnp.sum(moved * inner, axis=0, keepdims=True)
        dinner = dinner + conv_ref[tap : tap + 1, :] * moved
    low = dinner.astype(bf16)
    dinner_ref[...] = low
    select_grad_ref[...] = lax.dot_general(dsel, act_ref[...], first_dims, preferred_element_type=f32)
    outer, own = kept_ref.shape[1], kept_ref.shape[3]
    for core, out_ref in ((1, sent_ref), (0, kept_ref)):
        for cross in range(2):
            at = (2 * core + cross) * outer
            rows = [
                left_ref[pl.ds(pl.multiple_of(places_ref[at + j] * own, own), own), :] for j in range(outer)
            ]
            full = jnp.dot(jnp.concatenate(rows, axis=0), low, preferred_element_type=f32).astype(bf16)
            for j in range(outer):
                out_ref[cross, j, 0] = full[j * own : (j + 1) * own]


def inner_backward(places, dacts, dsel, select, inner, convolved, act, mask, conv_w, left):
    tokens, channels = inner.shape
    count = places.shape[0]
    outer, own = count // 4, left.shape[0] // count
    width = min([256] + [v.shape[1] for v in dacts])
    taps = conv_w.shape[0]
    picked = select.shape[1]
    bounds = [0]
    for v in dacts:
        bounds.append(bounds[-1] + v.shape[1] // width)

    def fixed(r, c):
        return pl.BlockSpec((r, c), lambda j, _: (0, 0))

    def part(r):
        return pl.BlockSpec((r, width), lambda j, _: (0, j))

    def held(low, high):
        return pl.BlockSpec((tokens, width), lambda j, _: (0, jnp.clip(j - low, 0, high - low - 1)))

    parts = pl.BlockSpec((2, outer, 1, own, width), lambda j, _: (0, 0, 0, 0, j))
    return pl.pallas_call(
        functools.partial(inner_back_kernel, tuple(bounds)),
        grid_spec=pltpu.PrefetchScalarGridSpec(
            num_scalar_prefetch=1,
            grid=(channels // width,),
            in_specs=[held(low, high) for low, high in zip(bounds[:-1], bounds[1:])]
            + [
                fixed(tokens, picked),
                pl.BlockSpec((width, picked), lambda j, _: (j, 0)),
                part(tokens),
                part(tokens),
                part(tokens),
                fixed(tokens, mask.shape[1]),
                part(taps),
                fixed(*left.shape),
            ],
            out_specs=[part(tokens), part(8), part(picked), parts, parts],
            scratch_shapes=[pltpu.VMEM((tokens, width), f32)],
        ),
        out_shape=[
            jax.ShapeDtypeStruct((tokens, channels), bf16),
            jax.ShapeDtypeStruct((8, channels), f32),
            jax.ShapeDtypeStruct((picked, channels), f32),
        ]
        + [jax.ShapeDtypeStruct((2, outer, 1, own, channels), bf16)] * 2,
        compiler_params=pltpu.CompilerParams(dimension_semantics=("arbitrary",), vmem_limit_bytes=52 * 2**20),
        cost_estimate=small_cost,
    )(places, *dacts, dsel, select, inner, convolved, act, mask, conv_w, left)


def project_kernel(count, where_ref, *refs):
    lefts, rights, out_ref = refs[:count], refs[count:-1], refs[-1]
    total = None
    for left, right in zip(lefts, rights):
        rows = jnp.concatenate([left[m] for m in range(left.shape[0])], axis=0)
        part = lax.dot_general(rows, right[...], last_dims, preferred_element_type=f32)
        total = part if total is None else total + part
    rows = out_ref.shape[1]
    for m in range(out_ref.shape[0]):
        out_ref[m] = total[m * rows : (m + 1) * rows].astype(out_ref.dtype)


def project(terms, where, shard_rows, kind):
    micro = terms[0][0].shape[0]
    dim = terms[0][3].shape[1]
    width = min(256, dim)

    def column(plane, at, wide):
        return pl.BlockSpec((None, width, wide), lambda i, _: (plane, i, at))

    def left_rows(at, wide):
        return pl.BlockSpec((micro, shard_rows, wide), lambda i, who: (0, who[0], at))

    return pl.pallas_call(
        functools.partial(project_kernel, len(terms)),
        grid_spec=pltpu.PrefetchScalarGridSpec(
            num_scalar_prefetch=1,
            grid=(dim // width,),
            in_specs=[left_rows(at, wide) for _, at, wide, _, _, _ in terms]
            + [column(plane, at, wide) for _, _, wide, _, plane, at in terms],
            out_specs=pl.BlockSpec((micro, shard_rows, width), lambda i, _: (0, 0, i)),
        ),
        out_shape=jax.ShapeDtypeStruct((micro, shard_rows, dim), kind),
        compiler_params=pltpu.CompilerParams(dimension_semantics=("arbitrary",), vmem_limit_bytes=48 * 2**20),
        cost_estimate=small_cost,
    )(where, *[t[0] for t in terms], *[t[3] for t in terms])


def project_all(terms):
    total = 0.0
    for left, left_at, wide, right, plane, at in terms:
        total = total + jnp.einsum(
            "mgc,dc->mgd",
            left[..., left_at * wide : (left_at + 1) * wide],
            right[plane, :, at * wide : (at + 1) * wide],
            preferred_element_type=f32,
        )
    return lax.psum_scatter(total.astype(bf16), "tensor", scatter_dimension=1, tiled=True)


def parts_kernel(kinds, outer, places_ref, *refs):
    out_ref = refs[-1]
    own = refs[0].shape[0]
    for kind in range(kinds):
        left = jnp.concatenate([r[...] for r in refs[kind * outer : (kind + 1) * outer]], axis=0)
        full = jnp.dot(left, refs[kinds * outer + kind][...], preferred_element_type=f32).astype(bf16)
        for j in range(outer):
            out_ref[j, kind] = full[j * own : (j + 1) * own]


def grad_parts(places, near, lefts, rights):
    kinds = len(lefts)
    count = places.shape[0]
    outer = count // 4
    own = lefts[0].shape[0] // count
    tokens = lefts[0].shape[1]
    width = rights[0].shape[1]
    offset = 0 if near else 2 * outer

    def left_spec(j):
        return pl.BlockSpec((own, tokens), lambda q, where: (where[offset + q * outer + j], 0))

    return pl.pallas_call(
        functools.partial(parts_kernel, kinds, outer),
        grid_spec=pltpu.PrefetchScalarGridSpec(
            num_scalar_prefetch=1,
            grid=(2,),
            in_specs=[left_spec(j) for _ in range(kinds) for j in range(outer)]
            + [pl.BlockSpec(v.shape, lambda q, where: (0, 0)) for v in rights],
            out_specs=pl.BlockSpec((None, outer, kinds, own, width), lambda q, where: (q, 0, 0, 0, 0)),
        ),
        out_shape=jax.ShapeDtypeStruct((2, outer, kinds, own, width), bf16),
        compiler_params=pltpu.CompilerParams(dimension_semantics=("arbitrary",), vmem_limit_bytes=48 * 2**20),
        cost_estimate=small_cost,
    )(places, *[v for v in lefts for _ in range(outer)], *rights)


def join(*trees):
    return lax.optimization_barrier(trees)


def summed(first, second, *more):
    total = first.astype(f32) + second.astype(f32)
    for v in more:
        total = total + v.astype(f32)
    return total


def sums_kernel(crosses, alongs, outer, *refs):
    ins = 2 * sum(crosses) + 3 * sum(alongs)
    given, outs = iter(refs[:ins]), iter(refs[ins:])
    for sources in crosses:
        out, at = next(outs), 0
        for _ in range(sources):
            kept, got = next(given), next(given)
            total = (kept[...].astype(f32) + got[...].astype(f32)).astype(bf16)
            out[..., at : at + total.shape[-1]] = total
            at += total.shape[-1]
    for sources in alongs:
        out, at = [next(outs) for _ in range(outer)], 0
        for _ in range(sources):
            kept, got, across = next(given), next(given), next(given)
            wide = kept.shape[-1]
            for j in range(outer):
                total = kept[j].astype(f32) + got[j].astype(f32) + across[j].astype(f32)
                out[j][..., at : at + wide] = total.astype(out[j].dtype)
            at += wide


def step_sums(crosses, alongs):
    cuts = 2
    in_specs, out_specs, out_shape, given = [], [], [], []
    outer = (crosses + alongs)[0][0][0].shape[1]

    def taken(shape, first, at, wide):
        block = (None,) + shape[1:-2] + (shape[-2] // cuts, wide)
        return pl.BlockSpec(block, lambda i: (first,) + (0,) * (len(shape) - 3) + (i, at))

    def plain(shape, at=0):
        return pl.BlockSpec(
            shape[:-2] + (shape[-2] // cuts, shape[-1]), lambda i: (0,) * (len(shape) - 2) + (i, at)
        )

    for sources in crosses:
        for kept, got, at, wide in sources:
            in_specs += [taken(kept.shape, 1, at, wide)] * 2
            given += [kept, got]
        out = sources[0][0].shape[1:-1] + (sum(v[3] for v in sources),)
        out_specs.append(plain(out))
        out_shape.append(jax.ShapeDtypeStruct(out, bf16))
    for sources in alongs:
        for kept, got, at, wide, across, across_at in sources:
            in_specs += [taken(kept.shape, 0, at, wide)] * 2 + [plain(across.shape[:-1] + (wide,), across_at)]
            given += [kept, got, across]
        out = sources[0][0].shape[2:-1] + (sum(v[3] for v in sources),)
        out_specs += [plain(out)] * outer
        out_shape += [jax.ShapeDtypeStruct(out, f32 if j == 0 else bf16) for j in range(outer)]
    outs = pl.pallas_call(
        functools.partial(
            sums_kernel, tuple(len(v) for v in crosses), tuple(len(v) for v in alongs), outer
        ),
        grid=(cuts,),
        in_specs=in_specs,
        out_specs=out_specs,
        out_shape=out_shape,
        compiler_params=pltpu.CompilerParams(dimension_semantics=("arbitrary",), vmem_limit_bytes=48 * 2**20),
        cost_estimate=small_cost,
    )(*given)
    outs = list(outs)
    first, rest = outs[: len(crosses)], outs[len(crosses) :]
    return first, [rest[i * outer : (i + 1) * outer] for i in range(len(alongs))]


def along_moves(rows):
    count = lax.axis_size("dp")
    return rows[:1] + [
        lax.ppermute(v, "dp", [(i, (i + 4 * (j + 1)) % count) for i in range(count)])
        for j, v in enumerate(rows[1:])
    ]


def final_kernel(turned, *refs):
    terms, outs = refs[: len(refs) - len(turned)], refs[len(refs) - len(turned) :]
    total = terms[0][...]
    for ref in terms[1:]:
        total = total + ref[...].astype(f32)
    for i, turn in enumerate(turned):
        outs[i][...] = total[i].T if turn else total[i]


def final_sum(terms, turned):
    kinds, own, width = terms[0].shape
    return pl.pallas_call(
        functools.partial(final_kernel, turned),
        out_shape=[jax.ShapeDtypeStruct((width, own) if turn else (own, width), f32) for turn in turned],
        compiler_params=pltpu.CompilerParams(vmem_limit_bytes=48 * 2**20),
        cost_estimate=small_cost,
    )(*terms)


def doubled(values):
    count = lax.axis_size("dp")
    here = lax.axis_index("dp")
    values = values[None]
    bit = 1
    while bit < count:
        other = swapped(values, "dp", bit)
        low = (here & bit) == 0
        values = jnp.concatenate([jnp.where(low, values, other), jnp.where(low, other, values)], axis=0)
        bit *= 2
    return values


def finish_kernel(hidden_ref, cot_ref, gain_ref, layer_ref, layer_away_ref, here_ref, away_ref, layer_out, grad_out):
    hidden = hidden_ref[...]
    scale = lax.rsqrt(jnp.mean(hidden * hidden, axis=-1, keepdims=True) + epsilon)
    normal = hidden * scale
    layer_out[...] = hidden + (layer_ref[...] + layer_away_ref[...].astype(f32))
    dnormed = here_ref[...] + away_ref[...].astype(f32)
    dnormal = dnormed * gain_ref[...]
    middle = jnp.mean(dnormal * normal, axis=-1, keepdims=True)
    grad_out[...] = cot_ref[...].astype(f32) + scale * (dnormal - normal * middle)


def finish(hidden, cotangent, gain, layer_here, layer_away, here, away):
    micro, rows, dim = hidden.shape
    total = micro * rows
    cut = min(64, total)

    def part():
        return pl.BlockSpec((cut, dim), lambda i: (i, 0))

    layer, grad = pl.pallas_call(
        finish_kernel,
        grid=(total // cut,),
        in_specs=[part(), part(), pl.BlockSpec((1, dim), lambda i: (0, 0))] + [part()] * 4,
        out_specs=[part(), part()],
        out_shape=[jax.ShapeDtypeStruct((total, dim), f32)] * 2,
        compiler_params=pltpu.CompilerParams(dimension_semantics=("arbitrary",), vmem_limit_bytes=48 * 2**20),
        cost_estimate=small_cost,
    )(*[v.reshape(-1, dim) for v in (hidden, cotangent, gain, layer_here, layer_away, here, away)])
    return layer.reshape(hidden.shape), grad.reshape(hidden.shape)


def on_device(
    hidden,
    cotangent,
    lengths,
    order,
    norm_gain,
    input_weight,
    conv_weight,
    conv_bias,
    select_weight,
    step_weight,
    step_bias,
    decay_log,
    skip_gain,
    output_weight,
):
    micro, shard_rows, model_dim = hidden.shape
    count = lax.axis_size("dp")
    outer = count // 4
    group_tok = shard_rows * lax.axis_size("tensor")
    tokens = micro * group_tok
    channels = input_weight.shape[2]
    taps = conv_weight.shape[0]
    states = decay_log.shape[0]
    own = conv_bias.shape[0]
    own_dim = norm_gain.shape[0]
    half = channels // 2
    quarter = channels // 4
    here = lax.axis_index("dp")
    ids = jnp.arange(count, dtype=jnp.int32)
    place, cross, core = here // 4, (here // 2) % 2, here % 2
    places = ((place + ids % outer) % outer) * 4 + (cross ^ (ids // outer) % 2) * 2 + (core ^ ids // (2 * outer))
    ranks = ((core ^ ids % 2) * 2 + (cross ^ (ids // 2) % 2)) * outer + (ids // 4 - place) % outer
    places, ranks = places.astype(jnp.int32), ranks.astype(jnp.int32)

    w_inner = lax.all_gather(input_weight[:, 0], "dp", axis=0, tiled=True)
    out_shard = output_weight.T
    weights = []
    for low, high in ((0, half), (half, channels)):
        both = jnp.stack([input_weight[:, 1, low:high], out_shard[:, low:high]])
        both = lax.all_gather(both, "dp", axis=1, tiled=True)
        weights.append(((both, 0, 0), (both, 1, 0)))

    pieces = [norm_gain, conv_weight, conv_bias, step_bias, decay_log, skip_gain]
    packed = doubled(jnp.concatenate([v.reshape(-1) for v in pieces]))
    narrow, packed = join(jnp.concatenate([select_weight.T, step_weight.reshape(-1, own)], axis=0), packed)
    full = []
    at = 0
    for v in pieces:
        part = packed[:, at : at + v.size]
        at += v.size
        if v.ndim == 2:
            part = part.reshape(count, v.shape[0], v.shape[1]).transpose(1, 0, 2).reshape(v.shape[0], -1)
        else:
            part = part.reshape(-1)
        full.append(part)
    gain_full, conv_w, conv_b, step_b, decay_lg, skip_g = full
    picked = select_weight.shape[1]
    narrow = jnp.stack([narrow] + [moved(narrow, j) for j in range(1, outer)])
    narrow = jnp.stack([narrow, swapped(narrow, "dp", 2)])
    narrow = jnp.stack([narrow, swapped(narrow, "dp", 1)]).reshape((count,) + narrow.shape[2:])
    narrow = jnp.take(narrow, ranks, axis=0)
    w_sel = narrow[:, :picked].transpose(0, 2, 1).reshape(channels, picked)
    w_step = narrow[:, picked:].reshape(-1, channels)
    rank_dim = w_step.shape[0]

    inverse_rms = lax.rsqrt(jnp.mean(hidden * hidden, axis=-1, keepdims=True) + epsilon)
    normal_rows = hidden * inverse_rms
    normed = tensor_gather((normal_rows * gain_full).astype(bf16), 1).reshape(tokens, model_dim)
    normed, cot_rows = join(normed, cotangent)
    cot_full = tensor_gather(cot_rows, 1).reshape(tokens, model_dim)

    position, live_mask = jax.vmap(lambda a, b: positions(a, b, group_tok))(lengths[:, 0], order[:, 0])
    mask = jnp.stack([live_mask] + [(position >= back).astype(f32) for back in range(1, taps)], axis=2)
    flat_mask = mask.reshape(tokens, taps)

    def grouped(v):
        return v.reshape(micro, group_tok, v.shape[-1])

    inner, convolved, act, selected = inner_forward(normed, [w_inner], flat_mask, conv_w, conv_b, w_sel)
    selected = tensor_sum(selected)
    lefts = (normed.T, cot_full.T)
    pre_step, rank_low, *tables = middle(selected, w_step, step_b, states)
    tables = tuple(grouped(v) if v.shape[0] == tokens else v.reshape(micro, -1, v.shape[-1]) for v in tables)
    rank_rows = grouped(rank_low)

    gated, dgate, dact, step_grads, sums, rank_grads, dins, douts = [[] for _ in range(8)]
    kept, got, across, total = {}, {}, {}, {}
    rows = (grouped(normed), grouped(cot_full))

    def scanned(number, skip_now):
        return scan_both_ways(
            2 * number,
            2,
            quarter,
            grouped(pre_step),
            grouped(act),
            *rows,
            weights[number],
            rank_rows,
            w_step,
            mask,
            tables,
            skip_now,
            decay_lg,
        )

    def hold(results):
        for held, v in zip((gated, dgate, dact), results[:3]):
            held.append(v.reshape(tokens, -1))
        for held, v in zip((step_grads, sums, rank_grads, dins, douts), results[3:]):
            held.append(v)

    def source(piece, at=0, wide=None):
        return kept[piece], got[piece], at, wide or kept[piece].shape[-1]

    def last_step(piece, name, at=0):
        return [source(piece) + (across[name], at)]

    hold(scanned(0, skip_g))
    places_now = places
    for piece, left, right in (("gate", lefts[0], dgate[0]), ("out", lefts[1], gated[0])):
        sent = grad_parts(places_now, False, (left,), (right,))
        sent, places_now = join(sent, places_now)
        got[piece] = swapped(sent, "dp", 1)
        kept[piece] = grad_parts(places_now, True, (left,), (right,))
    cross, _ = step_sums([[source("gate"), source("out")]], [])
    skip_now, cross = join(skip_g, cross)
    across["early"] = swapped(cross[0], "dp", 2)

    results = scanned(1, skip_now)
    results, across["early"] = join(results, across["early"])
    hold(results)
    _, along = step_sums([], [last_step("gate", "early"), last_step("out", "early", 1)])
    along, places_now, rank_grads = join(along, places_now, rank_grads)
    total["gate"] = along_moves(along[0])
    for piece, left, right in (("gate_late", lefts[0], dgate[1]), ("out_late", lefts[1], gated[1])):
        sent = grad_parts(places_now, False, (left,), (right,))
        sent, places_now = join(sent, places_now)
        got[piece] = swapped(sent, "dp", 1)
    rank_grad = sum(v[j] for v in rank_grads for j in range(v.shape[0]))
    select_terms = jnp.concatenate([rank_grad, unblocked(dins, states), unblocked(douts, states)], axis=2)
    select_terms, places_now = join(select_terms.reshape(tokens, -1), places_now)
    select_terms = tensor_sum(select_terms, bf16)
    places_now, total["gate"][1] = join(places_now, total["gate"][1])
    for piece, left, right in (("gate_late", lefts[0], dgate[1]), ("out_late", lefts[1], gated[1])):
        kept[piece] = grad_parts(places_now, True, (left,), (right,))
    two = lax.axis_size("tensor") == 2
    where = lax.axis_index("tensor").astype(jnp.int32)[None]
    kept["out_late"], where = join(kept["out_late"], where)
    out_terms = [(grouped(v), 0, v.shape[1]) + w[1] for v, w in zip(gated, weights)]
    layer_away = project(out_terms, 1 - where, shard_rows, bf16) if two else project_all(out_terms)
    names = ("gate_late", "out_late")
    select_terms, late_kept, late_got, total["gate"], layer_away = join(
        select_terms, [kept[n] for n in names], [got[n] for n in names], total["gate"], layer_away
    )
    for n, one, other in zip(names, late_kept, late_got):
        kept[n], got[n] = one, other
    select_low = select_terms.astype(bf16)
    cross, _ = step_sums([[source("gate_late")], [source("out_late")]], [])
    cross, select_low, along[1] = join(cross, select_low, along[1])
    across["gate_late"] = swapped(cross[0], "dp", 2)
    total["out"] = along_moves(along[1])
    dinner, conv_sums, select_grad, sent, kept["inner"] = inner_backward(
        places_now, dact, select_low, w_sel, inner, convolved, act, flat_mask, conv_w, lefts[0]
    )
    across["gate_late"], total["out"], dinner, conv_sums, select_grad, sent, kept["inner"], where, cross[1] = join(
        across["gate_late"], total["out"], dinner, conv_sums, select_grad, sent, kept["inner"], where, cross[1]
    )
    norm_terms = [(grouped(v), 0, v.shape[1]) + w[0] for v, w in zip(dgate, weights)]
    norm_terms.append((grouped(dinner), 0, channels, w_inner[None], 0, 0))
    got["inner"] = swapped(sent, "dp", 1)
    across["out_late"] = swapped(cross[1], "dp", 2)
    _, along = step_sums([], [last_step("gate_late", "gate_late")])
    along, where = join(along, where)
    total["gate_late"] = along_moves(along[0])
    if two:
        norm_away = project(norm_terms, 1 - where, shard_rows, bf16)
    else:
        norm_away = project_all(norm_terms)
    got["inner"], norm_away, where, total["gate_late"], across["out_late"] = join(
        got["inner"], norm_away, where, total["gate_late"], across["out_late"]
    )
    cross, along = step_sums(
        [[source("inner", 0, half)], [source("inner", 1, half)]], [last_step("out_late", "out_late")]
    )
    cross, along, where, norm_away, select_grad = join(cross, along, where, norm_away, select_grad)
    across["first"] = swapped(cross[0], "dp", 2)
    total["out_late"] = along_moves(along[0])
    if two:
        norm_away = swapped(norm_away, "tensor", 1)
        norm_here = project(norm_terms, where, shard_rows, f32)
        layer_here = project(out_terms, where, shard_rows, f32)
    else:
        norm_here, layer_here = [jnp.zeros(v.shape, f32) for v in (norm_away, layer_away)]
    across["first"], total["out_late"], cross[1], norm_here, layer_here, norm_away = join(
        across["first"], total["out_late"], cross[1], norm_here, layer_here, norm_away
    )
    step_grad = jnp.concatenate(step_grads, axis=1)
    step_grad = step_grad.reshape(count, rank_dim // count, count, own).transpose(1, 2, 0, 3)
    small = jnp.concatenate(
        [select_grad, step_grad.reshape(rank_dim, channels), conv_sums, jnp.concatenate(sums, axis=1)], axis=0
    )
    small = lax.psum_scatter(small, "dp", scatter_dimension=1, tiled=True)
    _, along = step_sums([], [[source("inner", 0, half) + (across["first"], 0)]])
    cross[1], along, layer_away = join(cross[1], along, layer_away)
    across["last"] = swapped(cross[1], "dp", 2)
    total["first"] = along_moves(along[0])
    if two:
        layer_away = swapped(layer_away, "tensor", 1)
    total["gate"], total["first"][1] = join(total["gate"], total["first"][1])
    gates = [final_sum(total[n], (False,))[0] for n in ("gate", "gate_late")]
    outs = [final_sum(total[n], (True,))[0] for n in ("out", "out_late")]
    across["last"], total["first"], gates, outs, layer_away, norm_here = join(
        across["last"], total["first"], gates, outs, layer_away, norm_here
    )
    _, along = step_sums([], [[source("inner", 1, half) + (across["last"], 0)]])
    along, norm_here = join(along, norm_here)
    total["last"] = along_moves(along[0])
    layer_rows, grad_rows = finish(hidden, cotangent, gain_full, layer_here, layer_away, norm_here, norm_away)
    gate_grad = jnp.concatenate(gates, axis=1)
    (first,) = final_sum(total["first"], (False,))
    own_input = input_weight.astype(f32)
    most = jnp.sum(own_input[:, 0, :half] * first, axis=1) + jnp.sum(own_input[:, 1] * gate_grad, axis=1)
    (last,) = final_sum(total["last"], (False,))
    gain_total = tensor_sum(most + jnp.sum(own_input[:, 0, half:] * last, axis=1)) / norm_gain
    at = picked + rank_dim
    return (
        layer_rows,
        grad_rows,
        gain_total,
        jnp.stack([jnp.concatenate([first, last], axis=1), gate_grad], axis=1),
        small[at : at + taps],
        small[at + taps],
        small[:picked].T,
        small[picked:at].reshape(-1, channels),
        small[at + 9],
        small[at + 16 :],
        small[at + 8],
        jnp.concatenate(outs, axis=0),
    )


def solution(mesh):
    in_specs = (
        P(None, ("dp", "tensor"), None),
        P(None, ("dp", "tensor"), None),
        P(None, "dp", None),
        P(None, "dp", None),
        P("dp"),
        P("dp", None, "tensor"),
        P(None, ("tensor", "dp")),
        P(("tensor", "dp")),
        P(("tensor", "dp"), None),
        P("dp", "tensor"),
        P(("tensor", "dp")),
        P(None, ("tensor", "dp")),
        P(("tensor", "dp")),
        P("tensor", "dp"),
    )
    out_specs = (
        P(None, ("dp", "tensor"), None),
        P(None, ("dp", "tensor"), None),
        P("dp"),
        P("dp", None, "tensor"),
        P(None, ("tensor", "dp")),
        P(("tensor", "dp")),
        P(("tensor", "dp"), None),
        P("dp", "tensor"),
        P(("tensor", "dp")),
        P(None, ("tensor", "dp")),
        P(("tensor", "dp")),
        P("tensor", "dp"),
    )
    return jax.shard_map(
        on_device, mesh=mesh, in_specs=in_specs, out_specs=out_specs, check_vma=False
    )
```

```python
import functools

import jax
import jax.numpy as jnp
from jax import lax
from jax.experimental import pallas as pl
from jax.experimental.pallas import tpu as pltpu
from jax.sharding import PartitionSpec as P

epsilon = 1e-05
log2e = 1.4426950408889634
far = 1e6
chunk = 16
f32 = jnp.float32
bf16 = jnp.bfloat16
highest = lax.Precision.HIGHEST
small_cost = pl.CostEstimate(flops=1, bytes_accessed=1, transcendentals=0)
last_dims = (((1,), (1,)), ((), ()))
first_dims = (((0,), (0,)), ((), ()))


def positions(length_row, order_row, slot_count):
    number = order_row.shape[0]
    picked = (order_row[:, None] == jnp.arange(number, dtype=jnp.int32)[None, :]).astype(jnp.int32)
    ordered = jnp.sum(picked * length_row[None, :], axis=1)
    seq_ends = jnp.cumsum(ordered)
    starts = jnp.concatenate([jnp.zeros((1,), jnp.int32), seq_ends])
    slot_ids = jnp.arange(slot_count, dtype=jnp.int32)
    seq_begin = jnp.max(jnp.where(starts[None, :] <= slot_ids[:, None], starts[None, :], 0), axis=1)
    return (slot_ids - seq_begin, (slot_ids < seq_ends[-1]).astype(jnp.float32))


def swapped(values, axis, bit):
    count = lax.axis_size(axis)
    return lax.ppermute(values, axis, [(i, i ^ bit) for i in range(count)])


def tensor_gather(values, axis):
    if lax.axis_size("tensor") != 2:
        return lax.all_gather(values, "tensor", axis=axis, tiled=True)
    other = swapped(values, "tensor", 1)
    mine_first = lax.axis_index("tensor") == 0
    low = jnp.where(mine_first, values, other)
    high = jnp.where(mine_first, other, values)
    return jnp.concatenate([low, high], axis=axis)


def tensor_sum(values, kind=f32):
    if lax.axis_size("tensor") != 2:
        return lax.psum(values, "tensor")
    return values + swapped(values.astype(kind), "tensor", 1).astype(f32)


def moved(values, offset):
    count = lax.axis_size("dp")
    return lax.ppermute(values, "dp", [((i + 4 * offset) % count, i) for i in range(count)])


def reduce_scatter(values):
    count = lax.axis_size("dp")
    outer = count // 4
    kind = values.dtype
    here = lax.axis_index("dp")
    parts = values.reshape((outer, 2, 2, values.shape[0] // count) + values.shape[1:])
    core = here % 2
    cross = (here // 2) % 2
    place = here // 4
    kept = lax.dynamic_index_in_dim(parts, core, 2, False)
    sent = lax.dynamic_index_in_dim(parts, 1 - core, 2, False)
    parts = (kept.astype(f32) + swapped(sent, "dp", 1).astype(f32)).astype(kind)
    kept = lax.dynamic_index_in_dim(parts, cross, 1, False)
    sent = lax.dynamic_index_in_dim(parts, 1 - cross, 1, False)
    parts = (kept.astype(f32) + swapped(sent, "dp", 2).astype(f32)).astype(kind)
    total = lax.dynamic_index_in_dim(parts, place, 0, False).astype(f32)
    for offset in range(1, outer):
        sent = lax.dynamic_index_in_dim(parts, (place + outer - offset) % outer, 0, False)
        total = total + moved(sent, offset).astype(f32)
    return total


def scan_kernel(
    states,
    pre_ref,
    act_ref,
    normed_ref,
    cot_ref,
    gate_weight_ref,
    out_weight_ref,
    rank_ref,
    step_weight_ref,
    mask_ref,
    in_ref,
    out_ref,
    in_block_ref,
    out_block_ref,
    skip_ref,
    decay_ref,
    gated_ref,
    dgate_ref,
    dact_ref,
    step_grad_ref,
    sums_ref,
    rank_grad_ref,
    din_ref,
    dout_ref,
    gate_s,
    dgated_s,
    step_s,
    drive_s,
    dscan_s,
    scanned_s,
    dpre_s,
    state_s,
    power_s,
    odd_s,
    even_s,
    odd_rate_s,
    even_rate_s,
    decay_s,
):
    tok, width = pre_ref.shape
    tiles = width // 128
    rows = chunk * states
    count = tok // chunk
    first = pl.program_id(1) == 0
    decay = -jnp.exp(decay_ref[...])
    decay_two = decay * log2e
    skip = skip_ref[0:1, :]
    row_ids = lax.broadcasted_iota(jnp.int32, (chunk, rows), 0)
    col_ids = lax.broadcasted_iota(jnp.int32, (chunk, rows), 1)
    ones_block = (lax.div(col_ids, states) == row_ids).astype(bf16)
    gate_s[...] = jnp.dot(normed_ref[...], gate_weight_ref[...], preferred_element_type=f32)
    dgated_s[...] = jnp.dot(cot_ref[...], out_weight_ref[...], preferred_element_type=f32)

    def spread(ref, at):
        one = ref[pl.ds(at, states), :]
        return jnp.concatenate([one] * tiles, axis=1) if tiles > 1 else one

    def softplus(v):
        return jnp.maximum(v, 0.0) + jnp.log1p(jnp.exp(-jnp.abs(v)))

    def run_forward(step, state, low_s):
        base = pl.multiple_of(step * chunk, chunk)
        cut = pl.ds(base, chunk)
        step_size = softplus(pre_ref[cut, :])
        keep = mask_ref[cut, 1:2]
        live = mask_ref[cut, 0:1]
        gate = gate_s[cut, :]
        step_s[cut, :] = step_size + far * (1.0 - keep)
        drive_s[cut, :] = step_size * act_ref[cut, :].astype(f32)
        dscan_s[cut, :] = dgated_s[cut, :] * live * gate * jax.nn.sigmoid(gate)
        for i in range(chunk):
            row = pl.ds(base + i, 1)
            at = pl.multiple_of((base + i) * states, states)
            power = step_s[row, :] * decay_two
            power_s[pl.ds(at, states), :] = power
            state = jnp.exp2(power) * state + drive_s[row, :] * spread(in_ref, at)
            state_s[pl.ds(at, states), :] = state
            low_s[pl.ds(i * states, states), :] = state.astype(bf16)
        return state

    def sum_forward(step, low_s):
        cut = pl.ds(pl.multiple_of(step * chunk, chunk), chunk)
        low = low_s[...]
        scanned_s[cut, :] = jnp.dot(out_block_ref[cut, :], low, preferred_element_type=f32)
        dout_ref[cut, :] = lax.dot_general(dscan_s[cut, :].astype(bf16), low, last_dims, preferred_element_type=f32)

    def forward(pair, state):
        sum_forward(jnp.maximum(2 * pair - 1, 0), odd_s)
        state = run_forward(2 * pair, state, even_s)
        sum_forward(2 * pair, even_s)
        return run_forward(2 * pair + 1, state, odd_s)

    zero = jnp.zeros((states, width), f32)
    odd_s[...] = jnp.zeros_like(odd_s)
    lax.fori_loop(0, count // 2, forward, zero)
    sum_forward(count - 1, odd_s)
    decay_s[...] = zero

    def run_backward(step, handed, low_s, rate_s):
        base = pl.multiple_of(step * chunk, chunk)
        acc = decay_s[...]
        for i in reversed(range(chunk)):
            row = pl.ds(base + i, 1)
            at = pl.multiple_of((base + i) * states, states)
            power = power_s[pl.ds(at, states), :]
            adjoint = dscan_s[row, :] * spread(out_ref, at) + handed
            low_s[pl.ds(i * states, states), :] = adjoint.astype(bf16)
            handed = jnp.exp2(power) * adjoint
            if i == 0:
                before = pl.multiple_of(jnp.maximum(at - states, 0), states)
            else:
                before = pl.multiple_of((base + (i - 1)) * states, states)
            rate = handed * state_s[pl.ds(before, states), :]
            rate_s[pl.ds(i * states, states), :] = (rate * decay).astype(bf16)
            acc = acc + rate * power
        decay_s[...] = acc
        return handed

    def sum_backward(step, low_s, rate_s, accs):
        skip_acc, bias_acc = accs
        cut = pl.ds(pl.multiple_of(step * chunk, chunk), chunk)
        low = low_s[...]
        in_sum = jnp.dot(in_block_ref[cut, :], low, preferred_element_type=f32)
        rate_sum = jnp.dot(ones_block, rate_s[...], preferred_element_type=f32)
        din_ref[cut, :] = lax.dot_general(drive_s[cut, :].astype(bf16), low, last_dims, preferred_element_type=f32)
        pre = pre_ref[cut, :]
        live = mask_ref[cut, 0:1]
        gate = gate_s[cut, :]
        sig = jax.nn.sigmoid(gate)
        act = act_ref[cut, :].astype(f32)
        dscan = dscan_s[cut, :]
        dpre = ((rate_sum + in_sum * act) * jax.nn.sigmoid(pre)).astype(bf16)
        dpre_s[cut, :] = dpre
        dact_ref[cut, :] = dscan * skip + in_sum * softplus(pre)
        branch = (scanned_s[cut, :] + skip * act) * live
        gated_ref[cut, :] = (branch * gate * sig).astype(bf16)
        dgate_ref[cut, :] = (dgated_s[cut, :] * branch * sig * (1.0 + gate * (1.0 - sig))).astype(bf16)
        skip_acc = skip_acc + jnp.sum((dscan * act).reshape(chunk // 8, 8, width), axis=0)
        bias_acc = bias_acc + jnp.sum(dpre.astype(f32).reshape(chunk // 8, 8, width), axis=0)
        return skip_acc, bias_acc

    eight = jnp.zeros((8, width), f32)
    last = count - 1
    handed = run_backward(last, zero, odd_s, odd_rate_s)

    def backward(pair, carry):
        handed, accs = carry
        step = last - 2 * pair
        accs = sum_backward(step, odd_s, odd_rate_s, accs)
        handed = run_backward(step - 1, handed, even_s, even_rate_s)
        accs = sum_backward(step - 1, even_s, even_rate_s, accs)
        handed = run_backward(step - 2, handed, odd_s, odd_rate_s)
        return handed, accs

    handed, accs = lax.fori_loop(0, count // 2 - 1, backward, (handed, (eight, eight)))
    accs = sum_backward(1, odd_s, odd_rate_s, accs)
    run_backward(0, handed, even_s, even_rate_s)
    skip_acc, bias_acc = sum_backward(0, even_s, even_rate_s, accs)
    rank_grad_ref[...] = lax.dot_general(dpre_s[...], step_weight_ref[...], last_dims, preferred_element_type=f32)
    step_part = lax.dot_general(rank_ref[...], dpre_s[...], first_dims, preferred_element_type=f32)
    small = jnp.concatenate(
        [jnp.sum(skip_acc, axis=0, keepdims=True), jnp.sum(bias_acc, axis=0, keepdims=True), jnp.zeros((6, width), f32)],
        axis=0,
    )

    @pl.when(first)
    def _():
        step_grad_ref[...] = step_part
        sums_ref[0:8, :] = small
        sums_ref[8:, :] = decay_s[...] * (1.0 / log2e)

    @pl.when(jnp.logical_not(first))
    def _():
        step_grad_ref[...] += step_part
        sums_ref[0:8, :] += small
        sums_ref[8:, :] += decay_s[...] * (1.0 / log2e)


def scan_both_ways(start, blocks, width, pre, act, normed, cot, weights, rank_low, step_weight, mask, tables, skip, decay_log):
    micro, tok, chans = pre.shape
    dim = normed.shape[2]
    states = decay_log.shape[0]
    rows = chunk * states
    rank = rank_low.shape[2]

    def whole(r, c):
        return pl.BlockSpec((None, r, c), lambda j, m: (m, 0, 0))

    def each(r, c):
        return pl.BlockSpec((None, None, r, c), lambda j, m: (j, m, 0, 0))

    def part(r):
        return pl.BlockSpec((None, r, width), lambda j, m: (m, 0, j))

    def later(r):
        return pl.BlockSpec((None, r, width), lambda j, m: (m, 0, j + start))

    def param(r, at):
        return pl.BlockSpec((r, width), lambda j, m: (0, j + at))

    def shaped(*dims, kind=f32):
        return jax.ShapeDtypeStruct(dims, kind)

    total = blocks * width
    return pl.pallas_call(
        functools.partial(scan_kernel, states),
        grid=(blocks, micro),
        in_specs=[later(tok)] * 2
        + [whole(tok, dim)] * 2
        + [pl.BlockSpec((None, dim, width), lambda j, m, k=k, at=at: (k, 0, j + at)) for _, k, at in weights]
        + [whole(tok, rank), param(rank, start), whole(tok, mask.shape[2])]
        + [whole(tok * states, 128)] * 2
        + [whole(tok, rows)] * 2
        + [param(1, start), param(states, start)],
        out_specs=[part(tok)] * 3
        + [param(rank, 0), param(8 + states, 0), each(tok, rank), each(tok, rows), each(tok, rows)],
        out_shape=[shaped(micro, tok, total, kind=bf16)] * 2
        + [shaped(micro, tok, total), shaped(rank, total), shaped(8 + states, total)]
        + [shaped(blocks, micro, tok, rank), shaped(blocks, micro, tok, rows), shaped(blocks, micro, tok, rows)],
        scratch_shapes=[pltpu.VMEM((tok, width), f32)] * 6
        + [pltpu.VMEM((tok, width), bf16)]
        + [pltpu.VMEM((tok * states, width), f32)] * 2
        + [pltpu.VMEM((rows, width), bf16)] * 4
        + [pltpu.VMEM((states, width), f32)],
        compiler_params=pltpu.CompilerParams(
            dimension_semantics=("arbitrary", "arbitrary"), vmem_limit_bytes=58 * 2**20
        ),
        cost_estimate=small_cost,
    )(pre, act, normed, cot, *[v for v, _, _ in weights], rank_low, step_weight, mask, *tables, skip[None], decay_log)


def halves(values):
    high = values.astype(bf16)
    return high, (values - high.astype(f32)).astype(bf16)


def middle_kernel(states, selected_ref, weight_ref, bias_ref, pre_ref, rank_ref, in_ref, out_ref, in_block_ref, out_block_ref):
    tokens = selected_ref.shape[0]
    rank = weight_ref.shape[0]
    rows = chunk * states
    selected = selected_ref[...]
    low = selected[:, :rank].astype(bf16)
    rank_ref[...] = low
    pre_ref[...] = jnp.dot(low, weight_ref[...], preferred_element_type=f32) + bias_ref[...]
    state_ids = lax.broadcasted_iota(jnp.int32, (states, rows), 0)
    col_ids = lax.broadcasted_iota(jnp.int32, (states, rows), 1)
    spreading = (lax.rem(col_ids, states) == state_ids).astype(bf16)
    row_ids = lax.broadcasted_iota(jnp.int32, (chunk, rows), 0)
    chunk_cols = lax.broadcasted_iota(jnp.int32, (chunk, rows), 1)
    same = lax.div(chunk_cols, states) == row_ids
    ones = jnp.ones((2 * chunk, 128), bf16)
    for at, lanes_ref, block_ref in ((rank, in_ref, in_block_ref), (rank + states, out_ref, out_block_ref)):
        tiled = [
            jnp.dot(v, spreading, preferred_element_type=f32) for v in halves(selected[:, at : at + states])
        ]
        for i in range(tokens // chunk):
            cut = slice(i * chunk, (i + 1) * chunk)
            high, rest = [jnp.where(same, v[cut], 0.0).astype(bf16) for v in tiled]
            block_ref[cut, :] = high
            lanes_ref[i * rows : (i + 1) * rows, :] = lax.dot_general(
                jnp.concatenate([high, rest], axis=0), ones, first_dims, preferred_element_type=f32
            )


def middle(selected, weight, bias, states):
    tokens, picked = selected.shape
    rank, channels = weight.shape
    rows = chunk * states
    cut = min(128, tokens)

    def fixed(r, c):
        return pl.BlockSpec((r, c), lambda i: (0, 0))

    def part(r, c):
        return pl.BlockSpec((r, c), lambda i: (i, 0))

    def shaped(r, c, kind):
        return jax.ShapeDtypeStruct((r, c), kind)

    return pl.pallas_call(
        functools.partial(middle_kernel, states),
        grid=(tokens // cut,),
        in_specs=[part(cut, picked), fixed(rank, channels), fixed(1, channels)],
        out_specs=[part(cut, channels), part(cut, rank)]
        + [part(cut * states, 128)] * 2
        + [part(cut, rows)] * 2,
        out_shape=[shaped(tokens, channels, f32), shaped(tokens, rank, bf16)]
        + [shaped(tokens * states, 128, f32)] * 2
        + [shaped(tokens, rows, bf16)] * 2,
        compiler_params=pltpu.CompilerParams(dimension_semantics=("arbitrary",), vmem_limit_bytes=48 * 2**20),
    )(selected, weight, bias[None])


def unblocked(fulls, states):
    tok, rows = fulls[0].shape[2:]
    same = jnp.arange(tok)[:, None] % chunk == jnp.arange(rows)[None, :] // states
    picks = (jnp.arange(rows)[:, None] % states == jnp.arange(states)[None, :]).astype(f32)
    full = sum(v[j] for v in fulls for j in range(v.shape[0]))
    return jnp.dot(jnp.where(same[None], full, 0.0), picks, precision=highest)


def behind(values, steps):
    return values if steps == 0 else pltpu.roll(values, steps, 0)


def ahead(values, steps):
    return values if steps == 0 else pltpu.roll(values, values.shape[0] - steps, 0)


def convolve(inner, mask_ref, weight_ref, bias_ref):
    taps = weight_ref.shape[0]
    total = bias_ref[...] + weight_ref[taps - 1 : taps, :] * inner
    for back in range(1, taps):
        tap = taps - 1 - back
        total = total + weight_ref[tap : tap + 1, :] * behind(inner, back) * mask_ref[:, back : back + 1]
    return total


def inner_kernel(bounds, normed_ref, *refs):
    *weight_refs, mask_ref, conv_ref, bias_ref, select_ref, inner_ref, convolved_ref, act_ref, selected_ref = refs
    tile = pl.program_id(0)
    for ref, low, high in zip(weight_refs, bounds[:-1], bounds[1:]):

        @pl.when(jnp.logical_and(tile >= low, tile < high))
        def _(ref=ref):
            inner_ref[...] = jnp.dot(normed_ref[...], ref[...], preferred_element_type=f32)

    convolved = convolve(inner_ref[...], mask_ref, conv_ref, bias_ref)
    convolved_ref[...] = convolved
    act = (convolved * jax.nn.sigmoid(convolved)).astype(bf16)
    act_ref[...] = act
    part = jnp.dot(act, select_ref[...], preferred_element_type=f32)
    selected_ref[...] = jnp.where(tile == 0, part, selected_ref[...] + part)


def inner_forward(normed, weights, mask, conv_w, conv_b, select):
    tokens, dim = normed.shape
    channels = sum(v.shape[1] for v in weights)
    width = min([256] + [v.shape[1] for v in weights])
    taps = conv_w.shape[0]
    picked = select.shape[1]
    bounds = [0]
    for v in weights:
        bounds.append(bounds[-1] + v.shape[1] // width)

    def fixed(r, c):
        return pl.BlockSpec((r, c), lambda j: (0, 0))

    def part(r):
        return pl.BlockSpec((r, width), lambda j: (0, j))

    def held(low, high):
        return pl.BlockSpec((dim, width), lambda j: (0, jnp.clip(j - low, 0, high - low - 1)))

    return pl.pallas_call(
        functools.partial(inner_kernel, tuple(bounds)),
        grid=(channels // width,),
        in_specs=[fixed(tokens, dim)]
        + [held(low, high) for low, high in zip(bounds[:-1], bounds[1:])]
        + [
            fixed(tokens, mask.shape[1]),
            part(taps),
            part(1),
            pl.BlockSpec((width, picked), lambda j: (j, 0)),
        ],
        out_specs=[part(tokens)] * 3 + [fixed(tokens, picked)],
        out_shape=[
            jax.ShapeDtypeStruct((tokens, channels), f32),
            jax.ShapeDtypeStruct((tokens, channels), f32),
            jax.ShapeDtypeStruct((tokens, channels), bf16),
            jax.ShapeDtypeStruct((tokens, picked), f32),
        ],
        compiler_params=pltpu.CompilerParams(dimension_semantics=("arbitrary",), vmem_limit_bytes=48 * 2**20),
        cost_estimate=small_cost,
    )(normed, *weights, mask, conv_w, conv_b[None], select)


def assemble_kernel(outer, places_ref, *refs):
    *groups, out_ref = refs
    for i, ref in enumerate(groups):

        @pl.when(lax.div(pl.program_id(0), outer) == i)
        def _(ref=ref):
            out_ref[...] = ref[...]


def assemble(groups, places):
    count = places.shape[0]
    outer = count // len(groups)
    rows, width = groups[0].shape
    own = rows // outer

    def held(i):
        return pl.BlockSpec((own, width), lambda r, _: (jnp.clip(r - i * outer, 0, outer - 1), 0))

    return pl.pallas_call(
        functools.partial(assemble_kernel, outer),
        grid_spec=pltpu.PrefetchScalarGridSpec(
            num_scalar_prefetch=1,
            grid=(count,),
            in_specs=[held(i) for i in range(len(groups))],
            out_specs=pl.BlockSpec((own, width), lambda r, where: (where[r], 0)),
        ),
        out_shape=jax.ShapeDtypeStruct((rows * len(groups), width), groups[0].dtype),
        compiler_params=pltpu.CompilerParams(dimension_semantics=("arbitrary",), vmem_limit_bytes=48 * 2**20),
        cost_estimate=small_cost,
    )(places, *groups)


def inner_back_kernel(bounds, places_ref, *refs):
    *dact_refs, dsel_ref, select_ref, inner_ref, convolved_ref, act_ref, mask_ref, conv_ref, left_ref = refs[:-6]
    dinner_ref, sums_ref, select_grad_ref, sent_ref, kept_ref, dact_s = refs[-6:]
    taps = conv_ref.shape[0]
    tile = pl.program_id(0)
    for ref, low, high in zip(dact_refs, bounds[:-1], bounds[1:]):

        @pl.when(jnp.logical_and(tile >= low, tile < high))
        def _(ref=ref):
            dact_s[...] = ref[...]

    inner = inner_ref[...]
    dsel = dsel_ref[...]
    convolved = convolved_ref[...]
    sig = jax.nn.sigmoid(convolved)
    dact = dact_s[...] + lax.dot_general(dsel, select_ref[...], last_dims, preferred_element_type=f32)
    dconv = dact * sig * (1.0 + convolved * (1.0 - sig))
    dinner = conv_ref[taps - 1 : taps, :] * dconv
    sums_ref[taps : taps + 1, :] = jnp.sum(dconv, axis=0, keepdims=True)
    sums_ref[taps - 1 : taps, :] = jnp.sum(dconv * inner, axis=0, keepdims=True)
    for back in range(1, taps):
        tap = taps - 1 - back
        moved = ahead(dconv * mask_ref[:, back : back + 1], back)
        sums_ref[tap : tap + 1, :] = jnp.sum(moved * inner, axis=0, keepdims=True)
        dinner = dinner + conv_ref[tap : tap + 1, :] * moved
    low = dinner.astype(bf16)
    dinner_ref[...] = low
    select_grad_ref[...] = lax.dot_general(dsel, act_ref[...], first_dims, preferred_element_type=f32)
    outer, own = kept_ref.shape[1], kept_ref.shape[3]
    for core, out_ref in ((1, sent_ref), (0, kept_ref)):
        for cross in range(2):
            at = (2 * core + cross) * outer
            rows = [
                left_ref[pl.ds(pl.multiple_of(places_ref[at + j] * own, own), own), :] for j in range(outer)
            ]
            full = jnp.dot(jnp.concatenate(rows, axis=0), low, preferred_element_type=f32).astype(bf16)
            for j in range(outer):
                out_ref[cross, j, 0] = full[j * own : (j + 1) * own]


def inner_backward(places, dacts, dsel, select, inner, convolved, act, mask, conv_w, left):
    tokens, channels = inner.shape
    count = places.shape[0]
    outer, own = count // 4, left.shape[0] // count
    width = min([256] + [v.shape[1] for v in dacts])
    taps = conv_w.shape[0]
    picked = select.shape[1]
    bounds = [0]
    for v in dacts:
        bounds.append(bounds[-1] + v.shape[1] // width)

    def fixed(r, c):
        return pl.BlockSpec((r, c), lambda j, _: (0, 0))

    def part(r):
        return pl.BlockSpec((r, width), lambda j, _: (0, j))

    def held(low, high):
        return pl.BlockSpec((tokens, width), lambda j, _: (0, jnp.clip(j - low, 0, high - low - 1)))

    parts = pl.BlockSpec((2, outer, 1, own, width), lambda j, _: (0, 0, 0, 0, j))
    return pl.pallas_call(
        functools.partial(inner_back_kernel, tuple(bounds)),
        grid_spec=pltpu.PrefetchScalarGridSpec(
            num_scalar_prefetch=1,
            grid=(channels // width,),
            in_specs=[held(low, high) for low, high in zip(bounds[:-1], bounds[1:])]
            + [
                fixed(tokens, picked),
                pl.BlockSpec((width, picked), lambda j, _: (j, 0)),
                part(tokens),
                part(tokens),
                part(tokens),
                fixed(tokens, mask.shape[1]),
                part(taps),
                fixed(*left.shape),
            ],
            out_specs=[part(tokens), part(8), part(picked), parts, parts],
            scratch_shapes=[pltpu.VMEM((tokens, width), f32)],
        ),
        out_shape=[
            jax.ShapeDtypeStruct((tokens, channels), bf16),
            jax.ShapeDtypeStruct((8, channels), f32),
            jax.ShapeDtypeStruct((picked, channels), f32),
        ]
        + [jax.ShapeDtypeStruct((2, outer, 1, own, channels), bf16)] * 2,
        compiler_params=pltpu.CompilerParams(dimension_semantics=("arbitrary",), vmem_limit_bytes=52 * 2**20),
        cost_estimate=small_cost,
    )(places, *dacts, dsel, select, inner, convolved, act, mask, conv_w, left)


def project_kernel(count, where_ref, *refs):
    lefts, rights, out_ref = refs[:count], refs[count:-1], refs[-1]
    total = None
    for left, right in zip(lefts, rights):
        rows = jnp.concatenate([left[m] for m in range(left.shape[0])], axis=0)
        part = lax.dot_general(rows, right[...], last_dims, preferred_element_type=f32)
        total = part if total is None else total + part
    rows = out_ref.shape[1]
    for m in range(out_ref.shape[0]):
        out_ref[m] = total[m * rows : (m + 1) * rows].astype(out_ref.dtype)


def project(terms, where, shard_rows, kind):
    micro = terms[0][0].shape[0]
    dim = terms[0][3].shape[1]
    width = min(256, dim)

    def column(plane, at, wide):
        return pl.BlockSpec((None, width, wide), lambda i, _: (plane, i, at))

    def left_rows(at, wide):
        return pl.BlockSpec((micro, shard_rows, wide), lambda i, who: (0, who[0], at))

    return pl.pallas_call(
        functools.partial(project_kernel, len(terms)),
        grid_spec=pltpu.PrefetchScalarGridSpec(
            num_scalar_prefetch=1,
            grid=(dim // width,),
            in_specs=[left_rows(at, wide) for _, at, wide, _, _, _ in terms]
            + [column(plane, at, wide) for _, _, wide, _, plane, at in terms],
            out_specs=pl.BlockSpec((micro, shard_rows, width), lambda i, _: (0, 0, i)),
        ),
        out_shape=jax.ShapeDtypeStruct((micro, shard_rows, dim), kind),
        compiler_params=pltpu.CompilerParams(dimension_semantics=("arbitrary",), vmem_limit_bytes=48 * 2**20),
        cost_estimate=small_cost,
    )(where, *[t[0] for t in terms], *[t[3] for t in terms])


def project_all(terms):
    total = 0.0
    for left, left_at, wide, right, plane, at in terms:
        total = total + jnp.einsum(
            "mgc,dc->mgd",
            left[..., left_at * wide : (left_at + 1) * wide],
            right[plane, :, at * wide : (at + 1) * wide],
            preferred_element_type=f32,
        )
    return lax.psum_scatter(total.astype(bf16), "tensor", scatter_dimension=1, tiled=True)


def parts_kernel(kinds, outer, places_ref, *refs):
    out_ref = refs[-1]
    own = refs[0].shape[0]
    for kind in range(kinds):
        left = jnp.concatenate([r[...] for r in refs[kind * outer : (kind + 1) * outer]], axis=0)
        full = jnp.dot(left, refs[kinds * outer + kind][...], preferred_element_type=f32).astype(bf16)
        for j in range(outer):
            out_ref[j, kind] = full[j * own : (j + 1) * own]


def grad_parts(places, near, lefts, rights):
    kinds = len(lefts)
    count = places.shape[0]
    outer = count // 4
    own = lefts[0].shape[0] // count
    tokens = lefts[0].shape[1]
    width = rights[0].shape[1]
    offset = 0 if near else 2 * outer

    def left_spec(j):
        return pl.BlockSpec((own, tokens), lambda q, where: (where[offset + q * outer + j], 0))

    return pl.pallas_call(
        functools.partial(parts_kernel, kinds, outer),
        grid_spec=pltpu.PrefetchScalarGridSpec(
            num_scalar_prefetch=1,
            grid=(2,),
            in_specs=[left_spec(j) for _ in range(kinds) for j in range(outer)]
            + [pl.BlockSpec(v.shape, lambda q, where: (0, 0)) for v in rights],
            out_specs=pl.BlockSpec((None, outer, kinds, own, width), lambda q, where: (q, 0, 0, 0, 0)),
        ),
        out_shape=jax.ShapeDtypeStruct((2, outer, kinds, own, width), bf16),
        compiler_params=pltpu.CompilerParams(dimension_semantics=("arbitrary",), vmem_limit_bytes=48 * 2**20),
        cost_estimate=small_cost,
    )(places, *[v for v in lefts for _ in range(outer)], *rights)


def join(*trees):
    return lax.optimization_barrier(trees)


def summed(first, second, *more):
    total = first.astype(f32) + second.astype(f32)
    for v in more:
        total = total + v.astype(f32)
    return total


def sums_kernel(crosses, alongs, outer, *refs):
    ins = 2 * sum(crosses) + 3 * sum(alongs)
    given, outs = iter(refs[:ins]), iter(refs[ins:])
    for sources in crosses:
        out, at = next(outs), 0
        for _ in range(sources):
            kept, got = next(given), next(given)
            total = (kept[...].astype(f32) + got[...].astype(f32)).astype(bf16)
            out[..., at : at + total.shape[-1]] = total
            at += total.shape[-1]
    for sources in alongs:
        out, at = [next(outs) for _ in range(outer)], 0
        for _ in range(sources):
            kept, got, across = next(given), next(given), next(given)
            wide = kept.shape[-1]
            for j in range(outer):
                total = kept[j].astype(f32) + got[j].astype(f32) + across[j].astype(f32)
                out[j][..., at : at + wide] = total.astype(out[j].dtype)
            at += wide


def step_sums(crosses, alongs):
    cuts = 2
    in_specs, out_specs, out_shape, given = [], [], [], []
    outer = (crosses + alongs)[0][0][0].shape[1]

    def taken(shape, first, at, wide):
        block = (None,) + shape[1:-2] + (shape[-2] // cuts, wide)
        return pl.BlockSpec(block, lambda i: (first,) + (0,) * (len(shape) - 3) + (i, at))

    def plain(shape, at=0):
        return pl.BlockSpec(
            shape[:-2] + (shape[-2] // cuts, shape[-1]), lambda i: (0,) * (len(shape) - 2) + (i, at)
        )

    for sources in crosses:
        for kept, got, at, wide in sources:
            in_specs += [taken(kept.shape, 1, at, wide)] * 2
            given += [kept, got]
        out = sources[0][0].shape[1:-1] + (sum(v[3] for v in sources),)
        out_specs.append(plain(out))
        out_shape.append(jax.ShapeDtypeStruct(out, bf16))
    for sources in alongs:
        for kept, got, at, wide, across, across_at in sources:
            in_specs += [taken(kept.shape, 0, at, wide)] * 2 + [plain(across.shape[:-1] + (wide,), across_at)]
            given += [kept, got, across]
        out = sources[0][0].shape[2:-1] + (sum(v[3] for v in sources),)
        out_specs += [plain(out)] * outer
        out_shape += [jax.ShapeDtypeStruct(out, f32 if j == 0 else bf16) for j in range(outer)]
    outs = pl.pallas_call(
        functools.partial(
            sums_kernel, tuple(len(v) for v in crosses), tuple(len(v) for v in alongs), outer
        ),
        grid=(cuts,),
        in_specs=in_specs,
        out_specs=out_specs,
        out_shape=out_shape,
        compiler_params=pltpu.CompilerParams(dimension_semantics=("arbitrary",), vmem_limit_bytes=48 * 2**20),
        cost_estimate=small_cost,
    )(*given)
    outs = list(outs)
    first, rest = outs[: len(crosses)], outs[len(crosses) :]
    return first, [rest[i * outer : (i + 1) * outer] for i in range(len(alongs))]


def along_moves(rows):
    count = lax.axis_size("dp")
    return rows[:1] + [
        lax.ppermute(v, "dp", [(i, (i + 4 * (j + 1)) % count) for i in range(count)])
        for j, v in enumerate(rows[1:])
    ]


def final_kernel(turned, *refs):
    terms, outs = refs[: len(refs) - len(turned)], refs[len(refs) - len(turned) :]
    total = terms[0][...]
    for ref in terms[1:]:
        total = total + ref[...].astype(f32)
    for i, turn in enumerate(turned):
        outs[i][...] = total[i].T if turn else total[i]


def final_sum(terms, turned):
    kinds, own, width = terms[0].shape
    return pl.pallas_call(
        functools.partial(final_kernel, turned),
        out_shape=[jax.ShapeDtypeStruct((width, own) if turn else (own, width), f32) for turn in turned],
        compiler_params=pltpu.CompilerParams(vmem_limit_bytes=48 * 2**20),
        cost_estimate=small_cost,
    )(*terms)


def doubled(values):
    count = lax.axis_size("dp")
    here = lax.axis_index("dp")
    values = values[None]
    bit = 1
    while bit < count:
        other = swapped(values, "dp", bit)
        low = (here & bit) == 0
        values = jnp.concatenate([jnp.where(low, values, other), jnp.where(low, other, values)], axis=0)
        bit *= 2
    return values


def finish_kernel(hidden_ref, cot_ref, gain_ref, layer_ref, layer_away_ref, here_ref, away_ref, layer_out, grad_out):
    hidden = hidden_ref[...]
    scale = lax.rsqrt(jnp.mean(hidden * hidden, axis=-1, keepdims=True) + epsilon)
    normal = hidden * scale
    layer_out[...] = hidden + (layer_ref[...] + layer_away_ref[...].astype(f32))
    dnormed = here_ref[...] + away_ref[...].astype(f32)
    dnormal = dnormed * gain_ref[...]
    middle = jnp.mean(dnormal * normal, axis=-1, keepdims=True)
    grad_out[...] = cot_ref[...].astype(f32) + scale * (dnormal - normal * middle)


def finish(hidden, cotangent, gain, layer_here, layer_away, here, away):
    micro, rows, dim = hidden.shape
    total = micro * rows
    cut = min(64, total)

    def part():
        return pl.BlockSpec((cut, dim), lambda i: (i, 0))

    layer, grad = pl.pallas_call(
        finish_kernel,
        grid=(total // cut,),
        in_specs=[part(), part(), pl.BlockSpec((1, dim), lambda i: (0, 0))] + [part()] * 4,
        out_specs=[part(), part()],
        out_shape=[jax.ShapeDtypeStruct((total, dim), f32)] * 2,
        compiler_params=pltpu.CompilerParams(dimension_semantics=("arbitrary",), vmem_limit_bytes=48 * 2**20),
        cost_estimate=small_cost,
    )(*[v.reshape(-1, dim) for v in (hidden, cotangent, gain, layer_here, layer_away, here, away)])
    return layer.reshape(hidden.shape), grad.reshape(hidden.shape)


def on_device(
    hidden,
    cotangent,
    lengths,
    order,
    norm_gain,
    input_weight,
    conv_weight,
    conv_bias,
    select_weight,
    step_weight,
    step_bias,
    decay_log,
    skip_gain,
    output_weight,
):
    micro, shard_rows, model_dim = hidden.shape
    count = lax.axis_size("dp")
    outer = count // 4
    group_tok = shard_rows * lax.axis_size("tensor")
    tokens = micro * group_tok
    channels = input_weight.shape[2]
    taps = conv_weight.shape[0]
    states = decay_log.shape[0]
    own = conv_bias.shape[0]
    own_dim = norm_gain.shape[0]
    half = channels // 2
    quarter = channels // 4
    here = lax.axis_index("dp")
    ids = jnp.arange(count, dtype=jnp.int32)
    place, cross, core = here // 4, (here // 2) % 2, here % 2
    places = ((place + ids % outer) % outer) * 4 + (cross ^ (ids // outer) % 2) * 2 + (core ^ ids // (2 * outer))
    ranks = ((core ^ ids % 2) * 2 + (cross ^ (ids // 2) % 2)) * outer + (ids // 4 - place) % outer
    places, ranks = places.astype(jnp.int32), ranks.astype(jnp.int32)

    w_inner = lax.all_gather(input_weight[:, 0], "dp", axis=0, tiled=True)
    out_shard = output_weight.T
    weights = []
    for low, high in ((0, half), (half, channels)):
        both = jnp.stack([input_weight[:, 1, low:high], out_shard[:, low:high]])
        both = lax.all_gather(both, "dp", axis=1, tiled=True)
        weights.append(((both, 0, 0), (both, 1, 0)))

    pieces = [norm_gain, conv_weight, conv_bias, step_bias, decay_log, skip_gain]
    packed = doubled(jnp.concatenate([v.reshape(-1) for v in pieces]))
    narrow, packed = join(jnp.concatenate([select_weight.T, step_weight.reshape(-1, own)], axis=0), packed)
    full = []
    at = 0
    for v in pieces:
        part = packed[:, at : at + v.size]
        at += v.size
        if v.ndim == 2:
            part = part.reshape(count, v.shape[0], v.shape[1]).transpose(1, 0, 2).reshape(v.shape[0], -1)
        else:
            part = part.reshape(-1)
        full.append(part)
    gain_full, conv_w, conv_b, step_b, decay_lg, skip_g = full
    picked = select_weight.shape[1]
    narrow = jnp.stack([narrow] + [moved(narrow, j) for j in range(1, outer)])
    narrow = jnp.stack([narrow, swapped(narrow, "dp", 2)])
    narrow = jnp.stack([narrow, swapped(narrow, "dp", 1)]).reshape((count,) + narrow.shape[2:])
    narrow = jnp.take(narrow, ranks, axis=0)
    w_sel = narrow[:, :picked].transpose(0, 2, 1).reshape(channels, picked)
    w_step = narrow[:, picked:].reshape(-1, channels)
    rank_dim = w_step.shape[0]

    inverse_rms = lax.rsqrt(jnp.mean(hidden * hidden, axis=-1, keepdims=True) + epsilon)
    normal_rows = hidden * inverse_rms
    normed = tensor_gather((normal_rows * gain_full).astype(bf16), 1).reshape(tokens, model_dim)
    normed, cot_rows = join(normed, cotangent)
    cot_full = tensor_gather(cot_rows, 1).reshape(tokens, model_dim)

    position, live_mask = jax.vmap(lambda a, b: positions(a, b, group_tok))(lengths[:, 0], order[:, 0])
    mask = jnp.stack([live_mask] + [(position >= back).astype(f32) for back in range(1, taps)], axis=2)
    flat_mask = mask.reshape(tokens, taps)

    def grouped(v):
        return v.reshape(micro, group_tok, v.shape[-1])

    inner, convolved, act, selected = inner_forward(normed, [w_inner], flat_mask, conv_w, conv_b, w_sel)
    selected = tensor_sum(selected)
    lefts = (normed.T, cot_full.T)
    pre_step, rank_low, *tables = middle(selected, w_step, step_b, states)
    tables = tuple(grouped(v) if v.shape[0] == tokens else v.reshape(micro, -1, v.shape[-1]) for v in tables)
    rank_rows = grouped(rank_low)

    gated, dgate, dact, step_grads, sums, rank_grads, dins, douts = [[] for _ in range(8)]
    kept, got, across, total = {}, {}, {}, {}
    rows = (grouped(normed), grouped(cot_full))

    def scanned(number, skip_now):
        return scan_both_ways(
            2 * number,
            2,
            quarter,
            grouped(pre_step),
            grouped(act),
            *rows,
            weights[number],
            rank_rows,
            w_step,
            mask,
            tables,
            skip_now,
            decay_lg,
        )

    def hold(results):
        for held, v in zip((gated, dgate, dact), results[:3]):
            held.append(v.reshape(tokens, -1))
        for held, v in zip((step_grads, sums, rank_grads, dins, douts), results[3:]):
            held.append(v)

    def source(piece, at=0, wide=None):
        return kept[piece], got[piece], at, wide or kept[piece].shape[-1]

    def last_step(piece, name, at=0):
        return [source(piece) + (across[name], at)]

    hold(scanned(0, skip_g))
    places_now = places
    for piece, left, right in (("gate", lefts[0], dgate[0]), ("out", lefts[1], gated[0])):
        sent = grad_parts(places_now, False, (left,), (right,))
        sent, places_now = join(sent, places_now)
        got[piece] = swapped(sent, "dp", 1)
        kept[piece] = grad_parts(places_now, True, (left,), (right,))
    cross, _ = step_sums([[source("gate"), source("out")]], [])
    skip_now, cross = join(skip_g, cross)
    across["early"] = swapped(cross[0], "dp", 2)

    results = scanned(1, skip_now)
    results, across["early"] = join(results, across["early"])
    hold(results)
    _, along = step_sums([], [last_step("gate", "early"), last_step("out", "early", 1)])
    along, places_now, rank_grads = join(along, places_now, rank_grads)
    total["gate"] = along_moves(along[0])
    rank_grad = sum(v[j] for v in rank_grads for j in range(v.shape[0]))
    select_terms = jnp.concatenate([rank_grad, unblocked(dins, states), unblocked(douts, states)], axis=2)
    select_terms, places_now = join(select_terms.reshape(tokens, -1), places_now)
    select_terms = tensor_sum(select_terms, bf16)
    places_now, total["gate"][1] = join(places_now, total["gate"][1])
    for piece, left, right in (("gate_late", lefts[0], dgate[1]), ("out_late", lefts[1], gated[1])):
        sent = grad_parts(places_now, False, (left,), (right,))
        sent, places_now = join(sent, places_now)
        got[piece] = swapped(sent, "dp", 1)
    for piece, left, right in (("gate_late", lefts[0], dgate[1]), ("out_late", lefts[1], gated[1])):
        kept[piece] = grad_parts(places_now, True, (left,), (right,))
    two = lax.axis_size("tensor") == 2
    where = lax.axis_index("tensor").astype(jnp.int32)[None]
    kept["out_late"], where = join(kept["out_late"], where)
    out_terms = [(grouped(v), 0, v.shape[1]) + w[1] for v, w in zip(gated, weights)]
    layer_away = project(out_terms, 1 - where, shard_rows, bf16) if two else project_all(out_terms)
    names = ("gate_late", "out_late")
    select_terms, late_kept, late_got, total["gate"], layer_away = join(
        select_terms, [kept[n] for n in names], [got[n] for n in names], total["gate"], layer_away
    )
    for n, one, other in zip(names, late_kept, late_got):
        kept[n], got[n] = one, other
    select_low = select_terms.astype(bf16)
    cross, _ = step_sums([[source("gate_late")], [source("out_late")]], [])
    cross, select_low, along[1] = join(cross, select_low, along[1])
    across["gate_late"] = swapped(cross[0], "dp", 2)
    total["out"] = along_moves(along[1])
    dinner, conv_sums, select_grad, sent, kept["inner"] = inner_backward(
        places_now, dact, select_low, w_sel, inner, convolved, act, flat_mask, conv_w, lefts[0]
    )
    across["gate_late"], total["out"], dinner, conv_sums, select_grad, sent, kept["inner"], where, cross[1] = join(
        across["gate_late"], total["out"], dinner, conv_sums, select_grad, sent, kept["inner"], where, cross[1]
    )
    norm_terms = [(grouped(v), 0, v.shape[1]) + w[0] for v, w in zip(dgate, weights)]
    norm_terms.append((grouped(dinner), 0, channels, w_inner[None], 0, 0))
    got["inner"] = swapped(sent, "dp", 1)
    across["out_late"] = swapped(cross[1], "dp", 2)
    _, along = step_sums([], [last_step("gate_late", "gate_late")])
    along, where = join(along, where)
    total["gate_late"] = along_moves(along[0])
    if two:
        norm_away = project(norm_terms, 1 - where, shard_rows, bf16)
    else:
        norm_away = project_all(norm_terms)
    got["inner"], norm_away, where, total["gate_late"], across["out_late"] = join(
        got["inner"], norm_away, where, total["gate_late"], across["out_late"]
    )
    cross, along = step_sums(
        [[source("inner", 0, half)], [source("inner", 1, half)]], [last_step("out_late", "out_late")]
    )
    cross, along, where, norm_away, select_grad = join(cross, along, where, norm_away, select_grad)
    across["first"] = swapped(cross[0], "dp", 2)
    total["out_late"] = along_moves(along[0])
    if two:
        norm_away = swapped(norm_away, "tensor", 1)
        norm_here = project(norm_terms, where, shard_rows, f32)
        layer_here = project(out_terms, where, shard_rows, f32)
    else:
        norm_here, layer_here = [jnp.zeros(v.shape, f32) for v in (norm_away, layer_away)]
    across["first"], total["out_late"], cross[1], norm_here, layer_here, norm_away = join(
        across["first"], total["out_late"], cross[1], norm_here, layer_here, norm_away
    )
    step_grad = jnp.concatenate(step_grads, axis=1)
    step_grad = step_grad.reshape(count, rank_dim // count, count, own).transpose(1, 2, 0, 3)
    small = jnp.concatenate(
        [select_grad, step_grad.reshape(rank_dim, channels), conv_sums, jnp.concatenate(sums, axis=1)], axis=0
    )
    small = lax.psum_scatter(small, "dp", scatter_dimension=1, tiled=True)
    _, along = step_sums([], [[source("inner", 0, half) + (across["first"], 0)]])
    cross[1], along, layer_away = join(cross[1], along, layer_away)
    across["last"] = swapped(cross[1], "dp", 2)
    total["first"] = along_moves(along[0])
    if two:
        layer_away = swapped(layer_away, "tensor", 1)
    total["gate"], total["first"][1] = join(total["gate"], total["first"][1])
    gates = [final_sum(total[n], (False,))[0] for n in ("gate", "gate_late")]
    outs = [final_sum(total[n], (True,))[0] for n in ("out", "out_late")]
    across["last"], total["first"], gates, outs, layer_away, norm_here = join(
        across["last"], total["first"], gates, outs, layer_away, norm_here
    )
    _, along = step_sums([], [[source("inner", 1, half) + (across["last"], 0)]])
    along, norm_here = join(along, norm_here)
    total["last"] = along_moves(along[0])
    layer_rows, grad_rows = finish(hidden, cotangent, gain_full, layer_here, layer_away, norm_here, norm_away)
    gate_grad = jnp.concatenate(gates, axis=1)
    (first,) = final_sum(total["first"], (False,))
    own_input = input_weight.astype(f32)
    most = jnp.sum(own_input[:, 0, :half] * first, axis=1) + jnp.sum(own_input[:, 1] * gate_grad, axis=1)
    (last,) = final_sum(total["last"], (False,))
    gain_total = tensor_sum(most + jnp.sum(own_input[:, 0, half:] * last, axis=1)) / norm_gain
    at = picked + rank_dim
    return (
        layer_rows,
        grad_rows,
        gain_total,
        jnp.stack([jnp.concatenate([first, last], axis=1), gate_grad], axis=1),
        small[at : at + taps],
        small[at + taps],
        small[:picked].T,
        small[picked:at].reshape(-1, channels),
        small[at + 9],
        small[at + 16 :],
        small[at + 8],
        jnp.concatenate(outs, axis=0),
    )


def solution(mesh):
    in_specs = (
        P(None, ("dp", "tensor"), None),
        P(None, ("dp", "tensor"), None),
        P(None, "dp", None),
        P(None, "dp", None),
        P("dp"),
        P("dp", None, "tensor"),
        P(None, ("tensor", "dp")),
        P(("tensor", "dp")),
        P(("tensor", "dp"), None),
        P("dp", "tensor"),
        P(("tensor", "dp")),
        P(None, ("tensor", "dp")),
        P(("tensor", "dp")),
        P("tensor", "dp"),
    )
    out_specs = (
        P(None, ("dp", "tensor"), None),
        P(None, ("dp", "tensor"), None),
        P("dp"),
        P("dp", None, "tensor"),
        P(None, ("tensor", "dp")),
        P(("tensor", "dp")),
        P(("tensor", "dp"), None),
        P("dp", "tensor"),
        P(("tensor", "dp")),
        P(None, ("tensor", "dp")),
        P(("tensor", "dp")),
        P("tensor", "dp"),
    )
    return jax.shard_map(
        on_device, mesh=mesh, in_specs=in_specs, out_specs=out_specs, check_vma=False
    )
```
